128 devices in a mesh: seq: 8 (over y, x_lo), fsdp: 16 (over z, x_hi, core).
Axes of the slice: x: 4 (x_hi: 2, x_lo: 2; x = x_hi * 2 + x_lo), y: 4, z: 4, core: 2. Of those that a mesh axis runs over, the one named last changes fastest.
Arguments:
- latents: bfloat16 [16, 1024, 1152], P('fsdp', 'seq'), may hold values from -6 to 6
- timestep: bfloat16 [16, 6912], P('fsdp'), may hold values from -0.5 to 0.5
- caption: bfloat16 [16, 120, 1152], P('fsdp'), may hold values from -6 to 6
- shift_table: bfloat16 [6912], P('fsdp'), may hold values from -0.5 to 0.5
- qkv_weight: bfloat16 [1152, 3456], P('fsdp'), may hold values from -0.1875 to 0.1875
- query_bias: bfloat16 [1152], P('fsdp'), may hold values from -2.5 to 2.5
- value_bias: bfloat16 [1152], P('fsdp'), may hold values from -2.5 to 2.5
- proj_weight: bfloat16 [1152, 1152], P('fsdp'), may hold values from -1.5 to 1.5
- proj_bias: bfloat16 [1152], P('fsdp'), may hold values from -2.5 to 2.5
- cross_query: bfloat16 [1152, 1152], P('fsdp'), may hold values from -0.1875 to 0.1875
- cross_qbias: bfloat16 [1152], P('fsdp'), may hold values from -2.5 to 2.5
- cross_kv: bfloat16 [1152, 2304], P('fsdp'), may hold values from -0.1875 to 0.1875
- cross_vbias: bfloat16 [1152], P('fsdp'), may hold values from -2.5 to 2.5
- cross_proj: bfloat16 [1152, 1152], P('fsdp'), may hold values from -0.75 to 0.75
- cross_pbias: bfloat16 [1152], P('fsdp'), may hold values from -2.5 to 2.5
- up_weight: bfloat16 [1152, 4608], P('fsdp'), may hold values from -0.1875 to 0.1875
- up_bias: bfloat16 [4608], P('fsdp'), may hold values from -2.5 to 2.5
- down_weight: bfloat16 [4608, 1152], P('fsdp'), may hold values from -0.09375 to 0.09375
- down_bias: bfloat16 [1152], P('fsdp'), may hold values from -2.5 to 2.5
- cotangent: bfloat16 [16, 1024, 1152], P('fsdp', 'seq'), may hold values from -6 to 6
Outputs:
- block_out: bfloat16 [16, 1024, 1152], P('fsdp', 'seq')
- grad_latents: float32 [16, 1024, 1152], P('fsdp', 'seq')
- grad_timestep: float32 [16, 6912], P('fsdp')
- grad_caption: float32 [16, 120, 1152], P('fsdp')
- grad_table: float32 [6912], P('fsdp')
- grad_qkv: float32 [1152, 3456], P('fsdp')
- grad_qbias: float32 [1152], P('fsdp')
- grad_vbias: float32 [1152], P('fsdp')
- grad_proj: float32 [1152, 1152], P('fsdp')
- grad_pbias: float32 [1152], P('fsdp')
- grad_cquery: float32 [1152, 1152], P('fsdp')
- grad_cqbias: float32 [1152], P('fsdp')
- grad_ckv: float32 [1152, 2304], P('fsdp')
- grad_cvbias: float32 [1152], P('fsdp')
- grad_cproj: float32 [1152, 1152], P('fsdp')
- grad_cpbias: float32 [1152], P('fsdp')
- grad_up: float32 [1152, 4608], P('fsdp')
- grad_ubias: float32 [4608], P('fsdp')
- grad_down: float32 [4608, 1152], P('fsdp')
- grad_dbias: float32 [1152], P('fsdp')
The draws below stay inside these ranges and needn't reach their ends.
All inputs are finite; a program needn't handle non-finite values.
Results may differ from the reference program's by a relative error of at most 0.03.
Values may be sent and summed in bfloat16 or wider, within the bound.
A program may use at most 192 MiB of HBM per device.

```python
import jax
import jax.numpy as jnp
from jax import lax

D = 1152
HEADS = 16
HD = 72
FF = 4608
TXT = 120
LEN = 1024
LATENTS = 16


def levels(own_key, dims, shards, least, high):
    loudness = 1.0
    for axis_at, parts in shards:
        steps = jax.random.uniform(jax.random.fold_in(jax.random.fold_in(own_key, 6), axis_at), (parts,), jnp.float32, least / len(shards), high / len(shards))
        loudness = loudness * jnp.repeat(jnp.exp(steps), dims[axis_at] // parts).reshape((-1,) + (1,) * (len(dims) - 1 - axis_at))
    return loudness


def gaussian(rng, extent, width, limit, cuts=(), kind=jnp.bfloat16):
    drawn = jax.random.normal(rng, extent, jnp.float32) * width
    if len(cuts) > 0:
        drawn = levels(rng, extent, cuts, -0.22, 0.18) * drawn
    return jnp.clip(drawn, min=-limit, max=limit).astype(kind)


def setup_inputs(seed: int = 0) -> dict:
    splits = jax.random.split(jax.random.key(seed), 21)
    latents = gaussian(splits[0], (LATENTS, LEN, D), 1.0, 6.0, ((0, 16), (1, 8)))
    timestep = jnp.clip(jax.random.uniform(splits[1], (LATENTS, 6 * D), jnp.float32, -0.5, 0.5) * levels(splits[1], (LATENTS, 6 * D), ((0, 16),), -0.4, 0.0), -0.5, 0.5).astype(jnp.bfloat16)
    caption = gaussian(splits[2], (LATENTS, TXT, D), 1.0, 6.0, ((0, 16),))
    shift_table = jnp.clip(jax.random.uniform(splits[3], (6 * D,), jnp.float32, -0.5, 0.5) * levels(splits[3], (6 * D,), ((0, 16),), -0.4, 0.0), -0.5, 0.5).astype(jnp.bfloat16)
    qkv_weight = gaussian(splits[4], (D, 3 * D), D ** -0.5, 0.1875, ((0, 16),))
    query_bias = gaussian(splits[5], (D,), 0.5, 2.5, ((0, 16),))
    value_bias = gaussian(splits[6], (D,), 0.5, 2.5, ((0, 16),))
    proj_weight = gaussian(splits[7], (D, D), (D // 64) ** -0.5, 1.5, ((0, 16),))
    proj_bias = gaussian(splits[8], (D,), 0.5, 2.5, ((0, 16),))
    cross_query = gaussian(splits[9], (D, D), D ** -0.5, 0.1875, ((0, 16),))
    cross_qbias = gaussian(splits[10], (D,), 0.5, 2.5, ((0, 16),))
    cross_kv = gaussian(splits[11], (D, 2 * D), D ** -0.5, 0.1875, ((0, 16),))
    cross_vbias = gaussian(splits[12], (D,), 0.5, 2.5, ((0, 16),))
    cross_proj = gaussian(splits[13], (D, D), (D // 16) ** -0.5, 0.75, ((0, 16),))
    cross_pbias = gaussian(splits[14], (D,), 0.5, 2.5, ((0, 16),))
    up_weight = gaussian(splits[15], (D, FF), D ** -0.5, 0.1875, ((0, 16),))
    up_bias = gaussian(splits[16], (FF,), 0.5, 2.5, ((0, 16),))
    down_weight = gaussian(splits[17], (FF, D), FF ** -0.5, 0.09375, ((0, 16),))
    down_bias = gaussian(splits[18], (D,), 0.5, 2.5, ((0, 16),))
    cotangent = gaussian(splits[19], (LATENTS, LEN, D), 1.0, 6.0, ((0, 16), (1, 8)))
    return dict(latents=latents, timestep=timestep, caption=caption, shift_table=shift_table, qkv_weight=qkv_weight, query_bias=query_bias, value_bias=value_bias, proj_weight=proj_weight, proj_bias=proj_bias, cross_query=cross_query, cross_qbias=cross_qbias, cross_kv=cross_kv, cross_vbias=cross_vbias, cross_proj=cross_proj, cross_pbias=cross_pbias, up_weight=up_weight, up_bias=up_bias, down_weight=down_weight, down_bias=down_bias, cotangent=cotangent)


@jax.custom_vjp
def low(v):
    return lax.optimization_barrier(v.astype(jnp.bfloat16)).astype(jnp.float32)

@jax.custom_vjp
def low_back(v):
    return v

def low_keep(v):
    return (low(v), None)

def low_pass(kept, grad):
    return (grad,)

def back_keep(v):
    return (v, None)

def back_low(kept, grad):
    return (low(grad),)
low.defvjp(low_keep, low_pass)
low_back.defvjp(back_keep, back_low)
epsilon = 1e-06
highest = lax.Precision.HIGHEST

def matmul(former, latter):
    return jnp.dot(former, latter, precision=highest)

def normalize(values):
    centre = values - lax.optimization_barrier(jnp.mean(values, axis=-1, keepdims=True))
    spread = lax.optimization_barrier(jnp.mean(centre * centre, axis=-1, keepdims=True))
    return centre * lax.rsqrt(spread + epsilon)

def head_attend(pieces):
    queries, key_rows, values = pieces
    scores = low_back(jnp.dot(queries, key_rows.T, precision=highest) * HD ** (-0.5))
    weights = jax.nn.softmax(scores, axis=-1)
    return jnp.dot(low(weights), values, precision=highest)

def by_heads(matrix):
    return matrix.reshape(matrix.shape[0], HEADS, HD).transpose(1, 0, 2)

def attention(queries, key_rows, values):
    output = lax.map(jax.checkpoint(head_attend), (by_heads(queries), by_heads(key_rows), by_heads(values)))
    return output.transpose(1, 0, 2).reshape(queries.shape[0], D)

def forward(params, inputs, embedding, caption_rows):
    shift_table, qkv_weight, query_bias, value_bias, proj_weight, proj_bias, cross_query, cross_qbias, cross_kv, cross_vbias, cross_proj, cross_pbias, up_weight, up_bias, down_weight, down_bias = params
    modulation = (shift_table + embedding).reshape(6, D)
    normed_one = low(normalize(inputs) * (1.0 + modulation[1]) + modulation[0])
    packed = matmul(normed_one, qkv_weight) + jnp.concatenate([query_bias, jnp.zeros_like(query_bias), value_bias])
    packed = low_back(low(packed))
    attended = low_back(low(attention(packed[:, :D], packed[:, D:2 * D], packed[:, 2 * D:])))
    branch_one = low_back(matmul(attended, proj_weight) + proj_bias)
    after_one = inputs + modulation[2] * branch_one
    middle = low(after_one)
    cross_rows = low_back(low(matmul(middle, cross_query) + cross_qbias))
    text_kv = matmul(low(caption_rows), cross_kv) + jnp.concatenate([jnp.zeros_like(cross_vbias), cross_vbias])
    text_kv = low_back(low(text_kv))
    crossed = low_back(low(attention(cross_rows, text_kv[:, :D], text_kv[:, D:])))
    branch_two = low_back(matmul(crossed, cross_proj) + cross_pbias)
    after_two = after_one + branch_two
    normed_two = low(normalize(after_two) * (1.0 + modulation[4]) + modulation[3])
    hidden = low_back(matmul(normed_two, up_weight) + up_bias)
    activated = low(jax.nn.gelu(hidden))
    branch_three = low_back(matmul(activated, down_weight) + down_bias)
    return after_two + modulation[5] * branch_three

def reference(latents, timestep, caption, shift_table, qkv_weight, query_bias, value_bias, proj_weight, proj_bias, cross_query, cross_qbias, cross_kv, cross_vbias, cross_proj, cross_pbias, up_weight, up_bias, down_weight, down_bias, cotangent):
    params = tuple((member.astype(jnp.float32) for member in (shift_table, qkv_weight, query_bias, value_bias, proj_weight, proj_bias, cross_query, cross_qbias, cross_kv, cross_vbias, cross_proj, cross_pbias, up_weight, up_bias, down_weight, down_bias)))

    def advance(totals, pieces):
        inputs, embedding, caption_rows, grad_rows = pieces
        output, pullback = jax.vjp(forward, params, inputs.astype(jnp.float32), embedding.astype(jnp.float32), caption_rows.astype(jnp.float32))
        grad_params, grad_inputs, grad_embed, grad_caption = pullback(grad_rows.astype(jnp.float32))
        totals = tuple((running + addend for running, addend in zip(totals, grad_params)))
        return (totals, (output.astype(jnp.bfloat16), grad_inputs, grad_embed, grad_caption))
    initial = tuple((jnp.zeros_like(member) for member in params))
    totals, (block_out, grad_latents, grad_timestep, grad_caption) = lax.scan(advance, initial, (latents, timestep, caption, cotangent))
    return (block_out, grad_latents, grad_timestep, grad_caption, totals[0], totals[1], totals[2], totals[3], totals[4], totals[5], totals[6], totals[7], totals[8], totals[9], totals[10], totals[11], totals[12], totals[13], totals[14], totals[15])
```

```python
import functools

import jax
import jax.numpy as jnp
from jax import lax
from jax.experimental import pallas as pl
from jax.experimental.pallas import tpu as pltpu
from jax.sharding import PartitionSpec as P

HD = 72
MESH = pl.DeviceIdType.MESH


epsilon = 1e-06


def for_sending(array):

    def short(part):
        return part.astype(jnp.bfloat16) if part.dtype == jnp.float32 else part

    return jax.tree.map(short, array)


def normalize(values):
    centre = values - jnp.mean(values, axis=-1, keepdims=True)
    spread = jnp.mean(centre * centre, axis=-1, keepdims=True)
    return centre * lax.rsqrt(spread + epsilon)


def modulate(values, shift, scale):
    return normalize(values) * (1.0 + scale) + shift


def project(former, latter):
    return jnp.dot(former, latter, preferred_element_type=jnp.float32)


def weight_grad(former, latter):
    return jnp.einsum("bli,blo->io", former, latter, preferred_element_type=jnp.float32)


def token_sum(values):
    return jnp.sum(values.astype(jnp.float32), axis=(0, 1))


def by_heads(matrix):
    return matrix.reshape(matrix.shape[:-1] + (matrix.shape[-1] // HD, HD))


def attend_forward(queries, key_rows, values):
    factor = HD ** (-0.5)
    scores = (
        jnp.einsum("qhd,khd->hqk", queries, key_rows, preferred_element_type=jnp.float32) * factor
    )
    largest = jnp.max(scores, axis=-1, keepdims=True)
    exponent = jnp.exp(scores - largest)
    partition = jnp.sum(exponent, axis=-1, keepdims=True)
    weights = (exponent / partition).astype(jnp.bfloat16)
    output = jnp.einsum("hqk,khd->qhd", weights, values, preferred_element_type=jnp.float32)
    return (output.astype(jnp.bfloat16), largest + jnp.log(partition))


def attend_backward(queries, key_rows, values, logsum, grad_out):
    factor = HD ** (-0.5)
    scores = (
        jnp.einsum("qhd,khd->hqk", queries, key_rows, preferred_element_type=jnp.float32) * factor
    )
    weights = jnp.exp(scores - logsum)
    grad_weights = jnp.einsum("qhd,khd->hqk", grad_out, values, preferred_element_type=jnp.float32)
    inner = jnp.sum(weights * grad_weights, axis=-1, keepdims=True)
    grad_scores = (weights * (grad_weights - inner)).astype(jnp.bfloat16)
    grad_q = (
        jnp.einsum("hqk,khd->qhd", grad_scores, key_rows, preferred_element_type=jnp.float32)
        * factor
    )
    grad_k = (
        jnp.einsum("hqk,qhd->khd", grad_scores, queries, preferred_element_type=jnp.float32)
        * factor
    )
    grad_v = jnp.einsum(
        "hqk,qhd->khd", weights.astype(jnp.bfloat16), grad_out, preferred_element_type=jnp.float32
    )
    return (grad_q, grad_k, grad_v)


def self_forward(gathered):
    output, logsum = attend_forward(
        by_heads(gathered[:, 0]), by_heads(gathered[:, 1]), by_heads(gathered[:, 2])
    )
    return (output.reshape(gathered.shape[0], -1), logsum)


def self_backward(pieces):
    gathered, logsum, grad_rows = pieces
    grad_q, grad_k, grad_v = attend_backward(
        by_heads(gathered[:, 0]),
        by_heads(gathered[:, 1]),
        by_heads(gathered[:, 2]),
        logsum,
        by_heads(grad_rows),
    )
    stacked = jnp.stack([grad_q, grad_k, grad_v], axis=1)
    return stacked.reshape(gathered.shape[0], 3, -1).astype(jnp.bfloat16)


def place():
    seq, fsdp = lax.axis_index("seq"), lax.axis_index("fsdp")
    y, x_lo = seq // 2, seq % 2
    z, rest = fsdp // 4, fsdp % 4
    x_hi, core = rest // 2, rest % 2
    return x_hi * 2 + x_lo, y, z, core


def device(x, y, z, core):
    return (y * 2 + x % 2, z * 4 + (x // 2) * 2 + core)


def step(value, by):
    return (value + by + 4) % 4


class Copies:
    def __init__(self, send, recv):
        self.send, self.recv, self.index, self.started = send, recv, {}, []

    def number(self, key):
        return self.index.setdefault(key, len(self.index))

    def push(self, key, src, dst, target):
        at = self.number(key)
        copy = pltpu.make_async_remote_copy(
            src_ref=src,
            dst_ref=dst,
            send_sem=self.send.at[at],
            recv_sem=self.recv.at[at],
            device_id=target,
            device_id_type=MESH,
        )
        copy.start()
        self.started.append(copy)

    def arrived(self, key, dst, source):
        at = self.number(key)
        pltpu.make_async_remote_copy(
            src_ref=dst,
            dst_ref=dst,
            send_sem=self.send.at[at],
            recv_sem=self.recv.at[at],
            device_id=source,
            device_id_type=MESH,
        ).wait_recv()

    def finish(self):
        for copy in self.started:
            copy.wait_send()


def greet(others):
    barrier = pltpu.get_barrier_semaphore()
    for other in others:
        pl.semaphore_signal(barrier, inc=1, device_id=other, device_id_type=MESH)
    pl.semaphore_wait(barrier, len(others))


def gather_kernel(up, qkv, cq, small, ckv, pair, o_up, o_qkv, o_cq, o_small, o_ckv, o_pair, local, send, recv):
    x, y, z, c = place()
    xh, xl = x // 2, x % 2
    here = (x, y, z, c)
    sibling = device(x, y, z, 1 - c)
    far = device(step(x, 2), y, z, c)
    along_x = [device(step(x, d), y, z, c) for d in (1, 2, 3)]
    along_y = [device(x, step(y, d), z, c) for d in (1, 2, 3)]
    along_z = [device(x, y, step(z, d), c) for d in (1, 2, 3)]
    greet([sibling] + along_x + along_y + along_z)
    copies = Copies(send, recv)
    width = up.shape[1] // 4
    quarter = lambda q: pl.ds(pl.multiple_of(q * width, 128), width)
    half = lambda ref, h: pl.ds(pl.multiple_of(h * (ref.shape[-1] // 2), 128), ref.shape[-1] // 2)
    whole = ((qkv, o_qkv, "qkv"), (cq, o_cq, "cq"), (small, o_small, "small"))
    halved = ((ckv, o_ckv, "ckv"), (pair, o_pair, "pair"))

    stays = []
    for source, out, _ in whole:
        stays.append((source, out.at[z, xh, c]))
    for source, out, _ in halved:
        stays.append((source.at[:, half(source, xl)], out.at[z, xh, c, :, half(source, xl)]))
    stays.append((up.at[:, quarter(y)], o_up.at[z, xh, c, :, quarter(y)]))
    stays = [pltpu.make_async_copy(a, b, local.at[i]) for i, (a, b) in enumerate(stays)]
    for copy in stays:
        copy.start()

    for source, out, name in whole:
        copies.push((name, "far"), source, out.at[z, xh, c], far)
        for d, target in zip((1, 2, 3), along_z):
            copies.push((name, "z", 0, d), source, out.at[z, xh, c], target)
        copies.push((name, "core", 0), source, out.at[z, xh, c], sibling)
    mine = up.at[:, quarter(y)]
    there = o_up.at[z, xh, c, :, quarter(y)]
    copies.push(("up", "far"), mine, there, far)
    for source, out, name in halved:
        for d, target in zip((1, 2, 3), along_z):
            copies.push(
                (name, "z", d),
                source.at[:, half(source, xl)],
                out.at[z, xh, c, :, half(source, xl)],
                target,
            )
    for d, target in zip((1, 2, 3), along_z):
        copies.push(("up", "z", 0, d), mine, there, target)
    for d, target in zip((1, 2, 3), along_y):
        copies.push(("up", "y", 0, 0, d), mine, there, target)
    for source, out, name in halved:
        for d, target in zip((1, 2, 3), along_x):
            copies.push(
                (name, "x", 0, d),
                source.at[:, half(source, xl)],
                out.at[z, xh, c, :, half(source, xl)],
                target,
            )
    for _, out, name in whole:
        block = out.at[z, 1 - xh, c]
        copies.arrived((name, "far"), block, far)
        for d, target in zip((1, 2, 3), along_z):
            copies.push((name, "z", 1, d), block, block, target)
        copies.push((name, "core", 1), block, block, sibling)
    block = o_up.at[z, 1 - xh, c, :, quarter(y)]
    copies.arrived(("up", "far"), block, far)
    for d, target in zip((1, 2, 3), along_z):
        copies.push(("up", "z", 1, d), block, block, target)
    for d, target in zip((1, 2, 3), along_y):
        copies.push(("up", "y", 0, 1, d), block, block, target)
    for dz in (1, 2, 3):
        from_z = step(z, -dz)
        for _, out, name in halved:
            block = out.at[from_z, xh, c, :, half(out, xl)]
            copies.arrived((name, "z", dz), block, device(x, y, from_z, c))
            for d, target in zip((1, 2, 3), along_x):
                copies.push((name, "x", dz, d), block, block, target)
        for flip in (0, 1):
            block = o_up.at[from_z, (xh + flip) % 2, c, :, quarter(y)]
            copies.arrived(("up", "z", flip, dz), block, device(x, y, from_z, c))
            for d, target in zip((1, 2, 3), along_y):
                copies.push(("up", "y", dz, flip, d), block, block, target)
    for copy in stays:
        copy.wait()
    for _, out, name in halved:
        block = out.at[:, xh, c, :, half(out, xl)]
        copies.push((name, "core", 0), block, block, sibling)
    block = o_up.at[:, :, c, :, quarter(y)]
    copies.push(("up", "core", 0), block, block, sibling)
    for dz in (1, 2, 3):
        from_z = step(z, -dz)
        for _, out, name in whole:
            for flip in (0, 1):
                block = out.at[from_z, (xh + flip) % 2, c]
                copies.arrived((name, "z", flip, dz), block, device(x, y, from_z, c))
            block = out.at[from_z, :, c]
            copies.push((name, "core", 1 + dz), block, block, sibling)
    for d in (1, 2, 3):
        from_x, from_y = step(x, -d), step(y, -d)
        for _, out, name in halved:
            for dz in (0, 1, 2, 3):
                block = out.at[step(z, -dz), from_x // 2, c, :, half(out, from_x % 2)]
                copies.arrived((name, "x", dz, d), block, device(from_x, y, z, c))
            block = out.at[:, from_x // 2, c, :, half(out, from_x % 2)]
            copies.push((name, "core", d), block, block, sibling)
        for dz in (0, 1, 2, 3):
            for flip in (0, 1):
                block = o_up.at[step(z, -dz), (xh + flip) % 2, c, :, quarter(from_y)]
                copies.arrived(("up", "y", dz, flip, d), block, device(x, from_y, z, c))
        block = o_up.at[:, :, c, :, quarter(from_y)]
        copies.push(("up", "core", d), block, block, sibling)
    for _, out, name in whole:
        copies.arrived((name, "core", 0), out.at[z, xh, 1 - c], sibling)
        copies.arrived((name, "core", 1), out.at[z, 1 - xh, 1 - c], sibling)
        for dz in (1, 2, 3):
            copies.arrived((name, "core", 1 + dz), out.at[step(z, -dz), :, 1 - c], sibling)
    for d in (0, 1, 2, 3):
        from_x, from_y = step(x, -d), step(y, -d)
        for _, out, name in halved:
            block = out.at[:, from_x // 2, 1 - c, :, half(out, from_x % 2)]
            copies.arrived((name, "core", d), block, sibling)
        block = o_up.at[:, :, 1 - c, :, quarter(from_y)]
        copies.arrived(("up", "core", d), block, sibling)
    copies.finish()


def gather_weights(*shards):
    count = 128
    outs = pl.pallas_call(
        gather_kernel,
        out_shape=tuple(
            jax.ShapeDtypeStruct((4, 2, 2) + shard.shape, shard.dtype) for shard in shards
        ),
        in_specs=[pl.BlockSpec(memory_space=pl.ANY)] * len(shards),
        out_specs=tuple(pl.BlockSpec(memory_space=pl.ANY) for _ in shards),
        scratch_shapes=[
            pltpu.SemaphoreType.DMA((8,)),
            pltpu.SemaphoreType.DMA((count,)),
            pltpu.SemaphoreType.DMA((count,)),
        ],
        compiler_params=pltpu.CompilerParams(collective_id=0, has_side_effects=True),
    )(*shards)
    return tuple(out.reshape((-1,) + out.shape[4:]) for out in outs)


def add_up(parts, out):
    blocks, _, columns = out.shape
    tile = next(t for t in (384, 640, 256, 128) if columns % t == 0)

    @pl.loop(0, blocks * (columns // tile))
    def _(i):
        block = i // (columns // tile)
        cols = pl.ds(pl.multiple_of((i % (columns // tile)) * tile, 128), tile)
        total = parts[0][block, :, cols].astype(jnp.float32)
        for part in parts[1:]:
            total = total + part[block, :, cols].astype(jnp.float32)
        out[block, :, cols] = total.astype(out.dtype)


def scatter_kernel(
    up, qkv, cq, mix, down, mod, cap,
    o_up, o_att, o_mix, o_down, o_mod, o_cap,
    u1, u1s, u2, u2s, u3, u3s,
    a1, a1s, a2, a2s, a3, a3s,
    m1, m1s, m2, m2s, m3, m3s,
    d1, d1s, d2, d2s, t1,
    local, send, recv,
):
    x, y, z, c = place()
    xh, xl = x // 2, x % 2
    seq = y * 2 + xl
    peers = [((seq + e) % 8, z * 4 + xh * 2 + c) for e in range(1, 8)]
    along_x = [device(step(x, d), y, z, c) for d in (1, 2, 3)]
    along_y = [device(x, step(y, d), z, c) for d in (1, 2, 3)]
    along_z = [device(x, y, step(z, d), c) for d in (1, 2, 3)]
    far_x = [device((1 - xh) * 2 + e, y, z, c) for e in (0, 1)]
    greet(peers + far_x + along_z)
    copies = Copies(send, recv)
    width = up.shape[-1] // 4
    columns = lambda q, w: pl.ds(pl.multiple_of(q * w, 128), w)
    side = mix.shape[-1] // 2
    piece = side // 4
    waits = []

    def keep(src, dst):
        copy = pltpu.make_async_copy(src, dst, local.at[len(waits)])
        copy.start()
        waits.append(copy)

    for d in (1, 2, 3):
        to_x, to_y, to_z = step(x, d), step(y, d), step(z, d)
        copies.push(("u1", d), up.at[:, :, :, columns(to_y, width)], u1.at[d], along_y[d - 1])
        copies.push(("a1", d), qkv.at[to_z], a1.at[d, :, :, pl.ds(0, 3 * width)], along_z[d - 1])
        copies.push(("c1", d), cq.at[to_z], a1.at[d, :, :, pl.ds(3 * width, width)], along_z[d - 1])
        copies.push(
            ("m1", d), mix.at[:, to_x // 2, :, columns(to_x % 2, side)], m1.at[d], along_x[d - 1]
        )
    for d in (1, 2, 3):
        copies.push(("d1", d), down.at[step(y, d)], d1.at[d], along_y[d - 1])
    for e in range(1, 8):
        copies.push(("t1", e), mod, t1.at[e], peers[e - 1])
        copies.push(("cap", e), cap, o_cap.at[seq], peers[e - 1])
    keep(up.at[:, :, :, columns(y, width)], u1.at[0])
    keep(qkv.at[z], a1.at[0, :, :, pl.ds(0, 3 * width)])
    keep(cq.at[z], a1.at[0, :, :, pl.ds(3 * width, width)])
    keep(mix.at[:, xh, :, columns(xl, side)], m1.at[0])
    keep(down.at[y], d1.at[0])
    keep(mod, t1.at[0])
    keep(cap, o_cap.at[seq])
    for copy in waits:
        copy.wait()

    for d in (1, 2, 3):
        copies.arrived(("d1", d), d1.at[d], along_y[3 - d])
    add_up([d1.at[pl.ds(i, 1)] for i in range(4)], d1s)
    copies.push(("d2",), d1s, d2, device(xh * 2 + 1 - xl, y, z, c))
    for d in (1, 2, 3):
        copies.arrived(("u1", d), u1.at[d], along_y[3 - d])
    for zz in range(4):
        add_up([u1.at[i, zz] for i in range(4)], u1s.at[zz])
    for d in (1, 2, 3):
        copies.push(("u2", d), u1s.at[step(z, d)], u2.at[d], along_z[d - 1])
    for d in (1, 2, 3):
        copies.arrived(("a1", d), a1.at[d, :, :, pl.ds(0, 3 * width)], along_z[3 - d])
        copies.arrived(("c1", d), a1.at[d, :, :, pl.ds(3 * width, width)], along_z[3 - d])
    add_up([a1.at[i] for i in range(4)], a1s)
    for d in (1, 2, 3):
        copies.push(("a2", d), a1s.at[:, :, columns(step(y, d), width)], a2.at[d], along_y[d - 1])
    for d in (1, 2, 3):
        copies.arrived(("m1", d), m1.at[d], along_x[3 - d])
    add_up([m1.at[i] for i in range(4)], m1s)
    for d in (1, 2, 3):
        copies.push(("m2", d), m1s.at[:, :, columns(step(y, d), piece)], m2.at[d], along_y[d - 1])

    copies.arrived(("d2",), d2, device(xh * 2 + 1 - xl, y, z, c))
    add_up([d1s, d2], d2s)
    keep(d2s.at[0], o_down.at[y])
    for d in (1, 2, 3):
        copies.push(("d3", d), d2s.at[0], o_down.at[y], along_y[d - 1])
    for d in (1, 2, 3):
        copies.arrived(("u2", d), u2.at[d], along_z[3 - d])
    add_up([u1s.at[z]] + [u2.at[d] for d in (1, 2, 3)], u2s)
    for d in (1, 2, 3):
        copies.push(("u3", d), u2s.at[step(x, d) // 2], u3.at[d], along_x[d - 1])
    for d in (1, 2, 3):
        copies.arrived(("a2", d), a2.at[d], along_y[3 - d])
    add_up([a1s.at[:, :, columns(y, width)]] + [a2.at[d] for d in (1, 2, 3)], a2s)
    for d in (1, 2, 3):
        copies.push(("a3", d), a2s.at[step(x, d) // 2], a3.at[d], along_x[d - 1])
    for d in (1, 2, 3):
        copies.arrived(("m2", d), m2.at[d], along_y[3 - d])
    add_up([m1s.at[:, :, columns(y, piece)]] + [m2.at[d] for d in (1, 2, 3)], m2s)
    for d in (1, 2, 3):
        copies.push(("m3", d), m2s.at[step(z, d)], m3.at[d], along_z[d - 1])

    for d in (1, 2, 3):
        copies.arrived(("u3", d), u3.at[d], along_x[3 - d])
    add_up([u2s.at[pl.ds(xh, 1)]] + [u3.at[pl.ds(d, 1)] for d in (1, 2, 3)], u3s)
    keep(u3s.at[0], o_up.at[:, columns(y, width)])
    for d in (1, 2, 3):
        copies.push(("u4", d), u3s.at[0], o_up.at[:, columns(y, width)], along_y[d - 1])
    for d in (1, 2, 3):
        copies.arrived(("a3", d), a3.at[d], along_x[3 - d])
    add_up([a2s.at[pl.ds(xh, 1)]] + [a3.at[pl.ds(d, 1)] for d in (1, 2, 3)], a3s)
    keep(a3s.at[0], o_att.at[:, columns(y, width)])
    for d in (1, 2, 3):
        copies.push(("a4", d), a3s.at[0], o_att.at[:, columns(y, width)], along_y[d - 1])
    for d in (1, 2, 3):
        copies.arrived(("m3", d), m3.at[d], along_z[3 - d])
    add_up([m2s.at[pl.ds(z, 1)]] + [m3.at[pl.ds(d, 1)] for d in (1, 2, 3)], m3s)
    spot = lambda s: columns((s % 2) * 4 + s // 2, piece)
    keep(m3s.at[0], o_mix.at[:, spot(seq)])
    for e in range(1, 8):
        copies.push(("m4", e), m3s.at[0], o_mix.at[:, spot(seq)], peers[e - 1])
    total = t1[0].astype(jnp.float32)
    for e in range(1, 8):
        copies.arrived(("t1", e), t1.at[e], peers[7 - e])
        total = total + t1[e].astype(jnp.float32)
    o_mod[...] = total
    for d in (1, 2, 3):
        from_y = step(y, -d)
        copies.arrived(("d3", d), o_down.at[from_y], along_y[3 - d])
        copies.arrived(("u4", d), o_up.at[:, columns(from_y, width)], along_y[3 - d])
        copies.arrived(("a4", d), o_att.at[:, columns(from_y, width)], along_y[3 - d])
    for e in range(1, 8):
        source = (seq + 8 - e) % 8
        copies.arrived(("cap", e), o_cap.at[source], peers[7 - e])
        copies.arrived(("m4", e), o_mix.at[:, spot(source)], peers[7 - e])
    for copy in waits[7:]:
        copy.wait()
    copies.finish()


def scatter_grads(up, qkv, cq, mix, down, mod, cap):
    width, side = up.shape[-1] // 4, mix.shape[-1] // 2
    piece = side // 4
    vmem = lambda *shape: pltpu.VMEM(shape, jnp.bfloat16)
    count = 64
    anywhere = pl.BlockSpec(memory_space=pl.ANY)
    return pl.pallas_call(
        scatter_kernel,
        out_shape=(
            jax.ShapeDtypeStruct((HD, 4 * width), jnp.bfloat16),
            jax.ShapeDtypeStruct((HD, 4 * width), jnp.bfloat16),
            jax.ShapeDtypeStruct((HD, 2 * side), jnp.bfloat16),
            jax.ShapeDtypeStruct((4, HD, width), jnp.bfloat16),
            jax.ShapeDtypeStruct(mod.shape, jnp.float32),
            jax.ShapeDtypeStruct((8,) + cap.shape, jnp.bfloat16),
        ),
        in_specs=[anywhere] * 7,
        out_specs=(anywhere,) * 4 + (pl.BlockSpec(memory_space=pltpu.VMEM), anywhere),
        scratch_shapes=[
            vmem(4, 4, 2, HD, width), vmem(4, 2, HD, width), vmem(4, 2, HD, width),
            vmem(2, HD, width), vmem(4, HD, width), vmem(1, HD, width),
            vmem(4, 2, HD, 4 * width), vmem(2, HD, 4 * width), vmem(4, 2, HD, width),
            vmem(2, HD, width), vmem(4, HD, width), vmem(1, HD, width),
            vmem(4, 4, HD, side), vmem(4, HD, side), vmem(4, 4, HD, piece),
            vmem(4, HD, piece), vmem(4, HD, piece), vmem(1, HD, piece),
            vmem(4, HD, width), vmem(1, HD, width), vmem(1, HD, width), vmem(1, HD, width),
            vmem(8, *mod.shape),
            pltpu.SemaphoreType.DMA((16,)),
            pltpu.SemaphoreType.DMA((count,)),
            pltpu.SemaphoreType.DMA((count,)),
        ],
        compiler_params=pltpu.CompilerParams(
            collective_id=1, has_side_effects=True, vmem_limit_bytes=48 * 1024 * 1024
        ),
    )(up, qkv, cq, mix, down, mod, cap)


def sibling_pairs():
    return [(i, i + 1 - 2 * (i % 2)) for i in range(16)]


def by_core(matrix):
    core = lax.axis_index("fsdp") % 2
    split = matrix.reshape((8, 2, -1) + matrix.shape[1:])
    pick = lambda which: lax.dynamic_index_in_dim(split, which, 1, keepdims=False).reshape(
        (-1,) + matrix.shape[1:]
    )
    return pick(core), pick(1 - core)


def pair_grad(former, latter):
    own, other = by_core(former.T)
    theirs = project(other, latter).astype(jnp.bfloat16)
    received = lax.ppermute(theirs, "fsdp", sibling_pairs())
    return (project(own, latter) + received.astype(jnp.float32)).astype(jnp.bfloat16)


def on_device(
    latents,
    timestep,
    caption,
    shift_table,
    qkv_weight,
    query_bias,
    value_bias,
    proj_weight,
    proj_bias,
    cross_query,
    cross_qbias,
    cross_kv,
    cross_vbias,
    cross_proj,
    cross_pbias,
    up_weight,
    up_bias,
    down_weight,
    down_bias,
    cotangent,
):
    full_down = lax.all_gather(down_weight, "fsdp", axis=0, tiled=True)
    small = jnp.concatenate(
        [
            shift_table.reshape(HD, 6),
            query_bias.reshape(HD, 1),
            value_bias.reshape(HD, 1),
            proj_bias.reshape(HD, 1),
            cross_qbias.reshape(HD, 1),
            cross_vbias.reshape(HD, 1),
            cross_pbias.reshape(HD, 1),
            down_bias.reshape(HD, 1),
            up_bias.reshape(HD, 4),
        ],
        axis=1,
    )
    small = jnp.pad(small, ((0, 0), (0, 128 - small.shape[1])))
    full_up, full_qkv, full_cquery, full_small, full_ckv, full_pair = gather_weights(
        up_weight,
        qkv_weight,
        cross_query,
        small,
        cross_kv,
        jnp.concatenate([proj_weight, cross_proj], axis=1),
    )
    full_proj, full_cproj = jnp.split(full_pair, 2, axis=1)
    full_table = full_small[:, :6].reshape(-1)
    full_qbias, full_vbias, full_pbias, full_cqbias, full_cvbias, full_cpbias, full_dbias = (
        full_small[:, 6 + i] for i in range(7)
    )
    full_ubias = full_small[:, 13:17].reshape(-1)
    latent_count, local_len, model_width = latents.shape
    inputs = latents.astype(jnp.float32)
    modulation = (full_table.astype(jnp.float32) + timestep.astype(jnp.float32)).reshape(
        latent_count, 6, 1, model_width
    )
    shift_one, scale_one, gate_one = (modulation[:, 0], modulation[:, 1], modulation[:, 2])
    shift_two, scale_two, gate_two = (modulation[:, 3], modulation[:, 4], modulation[:, 5])
    pre_one, pull_one = jax.vjp(modulate, inputs, shift_one, scale_one)
    normed_one = pre_one.astype(jnp.bfloat16)
    qkv_bias = jnp.concatenate([full_qbias, jnp.zeros_like(full_qbias), full_vbias]).astype(
        jnp.float32
    )
    packed = (project(normed_one, full_qkv) + qkv_bias).astype(jnp.bfloat16)
    packed = packed.reshape(latent_count, local_len, 3, model_width)
    head_major = lax.all_to_all(packed, "seq", split_axis=3, concat_axis=1, tiled=True)
    attended, logsum = lax.map(self_forward, head_major)
    tok_major = lax.all_to_all(attended, "seq", split_axis=1, concat_axis=2, tiled=True)
    branch_one = project(tok_major, full_proj) + full_pbias.astype(jnp.float32)
    after_one = inputs + gate_one * branch_one
    middle = after_one.astype(jnp.bfloat16)
    cross_rows = (project(middle, full_cquery) + full_cqbias.astype(jnp.float32)).astype(
        jnp.bfloat16
    )
    kv_bias = jnp.concatenate([jnp.zeros_like(full_cvbias), full_cvbias]).astype(jnp.float32)
    text_kv = (project(caption, full_ckv) + kv_bias).astype(jnp.bfloat16)
    text_keys = by_heads(text_kv[..., :model_width])
    text_values = by_heads(text_kv[..., model_width:])
    cross_heads, cross_logsum = jax.vmap(attend_forward)(
        by_heads(cross_rows), text_keys, text_values
    )
    crossed = cross_heads.reshape(latent_count, local_len, model_width)
    branch_two = project(crossed, full_cproj) + full_cpbias.astype(jnp.float32)
    after_two = after_one + branch_two
    pre_two, pull_two = jax.vjp(modulate, after_two, shift_two, scale_two)
    normed_two = pre_two.astype(jnp.bfloat16)
    hidden = project(normed_two, full_up) + full_ubias.astype(jnp.float32)
    activated, gelu_pull = jax.vjp(jax.nn.gelu, hidden)
    act_rows = activated.astype(jnp.bfloat16)
    branch_three = project(act_rows, full_down) + full_dbias.astype(jnp.float32)
    block_out = (after_two + gate_two * branch_three).astype(jnp.bfloat16)
    grad_out = cotangent.astype(jnp.float32)
    grad_gate_two = jnp.sum(grad_out * branch_three, axis=1, keepdims=True)
    grad_three = (gate_two * grad_out).astype(jnp.bfloat16)
    down_grad = weight_grad(act_rows, grad_three)
    down_bgrad = token_sum(grad_three)
    grad_act = project(grad_three, full_down.T)
    grad_hidden = gelu_pull(grad_act)[0].astype(jnp.bfloat16)
    up_grad = pair_grad(normed_two[0], grad_hidden[0])
    up_bgrad = token_sum(grad_hidden)
    grad_pre_two = project(grad_hidden, full_up.T)
    grad_mid_two, grad_shift_two, grad_scale_two = pull_two(grad_pre_two)
    grad_after_two = grad_out + grad_mid_two
    down_part = lax.psum_scatter(
        down_grad.astype(jnp.bfloat16), "fsdp", scatter_dimension=0, tiled=True
    )
    grad_branch_two = grad_after_two.astype(jnp.bfloat16)
    cproj_grad = pair_grad(crossed[0], grad_branch_two[0])
    cproj_bgrad = token_sum(grad_branch_two)
    grad_crossed = project(grad_branch_two, full_cproj.T).astype(jnp.bfloat16)
    grad_cq, grad_ck, grad_cv = jax.vmap(attend_backward)(
        by_heads(cross_rows), text_keys, text_values, cross_logsum, by_heads(grad_crossed)
    )
    grad_cross_rows = grad_cq.reshape(latent_count, local_len, model_width).astype(jnp.bfloat16)
    cquery_grad = pair_grad(middle[0], grad_cross_rows[0])
    cquery_bgrad = token_sum(grad_cross_rows)
    grad_after_one = grad_after_two + project(grad_cross_rows, full_cquery.T)
    text_partial = jnp.concatenate(
        [
            grad_ck.reshape(grad_ck.shape[:2] + (model_width,)),
            grad_cv.reshape(grad_cv.shape[:2] + (model_width,)),
        ],
        axis=-1,
    )
    text_piece = text_partial.shape[1] // 8
    text_pieces = lax.all_to_all(
        text_partial[0].astype(jnp.bfloat16).reshape(8, text_piece, -1), "seq", 0, 0
    )
    text_grad = jnp.sum(text_pieces.astype(jnp.float32), axis=0).astype(jnp.bfloat16)
    caption_part = lax.dynamic_slice_in_dim(
        caption[0], lax.axis_index("seq") * text_piece, text_piece, 0
    )
    ckv_grad = pair_grad(caption_part, text_grad)
    cvalue_bgrad = jnp.sum(text_grad[:, model_width:].astype(jnp.float32), axis=0)
    caption_piece = project(text_grad, full_ckv.T)
    grad_gate_one = jnp.sum(grad_after_one * branch_one, axis=1, keepdims=True)
    grad_branch_one = (gate_one * grad_after_one).astype(jnp.bfloat16)
    proj_grad = pair_grad(tok_major[0], grad_branch_one[0])
    proj_bgrad = token_sum(grad_branch_one)
    grad_tok = project(grad_branch_one, full_proj.T).astype(jnp.bfloat16)
    grad_heads = lax.all_to_all(grad_tok, "seq", split_axis=2, concat_axis=1, tiled=True)
    grad_packed_heads = lax.map(self_backward, (head_major, logsum, grad_heads))
    grad_packed = lax.all_to_all(grad_packed_heads, "seq", split_axis=1, concat_axis=3, tiled=True)
    grad_flat = grad_packed.reshape(latent_count, local_len, 3 * model_width)
    qkv_grad = pair_grad(normed_one[0], grad_flat[0])
    qbias_grad = token_sum(grad_packed[:, :, 0])
    vbias_grad = token_sum(grad_packed[:, :, 2])
    grad_pre_one = project(grad_flat, full_qkv.T)
    grad_norm_one, grad_shift_one, grad_scale_one = pull_one(grad_pre_one)
    grad_latents = grad_after_one + grad_norm_one
    grad_mod = jnp.concatenate(
        [
            grad_shift_one,
            grad_scale_one,
            grad_gate_one,
            grad_shift_two,
            grad_scale_two,
            grad_gate_two,
        ],
        axis=1,
    )
    grad_mod = grad_mod.reshape(latent_count, 6 * model_width)
    small_grad = jnp.concatenate(
        [
            grad_mod.reshape(-1, 6),
            qbias_grad.reshape(-1, 1),
            vbias_grad.reshape(-1, 1),
            proj_bgrad.reshape(-1, 1),
            cquery_bgrad.reshape(-1, 1),
            cvalue_bgrad.reshape(-1, 1),
            cproj_bgrad.reshape(-1, 1),
            down_bgrad.reshape(-1, 1),
            up_bgrad.reshape(-1, 4),
        ],
        axis=1,
    )
    small_own, small_other = by_core(small_grad)
    small_sum = small_own + lax.ppermute(
        small_other.astype(jnp.bfloat16), "fsdp", sibling_pairs()
    ).astype(jnp.float32)
    mix = jnp.concatenate(
        [
            proj_grad,
            ckv_grad,
            cproj_grad,
            jnp.pad(small_sum.astype(jnp.bfloat16), ((0, 0), (0, 512 - small_sum.shape[1]))),
        ],
        axis=1,
    )
    blocks = lambda grad: grad.reshape(4, 2, HD, -1)
    sum_up, sum_att, sum_mix, sum_down, sum_mod, caption_all = scatter_grads(
        blocks(up_grad),
        blocks(qkv_grad),
        blocks(cquery_grad),
        blocks(mix),
        down_part.reshape(4, HD, model_width),
        jnp.pad(grad_mod.astype(jnp.bfloat16).reshape(-1, 128), ((0, 10), (0, 0))),
        jnp.pad(caption_piece.astype(jnp.bfloat16), ((0, 1), (0, 0))),
    )
    wide = lambda part: part.astype(jnp.float32)
    sum_small = wide(sum_mix[:, 4 * model_width : 4 * model_width + 17])
    return (
        block_out,
        grad_latents,
        sum_mod[:54].reshape(1, -1),
        wide(caption_all[:, :text_piece].reshape(1, -1, model_width)),
        sum_small[:, :6].reshape(-1),
        wide(sum_att[:, : 3 * model_width]),
        sum_small[:, 6],
        sum_small[:, 7],
        wide(sum_mix[:, :model_width]),
        sum_small[:, 8],
        wide(sum_att[:, 3 * model_width :]),
        sum_small[:, 9],
        wide(sum_mix[:, model_width : 3 * model_width]),
        sum_small[:, 10],
        wide(sum_mix[:, 3 * model_width : 4 * model_width]),
        sum_small[:, 11],
        wide(sum_up),
        sum_small[:, 13:17].reshape(-1),
        wide(sum_down.reshape(4 * HD, model_width)),
        sum_small[:, 12],
    )


def solution(mesh):
    placed = (
        P("fsdp", "seq", None),
        P("fsdp", None),
        P("fsdp", None, None),
        P("fsdp"),
        P("fsdp", None),
        P("fsdp"),
        P("fsdp"),
        P("fsdp", None),
        P("fsdp"),
        P("fsdp", None),
        P("fsdp"),
        P("fsdp", None),
        P("fsdp"),
        P("fsdp", None),
        P("fsdp"),
        P("fsdp", None),
        P("fsdp"),
        P("fsdp", None),
        P("fsdp"),
        P("fsdp", "seq", None),
    )
    return jax.shard_map(
        on_device,
        mesh=mesh,
        in_specs=placed,
        out_specs=(
            P("fsdp", "seq", None),
            P("fsdp", "seq", None),
            P("fsdp", None),
            P("fsdp", None, None),
            P("fsdp"),
            P("fsdp", None),
            P("fsdp"),
            P("fsdp"),
            P("fsdp", None),
            P("fsdp"),
            P("fsdp", None),
            P("fsdp"),
            P("fsdp", None),
            P("fsdp"),
            P("fsdp", None),
            P("fsdp"),
            P("fsdp", None),
            P("fsdp"),
            P("fsdp", None),
            P("fsdp"),
        ),
        check_vma=False,
    )
```

```python
import functools

import jax
import jax.numpy as jnp
from jax import lax
from jax.experimental import pallas as pl
from jax.experimental.pallas import tpu as pltpu
from jax.sharding import PartitionSpec as P

HD = 72
MESH = pl.DeviceIdType.MESH


epsilon = 1e-06


def for_sending(array):

    def short(part):
        return part.astype(jnp.bfloat16) if part.dtype == jnp.float32 else part

    return jax.tree.map(short, array)


def normalize(values):
    centre = values - jnp.mean(values, axis=-1, keepdims=True)
    spread = jnp.mean(centre * centre, axis=-1, keepdims=True)
    return centre * lax.rsqrt(spread + epsilon)


def modulate(values, shift, scale):
    return normalize(values) * (1.0 + scale) + shift


def project(former, latter):
    return jnp.dot(former, latter, preferred_element_type=jnp.float32)


def weight_grad(former, latter):
    return jnp.einsum("bli,blo->io", former, latter, preferred_element_type=jnp.float32)


def token_sum(values):
    return jnp.sum(values.astype(jnp.float32), axis=(0, 1))


def by_heads(matrix):
    return matrix.reshape(matrix.shape[:-1] + (matrix.shape[-1] // HD, HD))


def attend_forward(queries, key_rows, values):
    factor = HD ** (-0.5)
    scores = (
        jnp.einsum("qhd,khd->hqk", queries, key_rows, preferred_element_type=jnp.float32) * factor
    )
    largest = jnp.max(scores, axis=-1, keepdims=True)
    exponent = jnp.exp(scores - largest)
    partition = jnp.sum(exponent, axis=-1, keepdims=True)
    weights = (exponent / partition).astype(jnp.bfloat16)
    output = jnp.einsum("hqk,khd->qhd", weights, values, preferred_element_type=jnp.float32)
    return (output.astype(jnp.bfloat16), largest + jnp.log(partition))


def attend_backward(queries, key_rows, values, logsum, grad_out):
    factor = HD ** (-0.5)
    scores = (
        jnp.einsum("qhd,khd->hqk", queries, key_rows, preferred_element_type=jnp.float32) * factor
    )
    weights = jnp.exp(scores - logsum)
    grad_weights = jnp.einsum("qhd,khd->hqk", grad_out, values, preferred_element_type=jnp.float32)
    inner = jnp.sum(weights * grad_weights, axis=-1, keepdims=True)
    grad_scores = (weights * (grad_weights - inner)).astype(jnp.bfloat16)
    grad_q = (
        jnp.einsum("hqk,khd->qhd", grad_scores, key_rows, preferred_element_type=jnp.float32)
        * factor
    )
    grad_k = (
        jnp.einsum("hqk,qhd->khd", grad_scores, queries, preferred_element_type=jnp.float32)
        * factor
    )
    grad_v = jnp.einsum(
        "hqk,qhd->khd", weights.astype(jnp.bfloat16), grad_out, preferred_element_type=jnp.float32
    )
    return (grad_q, grad_k, grad_v)


def place():
    seq, fsdp = lax.axis_index("seq"), lax.axis_index("fsdp")
    y, x_lo = seq // 2, seq % 2
    z, rest = fsdp // 4, fsdp % 4
    x_hi, core = rest // 2, rest % 2
    return x_hi * 2 + x_lo, y, z, core


def device(x, y, z, core):
    return (y * 2 + x % 2, z * 4 + (x // 2) * 2 + core)


def step(value, by):
    return (value + by + 4) % 4


class Copies:
    def __init__(self, send, recv):
        self.send, self.recv, self.index, self.started = send, recv, {}, []

    def number(self, key):
        return self.index.setdefault(key, len(self.index))

    def push(self, key, src, dst, target):
        at = self.number(key)
        copy = pltpu.make_async_remote_copy(
            src_ref=src,
            dst_ref=dst,
            send_sem=self.send.at[at],
            recv_sem=self.recv.at[at],
            device_id=target,
            device_id_type=MESH,
        )
        copy.start()
        self.started.append(copy)

    def arrived(self, key, dst, source):
        at = self.number(key)
        pltpu.make_async_remote_copy(
            src_ref=dst,
            dst_ref=dst,
            send_sem=self.send.at[at],
            recv_sem=self.recv.at[at],
            device_id=source,
            device_id_type=MESH,
        ).wait_recv()

    def finish(self):
        for copy in self.started:
            copy.wait_send()


def greet(others):
    barrier = pltpu.get_barrier_semaphore()
    for other in others:
        pl.semaphore_signal(barrier, inc=1, device_id=other, device_id_type=MESH)
    pl.semaphore_wait(barrier, len(others))


class Piece:
    def __init__(self, source, out, axis, dim, start, size):
        self.source, self.out, self.axis = source, out, axis
        self.dim, self.start, self.size = dim, start, size

    def cut(self, part):
        parts = {"x": 2, "y": 4, "z": 1}[self.axis]
        size = self.size // parts
        unit = 128 if self.dim == 1 else 16
        start = self.start if parts == 1 else pl.multiple_of(self.start + part * size, unit)
        window = pl.ds(start, size)
        return (slice(None), window) if self.dim == 1 else (window, slice(None))


class Gather:
    def __init__(self, pieces, copies, local):
        self.pieces, self.copies, self.local = pieces, copies, local
        self.x, self.y, self.z, self.c = x, y, z, c = place()
        self.xh, self.xl = x // 2, x % 2
        self.sibling = device(x, y, z, 1 - c)
        self.far = device(step(x, 2), y, z, c)
        self.lines = {
            "x": [device(step(x, d), y, z, c) for d in (1, 2, 3)],
            "y": [device(x, step(y, d), z, c) for d in (1, 2, 3)],
            "z": [device(x, y, step(z, d), c) for d in (1, 2, 3)],
        }
        self.part = {"x": self.xl, "y": y, "z": 0}

    def others(self):
        return [self.sibling] + self.lines["x"] + self.lines["y"] + self.lines["z"]

    def block(self, p, dz, flip, part, core=None):
        core = self.c if core is None else core
        return p.out.at[(step(self.z, -dz), (self.xh + flip) % 2, core) + p.cut(part)]

    def both(self, key, src, dst, axis):
        self.copies.push(key + (1,), src, dst, self.lines[axis][0])
        self.copies.push(key + (3,), src, dst, self.lines[axis][2])

    def first(self):
        self.stays = []
        for n, p in enumerate(self.pieces):
            mine = p.source.at[p.cut(self.part[p.axis])]
            there = self.block(p, 0, 0, self.part[p.axis])
            copy = pltpu.make_async_copy(mine, there, self.local.at[n])
            copy.start()
            self.stays.append(copy)
            if p.axis != "x":
                self.copies.push((n, "far"), mine, there, self.far)
            if p.axis != "z":
                for d in (1, 2, 3):
                    self.copies.push((n, "mid", 0, d), mine, there, self.lines["z"][d - 1])
        for n, p in enumerate(self.pieces):
            mine = p.source.at[p.cut(self.part[p.axis])]
            self.both((n, "end", 0, 0), mine, self.block(p, 0, 0, self.part[p.axis]), p.axis)

    def second(self):
        for n, p in enumerate(self.pieces):
            if p.axis == "x":
                continue
            block = self.block(p, 0, 1, self.part[p.axis])
            self.copies.arrived((n, "far"), block, self.far)
            if p.axis == "y":
                for d in (1, 2, 3):
                    self.copies.push((n, "mid", 1, d), block, block, self.lines["z"][d - 1])
            self.both((n, "end", 0, 1), block, block, p.axis)

    def third(self):
        for dz in (1, 3, 2):
            for n, p in enumerate(self.pieces):
                if p.axis == "z":
                    continue
                for flip in (0, 1) if p.axis == "y" else (0,):
                    block = self.block(p, dz, flip, self.part[p.axis])
                    self.copies.arrived((n, "mid", flip, dz), block, self.lines["z"][3 - dz])
                    self.both((n, "end", dz, flip), block, block, p.axis)

    def blocks(self, p):
        if p.axis == "z":
            return ((0, 0), (0, 1))
        return tuple((dz, f) for dz in (0, 1, 3, 2) for f in ((0, 1) if p.axis == "y" else (0,)))

    def ended(self, n, p, dz, flip, d):
        if p.axis == "z":
            block = self.block(p, d, flip, 0)
        elif p.axis == "y":
            block = self.block(p, dz, flip, step(self.y, -d))
        else:
            from_x = step(self.x, -d)
            block = p.out.at[(step(self.z, -dz), from_x // 2, self.c) + p.cut(from_x % 2)]
        self.copies.arrived((n, "end", dz, flip, d), block, self.lines[p.axis][3 - d])
        return block

    def group(self, p, d, core):
        if p.axis == "z":
            return p.out.at[(step(self.z, -d), slice(None), core) + p.cut(0)]
        if p.axis == "y":
            return p.out.at[(slice(None), slice(None), core) + p.cut(step(self.y, -d))]
        from_x = step(self.x, -d)
        return p.out.at[(slice(None), from_x // 2, core) + p.cut(from_x % 2)]

    def share(self, n, p, d):
        block = self.group(p, d, self.c)
        self.copies.push((n, "core", d), block, block, self.sibling)

    def fourth(self):
        for copy in self.stays:
            copy.wait()
        for n, p in enumerate(self.pieces):
            self.share(n, p, 0)
        for at in range(8):
            for n, p in enumerate(self.pieces):
                if at >= len(self.blocks(p)):
                    continue
                dz, flip = self.blocks(p)[at]
                line = self.lines[p.axis]
                for d in (1, 3):
                    block = self.ended(n, p, dz, flip, d)
                    if (at % 2 == 0) == (d == 1):
                        on = line[0] if d == 1 else line[2]
                        self.copies.push((n, "end", dz, flip, 2), block, block, on)
                if at == len(self.blocks(p)) - 1:
                    self.share(n, p, 1)
                    self.share(n, p, 3)

    def last(self):
        for n, p in enumerate(self.pieces):
            for dz, flip in self.blocks(p):
                self.ended(n, p, dz, flip, 2)
            self.share(n, p, 2)
        for d in (0, 1, 3, 2):
            for n, p in enumerate(self.pieces):
                block = self.group(p, d, 1 - self.c)
                self.copies.arrived((n, "core", d), block, self.sibling)


def early_kernel(qkv, small, o_qkv, o_small, local, send, recv):
    pieces = [
        Piece(small, o_small, "z", 0, 0, small.shape[0]),
        Piece(qkv, o_qkv, "z", 1, 18 * 128, 9 * 128),
        Piece(qkv, o_qkv, "x", 1, 8 * 128, 10 * 128),
        Piece(qkv, o_qkv, "y", 1, 0, 8 * 128),
    ]
    copies = Copies(send, recv)
    work = Gather(pieces, copies, local)
    greet(work.others())
    work.first()
    work.second()
    work.third()
    work.fourth()
    work.last()
    copies.finish()


def head_slices(rows):
    for j in range(rows.shape[1] // (16 * HD)):
        for h in range(16):
            at = j * 16 * HD + h * HD
            yield h // 2, 2 * j + h % 2, at


def exchange(copies, name, seq, peers, sent, got, local):
    for e in range(1, 8):
        copies.push((name, e), sent.at[(seq + e) % 8], got.at[seq], peers[e - 1])
    copy = pltpu.make_async_copy(sent.at[seq], got.at[seq], local)
    copy.start()
    return copy


def exchanged(copies, name, seq, peers, got, copy):
    copy.wait()
    for e in range(1, 8):
        copies.arrived((name, e), got.at[(seq + 8 - e) % 8], peers[7 - e])


def seq_peers():
    x, y, z, c = place()
    seq = y * 2 + x % 2
    return seq, [((seq + e) % 8, z * 4 + (x // 2) * 2 + c) for e in range(1, 8)]


def unique(x, y, z, c, extra):
    _, peers = seq_peers()
    far = [device((1 - x // 2) * 2 + e, y, z, c) for e in (0, 1)]
    return peers + far + [device(x, y, step(z, d), c) for d in (1, 2, 3)] + extra


CHUNK = 256


def attend(heads, h, out):
    tokens = 8 * 128
    keys = heads[:, 2 + h].reshape(tokens, HD)
    values = heads[:, 4 + h].reshape(tokens, HD)

    @pl.loop(0, tokens // CHUNK)
    def _(i):
        queries = heads[pl.ds(i * 2, 2), h].reshape(CHUNK, HD)
        scores = lax.dot_general(
            queries, keys, (((1,), (1,)), ((), ())), preferred_element_type=jnp.float32
        ) * (HD**-0.5)
        exponent = jnp.exp(scores - jnp.max(scores, axis=1, keepdims=True))
        weights = exponent * (1.0 / jnp.sum(exponent, axis=1, keepdims=True))
        got = jnp.dot(weights.astype(jnp.bfloat16), values, preferred_element_type=jnp.float32)
        out[pl.ds(i * 2, 2), h] = got.astype(jnp.bfloat16).reshape(2, 128, HD)


def attend_back(heads, grads, h, out, key_sum, value_sum):
    tokens = 8 * 128
    keys = heads[:, 2 + h].reshape(tokens, HD)
    values = heads[:, 4 + h].reshape(tokens, HD)
    key_sum[...] = jnp.zeros_like(key_sum)
    value_sum[...] = jnp.zeros_like(value_sum)
    across = (((1,), (1,)), ((), ()))

    @pl.loop(0, tokens // CHUNK)
    def _(i):
        queries = heads[pl.ds(i * 2, 2), h].reshape(CHUNK, HD)
        grad = grads[pl.ds(i * 2, 2), h].reshape(CHUNK, HD)
        scores = lax.dot_general(
            keys, queries, across, preferred_element_type=jnp.float32
        ) * (HD**-0.5)
        exponent = jnp.exp(scores - jnp.max(scores, axis=0, keepdims=True))
        weights = exponent * (1.0 / jnp.sum(exponent, axis=0, keepdims=True))
        grad_weights = lax.dot_general(values, grad, across, preferred_element_type=jnp.float32)
        inner = jnp.sum(weights * grad_weights, axis=0, keepdims=True)
        grad_scores = (weights * (grad_weights - inner)).astype(jnp.bfloat16)
        value_sum[...] += jnp.dot(
            weights.astype(jnp.bfloat16), grad, preferred_element_type=jnp.float32
        )
        key_sum[...] += jnp.dot(grad_scores, queries, preferred_element_type=jnp.float32)
        grad_q = lax.dot_general(
            grad_scores, keys, (((0,), (0,)), ((), ())), preferred_element_type=jnp.float32
        ) * (HD**-0.5)
        out[pl.ds(i * 2, 2), h] = grad_q.astype(jnp.bfloat16).reshape(2, 128, HD)

    out[:, 2 + h] = (key_sum[...] * (HD**-0.5)).astype(jnp.bfloat16).reshape(8, 128, HD)
    out[:, 4 + h] = value_sum[...].astype(jnp.bfloat16).reshape(8, 128, HD)


def late_kernel(
    up, cq, ckv, pair, down, packed,
    o_up, o_cq, o_ckv, o_pair, o_down, o_heads, o_rows,
    sent, heads, mixed, joined, local, send, recv,
):
    height = down.shape[0]
    pieces = [
        Piece(cq, o_cq, "z", 1, 0, cq.shape[1]),
        Piece(ckv, o_ckv, "z", 1, 0, ckv.shape[1]),
        Piece(pair, o_pair, "x", 1, 0, pair.shape[1]),
        Piece(up, o_up, "y", 1, 0, up.shape[1]),
        Piece(down, o_down, "x", 0, 128, height - 128),
        Piece(down, o_down, "y", 0, 0, 128),
    ]
    copies = Copies(send, recv)
    work = Gather(pieces, copies, local)
    seq, peers = seq_peers()
    greet(unique(work.x, work.y, work.z, work.c, [work.sibling]))
    for to, what, at in head_slices(packed):
        sent[to, what] = packed[:, at : at + HD]
    own = exchange(copies, "in", seq, peers, sent, heads, local.at[6])
    work.first()
    exchanged(copies, "in", seq, peers, heads, own)
    keep = pltpu.make_async_copy(heads, o_heads, local.at[7])
    keep.start()
    attend(heads, 0, mixed)
    work.second()
    attend(heads, 1, mixed)
    own = exchange(copies, "out", seq, peers, mixed, joined, local.at[8])
    work.third()
    work.fourth()
    exchanged(copies, "out", seq, peers, joined, own)
    for at, what, to in head_slices(o_rows):
        o_rows[:, to : to + HD] = joined[at, what]
    work.last()
    keep.wait()
    copies.finish()


def whole(out):
    return out.reshape((-1,) + out.shape[4:])


def full_shapes(shards):
    return tuple(jax.ShapeDtypeStruct((4, 2, 2) + s.shape, s.dtype) for s in shards)


def semaphores(*counts):
    return [pltpu.SemaphoreType.DMA((n,)) for n in counts]


ANYWHERE = pl.BlockSpec(memory_space=pl.ANY)
ON_CHIP = pl.BlockSpec(memory_space=pltpu.VMEM)


def parameters(collective):
    return pltpu.CompilerParams(
        collective_id=collective, has_side_effects=True, vmem_limit_bytes=48 * 1024 * 1024
    )


def gather_early(*shards):
    outs = pl.pallas_call(
        early_kernel,
        out_shape=full_shapes(shards),
        in_specs=[ANYWHERE] * 2,
        out_specs=(ANYWHERE,) * 2,
        scratch_shapes=semaphores(4, 128, 128),
        compiler_params=parameters(0),
    )(*shards)
    return tuple(whole(out) for out in outs)


def gather_late(shards, packed):
    bf16 = lambda *shape: jax.ShapeDtypeStruct(shape, jnp.bfloat16)
    vmem = lambda *shape: pltpu.VMEM(shape, jnp.bfloat16)
    outs = pl.pallas_call(
        late_kernel,
        out_shape=full_shapes(shards) + (bf16(8, 6, 128, HD), bf16(128, 16 * HD)),
        in_specs=[ANYWHERE] * 5 + [ON_CHIP],
        out_specs=(ANYWHERE,) * 6 + (ON_CHIP,),
        scratch_shapes=[
            vmem(8, 6, 128, HD), vmem(8, 6, 128, HD), vmem(8, 2, 128, HD), vmem(8, 2, 128, HD),
        ]
        + semaphores(9, 256, 256),
        compiler_params=parameters(1),
    )(*shards, packed)
    return tuple(whole(out) for out in outs[:5]) + outs[5:]


def add_up(parts, out):
    blocks, _, columns = out.shape
    tile = next(t for t in (384, 512, 256, 128) if columns % t == 0)

    @pl.loop(0, blocks * (columns // tile))
    def _(i):
        block = i // (columns // tile)
        cols = pl.ds(pl.multiple_of((i % (columns // tile)) * tile, 128), tile)
        total = parts[0][block, :, cols].astype(jnp.float32)
        for part in parts[1:]:
            total = total + part[block, :, cols].astype(jnp.float32)
        out[block, :, cols] = total.astype(out.dtype)


def columns(part, width, start=0):
    return pl.ds(pl.multiple_of(start + part * width, 128), width)


class Scatter:
    def __init__(self, by_y, by_x, by_z, outs, scratch, copies, keep):
        self.by_y, self.by_x, self.by_z = by_y, by_x, by_z
        self.o_up, self.o_mix, self.o_att = outs
        self.scratch, self.copies, self.keep = scratch, copies, keep
        self.x, self.y, self.z, self.c = x, y, z, c = place()
        self.xh, self.xl = x // 2, x % 2
        self.seq, self.peers = seq_peers()
        self.along_x = [device(step(x, d), y, z, c) for d in (1, 2, 3)]
        self.along_y = [device(x, step(y, d), z, c) for d in (1, 2, 3)]
        self.along_z = [device(x, y, step(z, d), c) for d in (1, 2, 3)]

    @staticmethod
    def buffers(by_y, by_x, by_z):
        vmem = lambda *shape: pltpu.VMEM(shape, jnp.bfloat16)
        wy, wx, wz = by_y // 4, by_x // 2, by_z
        return [
            vmem(4, 4, 2, HD, wy), vmem(4, 2, HD, wy), vmem(4, 2, HD, wy),
            vmem(2, HD, wy), vmem(4, HD, wy), vmem(1, HD, wy),
            vmem(4, 2, HD, wz), vmem(2, HD, wz), vmem(4, 2, HD, wz // 4),
            vmem(2, HD, wz // 4), vmem(4, HD, wz // 4), vmem(1, HD, wz // 4),
            vmem(4, 4, HD, wx), vmem(4, HD, wx), vmem(4, 4, HD, wx // 4),
            vmem(4, HD, wx // 4), vmem(4, HD, wx // 4), vmem(1, HD, wx // 4),
        ]

    def first(self):
        u1, a1, m1 = self.scratch[0], self.scratch[6], self.scratch[12]
        up, up_at, up_size = self.by_y
        mix, mix_at, mix_size = self.by_x
        for d in (1, 2, 3):
            to_x, to_y, to_z = step(self.x, d), step(self.y, d), step(self.z, d)
            cols = columns(to_y, up_size // 4, up_at)
            self.copies.push(("u1", d), up.at[:, :, :, cols], u1.at[d], self.along_y[d - 1])
            cols = columns(to_x % 2, mix_size // 2, mix_at)
            self.copies.push(
                ("m1", d), mix.at[:, to_x // 2, :, cols], m1.at[d], self.along_x[d - 1]
            )
            at = 0
            for n, (source, start, size) in enumerate(self.by_z):
                self.copies.push(
                    ("a1", n, d),
                    source.at[to_z, :, :, pl.ds(start, size)],
                    a1.at[d, :, :, pl.ds(at, size)],
                    self.along_z[d - 1],
                )
                at += size
        self.keep(up.at[:, :, :, columns(self.y, up_size // 4, up_at)], u1.at[0])
        self.keep(mix.at[:, self.xh, :, columns(self.xl, mix_size // 2, mix_at)], m1.at[0])
        at = 0
        for source, start, size in self.by_z:
            self.keep(
                source.at[self.z, :, :, pl.ds(start, size)], a1.at[0, :, :, pl.ds(at, size)]
            )
            at += size

    def second(self):
        u1, u1s, u2 = self.scratch[:3]
        a1, a1s, a2 = self.scratch[6:9]
        m1, m1s, m2 = self.scratch[12:15]
        for d in (1, 2, 3):
            at = 0
            for n, (_, _, size) in enumerate(self.by_z):
                got = a1.at[d, :, :, pl.ds(at, size)]
                self.copies.arrived(("a1", n, d), got, self.along_z[3 - d])
                at += size
        add_up([a1.at[i] for i in range(4)], a1s)
        for d in (1, 2, 3):
            cols = columns(step(self.y, d), a2.shape[-1])
            self.copies.push(("a2", d), a1s.at[:, :, cols], a2.at[d], self.along_y[d - 1])
        for d in (1, 2, 3):
            self.copies.arrived(("m1", d), m1.at[d], self.along_x[3 - d])
        add_up([m1.at[i] for i in range(4)], m1s)
        for d in (1, 2, 3):
            cols = columns(step(self.y, d), m2.shape[-1])
            self.copies.push(("m2", d), m1s.at[:, :, cols], m2.at[d], self.along_y[d - 1])
        for d in (1, 2, 3):
            self.copies.arrived(("u1", d), u1.at[d], self.along_y[3 - d])
        for zz in range(4):
            add_up([u1.at[i, zz] for i in range(4)], u1s.at[zz])
        for d in (1, 2, 3):
            self.copies.push(
                ("u2", d), u1s.at[step(self.z, d)], u2.at[d], self.along_z[d - 1]
            )

    def third(self):
        u1s, u2, u2s, u3 = self.scratch[1:5]
        a1s, a2, a2s, a3 = self.scratch[7:11]
        m1s, m2, m2s, m3 = self.scratch[13:17]
        for d in (1, 2, 3):
            self.copies.arrived(("a2", d), a2.at[d], self.along_y[3 - d])
        add_up(
            [a1s.at[:, :, columns(self.y, a2.shape[-1])]] + [a2.at[d] for d in (1, 2, 3)], a2s
        )
        for d in (1, 2, 3):
            to = step(self.x, d) // 2
            self.copies.push(("a3", d), a2s.at[to], a3.at[d], self.along_x[d - 1])
        for d in (1, 2, 3):
            self.copies.arrived(("m2", d), m2.at[d], self.along_y[3 - d])
        add_up(
            [m1s.at[:, :, columns(self.y, m2.shape[-1])]] + [m2.at[d] for d in (1, 2, 3)], m2s
        )
        for d in (1, 2, 3):
            self.copies.push(("m3", d), m2s.at[step(self.z, d)], m3.at[d], self.along_z[d - 1])
        for d in (1, 2, 3):
            self.copies.arrived(("u2", d), u2.at[d], self.along_z[3 - d])
        add_up([u1s.at[self.z]] + [u2.at[d] for d in (1, 2, 3)], u2s)
        for d in (1, 2, 3):
            to = step(self.x, d) // 2
            self.copies.push(("u3", d), u2s.at[to], u3.at[d], self.along_x[d - 1])

    def fourth(self):
        u2s, u3, u3s = self.scratch[3:6]
        a2s, a3, a3s = self.scratch[9:12]
        m2s, m3, m3s = self.scratch[15:18]
        for name, line, sums, got, total, out, mine in (
            ("a", self.along_x, a2s, a3, a3s, self.o_att, self.xh),
            ("u", self.along_x, u2s, u3, u3s, self.o_up, self.xh),
            ("m", self.along_z, m2s, m3, m3s, self.o_mix, self.z),
        ):
            for d in (1, 2, 3):
                self.copies.arrived((name + "3", d), got.at[d], line[3 - d])
            add_up([sums.at[pl.ds(mine, 1)]] + [got.at[pl.ds(d, 1)] for d in (1, 2, 3)], total)
            if name == "m":
                spot = out.at[:, self.spot(self.seq)]
                for e in range(1, 8):
                    self.copies.push(("m4", e), total.at[0], spot, self.peers[e - 1])
            else:
                spot = out.at[:, columns(self.y, total.shape[-1])]
                for d in (1, 2, 3):
                    self.copies.push((name + "4", d), total.at[0], spot, self.along_y[d - 1])
            self.keep(total.at[0], spot)

    def spot(self, seq):
        return columns((seq % 2) * 4 + seq // 2, self.scratch[17].shape[-1])

    def last(self):
        for d in (1, 2, 3):
            from_y = step(self.y, -d)
            for name, out in (("u4", self.o_up), ("a4", self.o_att)):
                got = out.at[:, columns(from_y, out.shape[-1] // 4)]
                self.copies.arrived((name, d), got, self.along_y[3 - d])
        for e in range(1, 8):
            got = self.o_mix.at[:, self.spot((self.seq + 8 - e) % 8)]
            self.copies.arrived(("m4", e), got, self.peers[7 - e])


class Stays:
    def __init__(self, local):
        self.local, self.copies, self.done = local, [], 0

    def __call__(self, src, dst):
        copy = pltpu.make_async_copy(src, dst, self.local.at[len(self.copies)])
        copy.start()
        self.copies.append(copy)

    def wait(self):
        for copy in self.copies[self.done :]:
            copy.wait()
        self.done = len(self.copies)


def back_kernel(
    up, mix, heads, grad_rows, o_up, o_mix, o_att, o_flat,
    sent, grads, mixed, joined, key_sum, value_sum, *rest,
):
    scratch, (local, send, recv) = rest[:18], rest[18:]
    copies, keep = Copies(send, recv), Stays(local)
    half = mix.shape[-1] // 2
    work = Scatter(
        (up, 0, up.shape[-1]), (mix, 0, half), [(mix, half, half)],
        (o_up, o_mix, o_att), scratch, copies, keep,
    )
    seq, peers = seq_peers()
    greet(unique(work.x, work.y, work.z, work.c, []))
    for to, what, at in head_slices(grad_rows):
        sent[to, what] = grad_rows[:, at : at + HD]
    own = exchange(copies, "in", seq, peers, sent, grads, local.at[16])
    work.first()
    exchanged(copies, "in", seq, peers, grads, own)
    for h in (0, 1):
        attend_back(heads, grads, h, mixed, key_sum, value_sum)
    own = exchange(copies, "out", seq, peers, mixed, joined, local.at[17])
    keep.wait()
    work.second()
    work.third()
    exchanged(copies, "out", seq, peers, joined, own)
    for at, what, to in head_slices(o_flat):
        o_flat[:, to : to + HD] = joined[at, what]
    work.fourth()
    work.last()
    keep.wait()
    copies.finish()


def scatter_back(up, mix, heads, grad_rows):
    half = mix.shape[-1] // 2
    bf16 = lambda *shape: jax.ShapeDtypeStruct(shape, jnp.bfloat16)
    vmem = lambda *shape: pltpu.VMEM(shape, jnp.bfloat16)
    return pl.pallas_call(
        back_kernel,
        out_shape=(
            bf16(HD, up.shape[-1]), bf16(HD, half), bf16(HD, half), bf16(128, 48 * HD),
        ),
        in_specs=[ANYWHERE] * 2 + [ON_CHIP] * 2,
        out_specs=(ANYWHERE,) * 3 + (ON_CHIP,),
        scratch_shapes=[
            vmem(8, 2, 128, HD), vmem(8, 2, 128, HD), vmem(8, 6, 128, HD), vmem(8, 6, 128, HD),
            pltpu.VMEM((1024, HD), jnp.float32), pltpu.VMEM((1024, HD), jnp.float32),
        ]
        + Scatter.buffers(up.shape[-1], half, half)
        + semaphores(18, 64, 64),
        compiler_params=parameters(2),
    )(up, mix, heads, grad_rows)


def rest_kernel(
    qkv, small, down, mod, cap, o_up, o_mix, o_att, o_down, o_mod, o_cap,
    d1, d1s, d2, d2s, t1, *rest,
):
    scratch, (local, send, recv) = rest[:18], rest[18:]
    copies, keep = Copies(send, recv), Stays(local)
    work = Scatter(
        (qkv, 0, 1024), (qkv, 1024, 1024), [(qkv, 2048, 1408), (small, 0, 128)],
        (o_up, o_mix, o_att), scratch, copies, keep,
    )
    seq, peers, along_y = work.seq, work.peers, work.along_y
    greet(unique(work.x, work.y, work.z, work.c, []))
    for d in (1, 2, 3):
        copies.push(("d1", d), down.at[step(work.y, d)], d1.at[d], along_y[d - 1])
    work.first()
    for e in range(1, 8):
        copies.push(("t1", e), mod, t1.at[e], peers[e - 1])
        copies.push(("cap", e), cap, o_cap.at[seq], peers[e - 1])
    keep(down.at[work.y], d1.at[0])
    keep(mod, t1.at[0])
    keep(cap, o_cap.at[seq])
    keep.wait()
    beside = device(work.xh * 2 + 1 - work.xl, work.y, work.z, work.c)
    for d in (1, 2, 3):
        copies.arrived(("d1", d), d1.at[d], along_y[3 - d])
    add_up([d1.at[pl.ds(i, 1)] for i in range(4)], d1s)
    copies.push(("d2",), d1s, d2, beside)
    work.second()
    copies.arrived(("d2",), d2, beside)
    add_up([d1s, d2], d2s)
    keep(d2s.at[0], o_down.at[work.y])
    for d in (1, 2, 3):
        copies.push(("d3", d), d2s.at[0], o_down.at[work.y], along_y[d - 1])
    work.third()
    total = t1[0].astype(jnp.float32)
    for e in range(1, 8):
        copies.arrived(("t1", e), t1.at[e], peers[7 - e])
        total = total + t1[e].astype(jnp.float32)
    o_mod[...] = total
    work.fourth()
    work.last()
    for d in (1, 2, 3):
        copies.arrived(("d3", d), o_down.at[step(work.y, -d)], along_y[3 - d])
    for e in range(1, 8):
        copies.arrived(("cap", e), o_cap.at[(seq + 8 - e) % 8], peers[7 - e])
    keep.wait()
    copies.finish()


def scatter_rest(qkv, small, down, mod, cap):
    width = down.shape[-1]
    bf16 = lambda *shape: jax.ShapeDtypeStruct(shape, jnp.bfloat16)
    vmem = lambda *shape: pltpu.VMEM(shape, jnp.bfloat16)
    return pl.pallas_call(
        rest_kernel,
        out_shape=(
            bf16(HD, 1024), bf16(HD, 1024), bf16(HD, 1536), bf16(4, HD, width),
            jax.ShapeDtypeStruct(mod.shape, jnp.float32), bf16(8, *cap.shape),
        ),
        in_specs=[ANYWHERE] * 5,
        out_specs=(ANYWHERE,) * 4 + (ON_CHIP, ANYWHERE),
        scratch_shapes=[
            vmem(4, HD, width), vmem(1, HD, width), vmem(1, HD, width), vmem(1, HD, width),
            vmem(8, *mod.shape),
        ]
        + Scatter.buffers(1024, 1024, 1536)
        + semaphores(18, 80, 80),
        compiler_params=parameters(3),
    )(qkv, small, down, mod, cap)


def sibling_pairs():
    return [(i, i + 1 - 2 * (i % 2)) for i in range(16)]


def by_core(matrix):
    core = lax.axis_index("fsdp") % 2
    split = matrix.reshape((8, 2, -1) + matrix.shape[1:])
    pick = lambda which: lax.dynamic_index_in_dim(split, which, 1, keepdims=False).reshape(
        (-1,) + matrix.shape[1:]
    )
    return pick(core), pick(1 - core)


def pair_grad(former, latter):
    own, other = by_core(former.T)
    theirs = project(other, latter).astype(jnp.bfloat16)
    received = lax.ppermute(theirs, "fsdp", sibling_pairs())
    return (project(own, latter) + received.astype(jnp.float32)).astype(jnp.bfloat16)


def on_device(
    latents,
    timestep,
    caption,
    shift_table,
    qkv_weight,
    query_bias,
    value_bias,
    proj_weight,
    proj_bias,
    cross_query,
    cross_qbias,
    cross_kv,
    cross_vbias,
    cross_proj,
    cross_pbias,
    up_weight,
    up_bias,
    down_weight,
    down_bias,
    cotangent,
):
    group = lax.axis_index("fsdp")
    small = jnp.zeros((32 * HD * 16,), jnp.bfloat16)
    at = 0
    for vector in (
        shift_table, query_bias, value_bias, proj_bias, cross_qbias, cross_vbias, cross_pbias,
        down_bias, up_bias,
    ):
        small = lax.dynamic_update_slice(small, vector, (at + group * vector.shape[0],))
        at += 16 * vector.shape[0]
    full_qkv, each_small = gather_early(qkv_weight, small.reshape(32, -1))
    full_small = jnp.sum(each_small.reshape(16, 32, -1).astype(jnp.float32), axis=0)
    full_table = full_small[:6]
    full_qbias, full_vbias, full_pbias, full_cqbias, full_cvbias, full_cpbias, full_dbias = (
        full_small[6 + i] for i in range(7)
    )
    full_ubias = full_small[13:17].reshape(-1)
    latent_count, local_len, model_width = latents.shape
    inputs = latents.astype(jnp.float32)
    modulation = (full_table + timestep.astype(jnp.float32).reshape(6, model_width)).reshape(
        latent_count, 6, 1, model_width
    )
    shift_one, scale_one, gate_one = (modulation[:, 0], modulation[:, 1], modulation[:, 2])
    shift_two, scale_two, gate_two = (modulation[:, 3], modulation[:, 4], modulation[:, 5])
    pre_one, pull_one = jax.vjp(modulate, inputs, shift_one, scale_one)
    normed_one = pre_one.astype(jnp.bfloat16)
    qkv_bias = jnp.concatenate([full_qbias, jnp.zeros_like(full_qbias), full_vbias]).astype(
        jnp.float32
    )
    packed = (project(normed_one, full_qkv) + qkv_bias).astype(jnp.bfloat16)
    full_up, full_cquery, full_ckv, full_pair, full_down, heads, rows = gather_late(
        (
            up_weight,
            cross_query,
            cross_kv,
            jnp.concatenate([proj_weight, cross_proj], axis=1),
            down_weight,
        ),
        packed[0],
    )
    full_proj, full_cproj = jnp.split(full_pair, 2, axis=1)
    tok_major = rows[None]
    branch_one = project(tok_major, full_proj) + full_pbias.astype(jnp.float32)
    after_one = inputs + gate_one * branch_one
    middle = after_one.astype(jnp.bfloat16)
    cross_rows = (project(middle, full_cquery) + full_cqbias.astype(jnp.float32)).astype(
        jnp.bfloat16
    )
    kv_bias = jnp.concatenate([jnp.zeros_like(full_cvbias), full_cvbias]).astype(jnp.float32)
    text_kv = (project(caption, full_ckv) + kv_bias).astype(jnp.bfloat16)
    text_keys = by_heads(text_kv[..., :model_width])
    text_values = by_heads(text_kv[..., model_width:])
    cross_heads, cross_logsum = jax.vmap(attend_forward)(
        by_heads(cross_rows), text_keys, text_values
    )
    crossed = cross_heads.reshape(latent_count, local_len, model_width)
    branch_two = project(crossed, full_cproj) + full_cpbias.astype(jnp.float32)
    after_two = after_one + branch_two
    pre_two, pull_two = jax.vjp(modulate, after_two, shift_two, scale_two)
    normed_two = pre_two.astype(jnp.bfloat16)
    hidden = project(normed_two, full_up) + full_ubias.astype(jnp.float32)
    activated, gelu_pull = jax.vjp(jax.nn.gelu, hidden)
    act_rows = activated.astype(jnp.bfloat16)
    branch_three = project(act_rows, full_down) + full_dbias.astype(jnp.float32)
    block_out = (after_two + gate_two * branch_three).astype(jnp.bfloat16)
    grad_out = cotangent.astype(jnp.float32)
    grad_gate_two = jnp.sum(grad_out * branch_three, axis=1, keepdims=True)
    grad_three = (gate_two * grad_out).astype(jnp.bfloat16)
    down_grad = weight_grad(act_rows, grad_three)
    down_bgrad = token_sum(grad_three)
    grad_act = project(grad_three, full_down.T)
    grad_hidden = gelu_pull(grad_act)[0].astype(jnp.bfloat16)
    up_grad = pair_grad(normed_two[0], grad_hidden[0])
    up_bgrad = token_sum(grad_hidden)
    grad_pre_two = project(grad_hidden, full_up.T)
    grad_mid_two, grad_shift_two, grad_scale_two = pull_two(grad_pre_two)
    grad_after_two = grad_out + grad_mid_two
    down_part = lax.psum_scatter(
        down_grad.astype(jnp.bfloat16), "fsdp", scatter_dimension=0, tiled=True
    )
    grad_branch_two = grad_after_two.astype(jnp.bfloat16)
    cproj_grad = pair_grad(crossed[0], grad_branch_two[0])
    cproj_bgrad = token_sum(grad_branch_two)
    grad_crossed = project(grad_branch_two, full_cproj.T).astype(jnp.bfloat16)
    grad_cq, grad_ck, grad_cv = jax.vmap(attend_backward)(
        by_heads(cross_rows), text_keys, text_values, cross_logsum, by_heads(grad_crossed)
    )
    grad_cross_rows = grad_cq.reshape(latent_count, local_len, model_width).astype(jnp.bfloat16)
    cquery_grad = pair_grad(middle[0], grad_cross_rows[0])
    cquery_bgrad = token_sum(grad_cross_rows)
    grad_after_one = grad_after_two + project(grad_cross_rows, full_cquery.T)
    text_partial = jnp.concatenate(
        [
            grad_ck.reshape(grad_ck.shape[:2] + (model_width,)),
            grad_cv.reshape(grad_cv.shape[:2] + (model_width,)),
        ],
        axis=-1,
    )
    text_piece = text_partial.shape[1] // 8
    text_pieces = lax.all_to_all(
        text_partial[0].astype(jnp.bfloat16).reshape(8, text_piece, -1), "seq", 0, 0
    )
    text_grad = jnp.sum(text_pieces.astype(jnp.float32), axis=0).astype(jnp.bfloat16)
    caption_part = lax.dynamic_slice_in_dim(
        caption[0], lax.axis_index("seq") * text_piece, text_piece, 0
    )
    ckv_grad = pair_grad(caption_part, text_grad)
    cvalue_bgrad = jnp.sum(text_grad[:, model_width:].astype(jnp.float32), axis=0)
    caption_piece = project(text_grad, full_ckv.T)
    grad_gate_one = jnp.sum(grad_after_one * branch_one, axis=1, keepdims=True)
    grad_branch_one = (gate_one * grad_after_one).astype(jnp.bfloat16)
    proj_grad = pair_grad(tok_major[0], grad_branch_one[0])
    proj_bgrad = token_sum(grad_branch_one)
    grad_tok = project(grad_branch_one, full_proj.T).astype(jnp.bfloat16)
    blocks = lambda grad: grad.reshape(4, 2, HD, -1)
    mix = jnp.concatenate(
        [proj_grad, cproj_grad, cquery_grad, ckv_grad, jnp.zeros((8 * HD, 384), jnp.bfloat16)],
        axis=1,
    )
    sum_up, sum_mix, sum_att, flat = scatter_back(
        blocks(up_grad), blocks(mix), heads, grad_tok[0]
    )
    sum_mix = jnp.concatenate([sum_mix, sum_att], axis=1)
    grad_flat = flat[None]
    qkv_grad = pair_grad(normed_one[0], grad_flat[0])
    qbias_grad = token_sum(grad_flat[..., :model_width])
    vbias_grad = token_sum(grad_flat[..., 2 * model_width :])
    grad_pre_one = project(grad_flat, full_qkv.T)
    grad_norm_one, grad_shift_one, grad_scale_one = pull_one(grad_pre_one)
    grad_latents = grad_after_one + grad_norm_one
    grad_mod = jnp.concatenate(
        [
            grad_shift_one,
            grad_scale_one,
            grad_gate_one,
            grad_shift_two,
            grad_scale_two,
            grad_gate_two,
        ],
        axis=1,
    )
    grad_mod = grad_mod.reshape(latent_count, 6 * model_width)
    small_grad = jnp.concatenate(
        [
            grad_mod.reshape(-1, 6),
            qbias_grad.reshape(-1, 1),
            vbias_grad.reshape(-1, 1),
            proj_bgrad.reshape(-1, 1),
            cquery_bgrad.reshape(-1, 1),
            cvalue_bgrad.reshape(-1, 1),
            cproj_bgrad.reshape(-1, 1),
            down_bgrad.reshape(-1, 1),
            up_bgrad.reshape(-1, 4),
        ],
        axis=1,
    )
    small_own, small_other = by_core(small_grad)
    small_sum = small_own + lax.ppermute(
        small_other.astype(jnp.bfloat16), "fsdp", sibling_pairs()
    ).astype(jnp.float32)
    sum_q, sum_k, sum_v, sum_down, sum_mod, caption_all = scatter_rest(
        blocks(qkv_grad),
        jnp.pad(blocks(small_sum.astype(jnp.bfloat16)), ((0, 0), (0, 0), (0, 0), (0, 111))),
        down_part.reshape(4, HD, model_width),
        jnp.pad(grad_mod.astype(jnp.bfloat16).reshape(-1, 128), ((0, 10), (0, 0))),
        jnp.pad(caption_piece.astype(jnp.bfloat16), ((0, 1), (0, 0))),
    )
    wide = lambda part: part.astype(jnp.float32)
    sum_small = wide(sum_v[:, 1408 : 1408 + 17])
    return (
        block_out,
        grad_latents,
        sum_mod[:54].reshape(1, -1),
        wide(caption_all[:, :text_piece].reshape(1, -1, model_width)),
        sum_small[:, :6].reshape(-1),
        jnp.concatenate([wide(sum_q), wide(sum_k), wide(sum_v[:, :1408])], axis=1),
        sum_small[:, 6],
        sum_small[:, 7],
        wide(sum_mix[:, :model_width]),
        sum_small[:, 8],
        wide(sum_mix[:, 2 * model_width : 3 * model_width]),
        sum_small[:, 9],
        wide(sum_mix[:, 3 * model_width : 5 * model_width]),
        sum_small[:, 10],
        wide(sum_mix[:, model_width : 2 * model_width]),
        sum_small[:, 11],
        wide(sum_up),
        sum_small[:, 13:17].reshape(-1),
        wide(sum_down.reshape(4 * HD, model_width)),
        sum_small[:, 12],
    )


def solution(mesh):
    placed = (
        P("fsdp", "seq", None),
        P("fsdp", None),
        P("fsdp", None, None),
        P("fsdp"),
        P("fsdp", None),
        P("fsdp"),
        P("fsdp"),
        P("fsdp", None),
        P("fsdp"),
        P("fsdp", None),
        P("fsdp"),
        P("fsdp", None),
        P("fsdp"),
        P("fsdp", None),
        P("fsdp"),
        P("fsdp", None),
        P("fsdp"),
        P("fsdp", None),
        P("fsdp"),
        P("fsdp", "seq", None),
    )
    return jax.shard_map(
        on_device,
        mesh=mesh,
        in_specs=placed,
        out_specs=(
            P("fsdp", "seq", None),
            P("fsdp", "seq", None),
            P("fsdp", None),
            P("fsdp", None, None),
            P("fsdp"),
            P("fsdp", None),
            P("fsdp"),
            P("fsdp"),
            P("fsdp", None),
            P("fsdp"),
            P("fsdp", None),
            P("fsdp"),
            P("fsdp", None),
            P("fsdp"),
            P("fsdp", None),
            P("fsdp"),
            P("fsdp", None),
            P("fsdp"),
            P("fsdp", None),
            P("fsdp"),
        ),
        check_vma=False,
    )
```

```python
import functools

import jax
import jax.numpy as jnp
from jax import lax
from jax.experimental import pallas as pl
from jax.experimental.pallas import tpu as pltpu
from jax.sharding import PartitionSpec as P

HD = 72
MESH = pl.DeviceIdType.MESH


epsilon = 1e-06


def for_sending(array):

    def short(part):
        return part.astype(jnp.bfloat16) if part.dtype == jnp.float32 else part

    return jax.tree.map(short, array)


def normalize(values):
    centre = values - jnp.mean(values, axis=-1, keepdims=True)
    spread = jnp.mean(centre * centre, axis=-1, keepdims=True)
    return centre * lax.rsqrt(spread + epsilon)


def modulate(values, shift, scale):
    return normalize(values) * (1.0 + scale) + shift


def project(former, latter):
    return jnp.dot(former, latter, preferred_element_type=jnp.float32)


def token_sum(values):
    return jnp.sum(values.astype(jnp.float32), axis=(0, 1))


def by_heads(matrix):
    return matrix.reshape(matrix.shape[:-1] + (matrix.shape[-1] // HD, HD))


def attend_forward(queries, key_rows, values):
    factor = HD ** (-0.5)
    scores = (
        jnp.einsum("qhd,khd->hqk", queries, key_rows, preferred_element_type=jnp.float32) * factor
    )
    largest = jnp.max(scores, axis=-1, keepdims=True)
    exponent = jnp.exp(scores - largest)
    partition = jnp.sum(exponent, axis=-1, keepdims=True)
    weights = (exponent / partition).astype(jnp.bfloat16)
    output = jnp.einsum("hqk,khd->qhd", weights, values, preferred_element_type=jnp.float32)
    return (output.astype(jnp.bfloat16), largest + jnp.log(partition))


def place():
    seq, fsdp = lax.axis_index("seq"), lax.axis_index("fsdp")
    y, x_lo = seq // 2, seq % 2
    z, rest = fsdp // 4, fsdp % 4
    x_hi, core = rest // 2, rest % 2
    return x_hi * 2 + x_lo, y, z, core


def device(x, y, z, core):
    return (y * 2 + x % 2, z * 4 + (x // 2) * 2 + core)


def step(value, by):
    return (value + by + 4) % 4


class Copies:
    def __init__(self, send, recv):
        self.send, self.recv, self.index, self.started = send, recv, {}, []

    def number(self, key):
        return self.index.setdefault(key, len(self.index))

    def push(self, key, src, dst, target):
        at = self.number(key)
        copy = pltpu.make_async_remote_copy(
            src_ref=src,
            dst_ref=dst,
            send_sem=self.send.at[at],
            recv_sem=self.recv.at[at],
            device_id=target,
            device_id_type=MESH,
        )
        copy.start()
        self.started.append(copy)

    def arrived(self, key, dst, source):
        at = self.number(key)
        pltpu.make_async_remote_copy(
            src_ref=dst,
            dst_ref=dst,
            send_sem=self.send.at[at],
            recv_sem=self.recv.at[at],
            device_id=source,
            device_id_type=MESH,
        ).wait_recv()

    def finish(self):
        for copy in self.started:
            copy.wait_send()


def greet(others):
    barrier = pltpu.get_barrier_semaphore()
    for other in others:
        pl.semaphore_signal(barrier, inc=1, device_id=other, device_id_type=MESH)
    pl.semaphore_wait(barrier, len(others))


class Piece:
    def __init__(self, source, out, axis, dim, start, size):
        self.source, self.out, self.axis = source, out, axis
        self.dim, self.start, self.size = dim, start, size

    def cut(self, part):
        parts = {"x": 2, "y": 4, "z": 1}[self.axis]
        size = self.size // parts
        unit = 128 if self.dim == 1 else 16
        start = self.start if parts == 1 else pl.multiple_of(self.start + part * size, unit)
        window = pl.ds(start, size)
        return (slice(None), window) if self.dim == 1 else (window, slice(None))


class Gather:
    def __init__(self, pieces, copies, local):
        self.pieces, self.copies, self.local = pieces, copies, local
        self.x, self.y, self.z, self.c = x, y, z, c = place()
        self.xh, self.xl = x // 2, x % 2
        self.sibling = device(x, y, z, 1 - c)
        self.far = device(step(x, 2), y, z, c)
        self.lines = {
            "x": [device(step(x, d), y, z, c) for d in (1, 2, 3)],
            "y": [device(x, step(y, d), z, c) for d in (1, 2, 3)],
            "z": [device(x, y, step(z, d), c) for d in (1, 2, 3)],
        }
        self.part = {"x": self.xl, "y": y, "z": 0}

    def others(self):
        return [self.sibling] + self.lines["x"] + self.lines["y"] + self.lines["z"]

    def block(self, p, dz, flip, part, core=None):
        core = self.c if core is None else core
        return p.out.at[(step(self.z, -dz), (self.xh + flip) % 2, core) + p.cut(part)]

    def both(self, key, src, dst, axis):
        self.copies.push(key + (1,), src, dst, self.lines[axis][0])
        self.copies.push(key + (3,), src, dst, self.lines[axis][2])

    def first(self):
        self.stays = []
        for n, p in enumerate(self.pieces):
            mine = p.source.at[p.cut(self.part[p.axis])]
            there = self.block(p, 0, 0, self.part[p.axis])
            copy = pltpu.make_async_copy(mine, there, self.local.at[n])
            copy.start()
            self.stays.append(copy)
            if p.axis != "x":
                self.copies.push((n, "far"), mine, there, self.far)
            if p.axis != "z":
                for d in (1, 2, 3):
                    self.copies.push((n, "mid", 0, d), mine, there, self.lines["z"][d - 1])
        for n, p in enumerate(self.pieces):
            mine = p.source.at[p.cut(self.part[p.axis])]
            self.both((n, "end", 0, 0), mine, self.block(p, 0, 0, self.part[p.axis]), p.axis)

    def second(self):
        for n, p in enumerate(self.pieces):
            if p.axis == "x":
                continue
            block = self.block(p, 0, 1, self.part[p.axis])
            self.copies.arrived((n, "far"), block, self.far)
            if p.axis == "y":
                for d in (1, 2, 3):
                    self.copies.push((n, "mid", 1, d), block, block, self.lines["z"][d - 1])
            self.both((n, "end", 0, 1), block, block, p.axis)

    def third(self):
        for dz in (1, 3, 2):
            for n, p in enumerate(self.pieces):
                if p.axis == "z":
                    continue
                for flip in (0, 1) if p.axis == "y" else (0,):
                    block = self.block(p, dz, flip, self.part[p.axis])
                    self.copies.arrived((n, "mid", flip, dz), block, self.lines["z"][3 - dz])
                    self.both((n, "end", dz, flip), block, block, p.axis)

    def blocks(self, p):
        if p.axis == "z":
            return ((0, 0), (0, 1))
        return tuple((dz, f) for dz in (0, 1, 3, 2) for f in ((0, 1) if p.axis == "y" else (0,)))

    def ended(self, n, p, dz, flip, d):
        if p.axis == "z":
            block = self.block(p, d, flip, 0)
        elif p.axis == "y":
            block = self.block(p, dz, flip, step(self.y, -d))
        else:
            from_x = step(self.x, -d)
            block = p.out.at[(step(self.z, -dz), from_x // 2, self.c) + p.cut(from_x % 2)]
        self.copies.arrived((n, "end", dz, flip, d), block, self.lines[p.axis][3 - d])
        return block

    def group(self, p, d, core):
        if p.axis == "z":
            return p.out.at[(step(self.z, -d), slice(None), core) + p.cut(0)]
        if p.axis == "y":
            return p.out.at[(slice(None), slice(None), core) + p.cut(step(self.y, -d))]
        from_x = step(self.x, -d)
        return p.out.at[(slice(None), from_x // 2, core) + p.cut(from_x % 2)]

    def share(self, n, p, d):
        block = self.group(p, d, self.c)
        self.copies.push((n, "core", d), block, block, self.sibling)

    def fourth(self):
        for copy in self.stays:
            copy.wait()
        for n, p in enumerate(self.pieces):
            self.share(n, p, 0)
        for at in range(8):
            for n, p in enumerate(self.pieces):
                if at >= len(self.blocks(p)):
                    continue
                dz, flip = self.blocks(p)[at]
                line = self.lines[p.axis]
                for d in (1, 3):
                    block = self.ended(n, p, dz, flip, d)
                    if (at % 2 == 0) == (d == 1):
                        on = line[0] if d == 1 else line[2]
                        self.copies.push((n, "end", dz, flip, 2), block, block, on)
                if at == len(self.blocks(p)) - 1:
                    self.share(n, p, 1)
                    self.share(n, p, 3)

    def last(self):
        for n, p in enumerate(self.pieces):
            for dz, flip in self.blocks(p):
                self.ended(n, p, dz, flip, 2)
            self.share(n, p, 2)
        for d in (0, 1, 3, 2):
            for n, p in enumerate(self.pieces):
                block = self.group(p, d, 1 - self.c)
                self.copies.arrived((n, "core", d), block, self.sibling)


def early_kernel(qkv, small, o_qkv, o_small, local, send, recv):
    pieces = [
        Piece(small, o_small, "z", 0, 0, small.shape[0]),
        Piece(qkv, o_qkv, "z", 1, 18 * 128, 9 * 128),
        Piece(qkv, o_qkv, "x", 1, 8 * 128, 10 * 128),
        Piece(qkv, o_qkv, "y", 1, 0, 8 * 128),
    ]
    copies = Copies(send, recv)
    work = Gather(pieces, copies, local)
    greet(work.others())
    work.first()
    work.second()
    work.third()
    work.fourth()
    work.last()
    copies.finish()


PAIR = 2 * HD


def head_slices(rows):
    for j in range(rows.shape[1] // (8 * PAIR)):
        for to in range(8):
            yield to, pl.ds(j * PAIR, PAIR), pl.ds((j * 8 + to) * PAIR, PAIR)


def exchange(copies, name, seq, peers, sent, got, local):
    for e in range(1, 8):
        copies.push((name, e), sent.at[(seq + e) % 8], got.at[seq], peers[e - 1])
    copy = pltpu.make_async_copy(sent.at[seq], got.at[seq], local)
    copy.start()
    return copy


def exchanged(copies, name, seq, peers, got, copy):
    copy.wait()
    for e in range(1, 8):
        copies.arrived((name, e), got.at[(seq + 8 - e) % 8], peers[7 - e])


def seq_peers():
    x, y, z, c = place()
    seq = y * 2 + x % 2
    return seq, [((seq + e) % 8, z * 4 + (x // 2) * 2 + c) for e in range(1, 8)]


def unique(x, y, z, c, extra):
    _, peers = seq_peers()
    far = [device((1 - x // 2) * 2 + e, y, z, c) for e in (0, 1)]
    return peers + far + [device(x, y, step(z, d), c) for d in (1, 2, 3)] + extra


CHUNK = 256


def head(which, h):
    return pl.ds(which * PAIR + h * HD, HD)


def attend(heads, h, out):
    tokens = 8 * 128
    keys = heads[:, :, head(1, h)].reshape(tokens, HD)
    values = heads[:, :, head(2, h)].reshape(tokens, HD)

    @pl.loop(0, tokens // CHUNK)
    def _(i):
        queries = heads[pl.ds(i * 2, 2), :, head(0, h)].reshape(CHUNK, HD)
        scores = lax.dot_general(
            queries, keys, (((1,), (1,)), ((), ())), preferred_element_type=jnp.float32
        ) * (HD**-0.5)
        exponent = jnp.exp(scores - jnp.max(scores, axis=1, keepdims=True))
        weights = exponent * (1.0 / jnp.sum(exponent, axis=1, keepdims=True))
        got = jnp.dot(weights.astype(jnp.bfloat16), values, preferred_element_type=jnp.float32)
        out[pl.ds(i * 2, 2), :, head(0, h)] = got.astype(jnp.bfloat16).reshape(2, 128, HD)


def head_back(queries, keys, values, grad, mask):
    across = (((1,), (1,)), ((), ()))
    scores = lax.dot_general(keys, queries, across, preferred_element_type=jnp.float32)
    scores = scores * (HD**-0.5) if mask is None else scores * (HD**-0.5) + mask
    exponent = jnp.exp(scores - jnp.max(scores, axis=0, keepdims=True))
    weights = exponent * (1.0 / jnp.sum(exponent, axis=0, keepdims=True))
    grad_weights = lax.dot_general(values, grad, across, preferred_element_type=jnp.float32)
    inner = jnp.sum(weights * grad_weights, axis=0, keepdims=True)
    grad_scores = (weights * (grad_weights - inner)).astype(jnp.bfloat16)
    grad_q = lax.dot_general(
        grad_scores, keys, (((0,), (0,)), ((), ())), preferred_element_type=jnp.float32
    ) * (HD**-0.5)
    return weights.astype(jnp.bfloat16), grad_scores, grad_q.astype(jnp.bfloat16)


def attend_back(heads, grads, h, out, key_sum, value_sum):
    tokens = 8 * 128
    keys = heads[:, :, head(1, h)].reshape(tokens, HD)
    values = heads[:, :, head(2, h)].reshape(tokens, HD)
    key_sum[...] = jnp.zeros_like(key_sum)
    value_sum[...] = jnp.zeros_like(value_sum)

    @pl.loop(0, tokens // CHUNK)
    def _(i):
        queries = heads[pl.ds(i * 2, 2), :, head(0, h)].reshape(CHUNK, HD)
        grad = grads[pl.ds(i * 2, 2), :, head(0, h)].reshape(CHUNK, HD)
        weights, grad_scores, grad_q = head_back(queries, keys, values, grad, None)
        value_sum[...] += project(weights, grad)
        key_sum[...] += project(grad_scores, queries)
        out[pl.ds(i * 2, 2), :, head(0, h)] = grad_q.reshape(2, 128, HD)

    out[:, :, head(1, h)] = (key_sum[...] * (HD**-0.5)).astype(jnp.bfloat16).reshape(8, 128, HD)
    out[:, :, head(2, h)] = value_sum[...].astype(jnp.bfloat16).reshape(8, 128, HD)


def cross_kernel(queries, text, grad_out, weight, grad_queries, grad_text, *, real):
    grad = lax.dot_general(
        grad_out[...], weight[...], (((1,), (1,)), ((), ())), preferred_element_type=jnp.float32
    ).astype(jnp.bfloat16)
    rows = lax.broadcasted_iota(jnp.int32, (text.shape[0], queries.shape[0]), 0)
    mask = jnp.where(rows < real, 0.0, -1e30)
    width = queries.shape[1]
    for h in range(width // HD):
        mine, values = pl.ds(h * HD, HD), pl.ds(width + h * HD, HD)
        slopes = grad[:, h * HD : (h + 1) * HD]
        weights, grad_scores, grad_q = head_back(
            queries[:, mine], text[:, mine], text[:, values], slopes, mask
        )
        grad_queries[:, mine] = grad_q
        grad_key = project(grad_scores, queries[:, mine]) * (HD**-0.5)
        grad_text[:, mine] = grad_key.astype(jnp.bfloat16)
        grad_text[:, values] = project(weights, slopes).astype(jnp.bfloat16)


def cross_back(queries, text, grad_out, weight):
    real = text.shape[0]
    text = jnp.pad(text, ((0, -real % 128), (0, 0)))
    bf16 = lambda like: jax.ShapeDtypeStruct(like.shape, jnp.bfloat16)
    return pl.pallas_call(
        functools.partial(cross_kernel, real=real),
        out_shape=(bf16(queries), bf16(text)),
        in_specs=[ON_CHIP] * 4,
        out_specs=(ON_CHIP,) * 2,
        compiler_params=pltpu.CompilerParams(vmem_limit_bytes=48 * 1024 * 1024),
    )(queries, text, grad_out, weight)


def late_kernel(
    up, cq, ckv, pair, down, packed,
    o_up, o_cq, o_ckv, o_pair, o_down, o_heads, o_rows,
    sent, heads, mixed, joined, local, send, recv,
):
    height = down.shape[0]
    pieces = [
        Piece(cq, o_cq, "z", 1, 0, cq.shape[1]),
        Piece(ckv, o_ckv, "z", 1, 0, ckv.shape[1]),
        Piece(pair, o_pair, "x", 1, 0, pair.shape[1]),
        Piece(up, o_up, "y", 1, 0, up.shape[1]),
        Piece(down, o_down, "x", 0, 128, height - 128),
        Piece(down, o_down, "y", 0, 0, 128),
    ]
    copies = Copies(send, recv)
    work = Gather(pieces, copies, local)
    seq, peers = seq_peers()
    greet(unique(work.x, work.y, work.z, work.c, [work.sibling]))
    for to, what, at in head_slices(packed):
        sent[to, :, what] = packed[:, at]
    own = exchange(copies, "in", seq, peers, sent, heads, local.at[6])
    work.first()
    exchanged(copies, "in", seq, peers, heads, own)
    keep = pltpu.make_async_copy(heads, o_heads, local.at[7])
    keep.start()
    attend(heads, 0, mixed)
    work.second()
    attend(heads, 1, mixed)
    own = exchange(copies, "out", seq, peers, mixed, joined, local.at[8])
    work.third()
    work.fourth()
    exchanged(copies, "out", seq, peers, joined, own)
    for at, what, to in head_slices(o_rows):
        o_rows[:, to] = joined[at, :, what]
    work.last()
    keep.wait()
    copies.finish()


def whole(out):
    return out.reshape((-1,) + out.shape[4:])


def full_shapes(shards):
    return tuple(jax.ShapeDtypeStruct((4, 2, 2) + s.shape, s.dtype) for s in shards)


def semaphores(*counts):
    return [pltpu.SemaphoreType.DMA((n,)) for n in counts]


ANYWHERE = pl.BlockSpec(memory_space=pl.ANY)
ON_CHIP = pl.BlockSpec(memory_space=pltpu.VMEM)


def parameters(collective):
    return pltpu.CompilerParams(
        collective_id=collective, has_side_effects=True, vmem_limit_bytes=48 * 1024 * 1024
    )


def gather_early(*shards):
    outs = pl.pallas_call(
        early_kernel,
        out_shape=full_shapes(shards),
        in_specs=[ANYWHERE] * 2,
        out_specs=(ANYWHERE,) * 2,
        scratch_shapes=semaphores(4, 128, 128),
        compiler_params=parameters(0),
    )(*shards)
    return tuple(whole(out) for out in outs)


def gather_late(shards, packed):
    bf16 = lambda *shape: jax.ShapeDtypeStruct(shape, jnp.bfloat16)
    vmem = lambda *shape: pltpu.VMEM(shape, jnp.bfloat16)
    outs = pl.pallas_call(
        late_kernel,
        out_shape=full_shapes(shards) + (bf16(8, 128, 3 * PAIR), bf16(128, 8 * PAIR)),
        in_specs=[ANYWHERE] * 5 + [ON_CHIP],
        out_specs=(ANYWHERE,) * 6 + (ON_CHIP,),
        scratch_shapes=[
            vmem(8, 128, 3 * PAIR), vmem(8, 128, 3 * PAIR), vmem(8, 128, PAIR), vmem(8, 128, PAIR),
        ]
        + semaphores(9, 256, 256),
        compiler_params=parameters(1),
    )(*shards, packed)
    return tuple(whole(out) for out in outs[:5]) + outs[5:]


def add_up(parts, out):
    blocks, _, columns = out.shape
    tile = next(t for t in (384, 512, 256, 128) if columns % t == 0)

    @pl.loop(0, blocks * (columns // tile))
    def _(i):
        block = i // (columns // tile)
        cols = pl.ds(pl.multiple_of((i % (columns // tile)) * tile, 128), tile)
        total = parts[0][block, :, cols].astype(jnp.float32)
        for part in parts[1:]:
            total = total + part[block, :, cols].astype(jnp.float32)
        out[block, :, cols] = total.astype(out.dtype)


def columns(part, width, start=0):
    return pl.ds(pl.multiple_of(start + part * width, 128), width)


class Scatter:
    def __init__(self, by_y, by_x, by_z, outs, scratch, copies, keep):
        self.by_y, self.by_x, self.by_z = by_y, by_x, by_z
        self.o_up, self.o_mix, self.o_att = outs
        self.scratch, self.copies, self.keep = scratch, copies, keep
        self.x, self.y, self.z, self.c = x, y, z, c = place()
        self.xh, self.xl = x // 2, x % 2
        self.seq, self.peers = seq_peers()
        self.along_x = [device(step(x, d), y, z, c) for d in (1, 2, 3)]
        self.along_y = [device(x, step(y, d), z, c) for d in (1, 2, 3)]
        self.along_z = [device(x, y, step(z, d), c) for d in (1, 2, 3)]

    @staticmethod
    def buffers(by_y, by_x, by_z):
        vmem = lambda *shape: pltpu.VMEM(shape, jnp.bfloat16)
        wy, wx, wz = by_y // 4, by_x // 2, by_z
        return [
            vmem(4, 4, 2, HD, wy), vmem(4, 2, HD, wy), vmem(4, 2, HD, wy),
            vmem(2, HD, wy), vmem(4, HD, wy), vmem(1, HD, wy),
            vmem(4, 2, HD, wz), vmem(2, HD, wz), vmem(4, 1, HD, wz // 2),
            vmem(1, HD, wz // 2), vmem(4, 1, HD, wz // 8), vmem(1, HD, wz // 8),
            vmem(4, 4, HD, wx), vmem(4, HD, wx), vmem(4, 4, HD, wx // 4),
            vmem(4, HD, wx // 4), vmem(4, HD, wx // 4), vmem(1, HD, wx // 4),
        ]

    def first(self):
        u1, a1, m1 = self.scratch[0], self.scratch[6], self.scratch[12]
        up, up_at, up_size = self.by_y
        for d in (1, 2, 3):
            to_x, to_y, to_z = step(self.x, d), step(self.y, d), step(self.z, d)
            cols = columns(to_y, up_size // 4, up_at)
            self.copies.push(("u1", d), up.at[:, :, :, cols], u1.at[d], self.along_y[d - 1])
            at = 0
            for n, (source, start, size) in enumerate(self.by_x):
                self.copies.push(
                    ("m1", n, d),
                    source.at[:, to_x // 2, :, columns(to_x % 2, size // 2, start)],
                    m1.at[d, :, :, pl.ds(at, size // 2)],
                    self.along_x[d - 1],
                )
                at += size // 2
            at = 0
            for n, (source, start, size) in enumerate(self.by_z):
                self.copies.push(
                    ("a1", n, d),
                    source.at[to_z, :, :, pl.ds(start, size)],
                    a1.at[d, :, :, pl.ds(at, size)],
                    self.along_z[d - 1],
                )
                at += size
        self.keep(up.at[:, :, :, columns(self.y, up_size // 4, up_at)], u1.at[0])
        at = 0
        for source, start, size in self.by_x:
            self.keep(
                source.at[:, self.xh, :, columns(self.xl, size // 2, start)],
                m1.at[0, :, :, pl.ds(at, size // 2)],
            )
            at += size // 2
        at = 0
        for source, start, size in self.by_z:
            self.keep(
                source.at[self.z, :, :, pl.ds(start, size)], a1.at[0, :, :, pl.ds(at, size)]
            )
            at += size

    def second(self):
        u1, u1s, u2 = self.scratch[:3]
        a1, a1s, a2 = self.scratch[6:9]
        m1, m1s, m2 = self.scratch[12:15]
        for d in (1, 2, 3):
            at = 0
            for n, (_, _, size) in enumerate(self.by_z):
                got = a1.at[d, :, :, pl.ds(at, size)]
                self.copies.arrived(("a1", n, d), got, self.along_z[3 - d])
                at += size
        add_up([a1.at[i] for i in range(4)], a1s)
        for d in (1, 2, 3):
            to = step(self.x, d)
            part = a1s.at[pl.ds(to // 2, 1), :, columns(to % 2, a2.shape[-1])]
            self.copies.push(("a2", d), part, a2.at[d], self.along_x[d - 1])
        for d in (1, 2, 3):
            at = 0
            for n, (_, _, size) in enumerate(self.by_x):
                got = m1.at[d, :, :, pl.ds(at, size // 2)]
                self.copies.arrived(("m1", n, d), got, self.along_x[3 - d])
                at += size // 2
        add_up([m1.at[i] for i in range(4)], m1s)
        for d in (1, 2, 3):
            cols = columns(step(self.y, d), m2.shape[-1])
            self.copies.push(("m2", d), m1s.at[:, :, cols], m2.at[d], self.along_y[d - 1])
        for d in (1, 2, 3):
            self.copies.arrived(("u1", d), u1.at[d], self.along_y[3 - d])
        for zz in range(4):
            add_up([u1.at[i, zz] for i in range(4)], u1s.at[zz])
        for d in (1, 2, 3):
            self.copies.push(
                ("u2", d), u1s.at[step(self.z, d)], u2.at[d], self.along_z[d - 1]
            )

    def third(self):
        u1s, u2, u2s, u3 = self.scratch[1:5]
        a1s, a2, a2s, a3 = self.scratch[7:11]
        m1s, m2, m2s, m3 = self.scratch[13:17]
        for d in (1, 2, 3):
            self.copies.arrived(("a2", d), a2.at[d], self.along_x[3 - d])
        mine = a1s.at[pl.ds(self.xh, 1), :, columns(self.xl, a2.shape[-1])]
        add_up([mine] + [a2.at[d] for d in (1, 2, 3)], a2s)
        for d in (1, 2, 3):
            part = a2s.at[:, :, columns(step(self.y, d), a3.shape[-1])]
            self.copies.push(("a3", d), part, a3.at[d], self.along_y[d - 1])
        for d in (1, 2, 3):
            self.copies.arrived(("m2", d), m2.at[d], self.along_y[3 - d])
        add_up(
            [m1s.at[:, :, columns(self.y, m2.shape[-1])]] + [m2.at[d] for d in (1, 2, 3)], m2s
        )
        for d in (1, 2, 3):
            self.copies.push(("m3", d), m2s.at[step(self.z, d)], m3.at[d], self.along_z[d - 1])
        for d in (1, 2, 3):
            self.copies.arrived(("u2", d), u2.at[d], self.along_z[3 - d])
        add_up([u1s.at[self.z]] + [u2.at[d] for d in (1, 2, 3)], u2s)
        for d in (1, 2, 3):
            to = step(self.x, d) // 2
            self.copies.push(("u3", d), u2s.at[to], u3.at[d], self.along_x[d - 1])

    def fourth(self):
        u2s, u3, u3s = self.scratch[3:6]
        a2s, a3, a3s = self.scratch[9:12]
        m2s, m3, m3s = self.scratch[15:18]
        own = a2s.at[:, :, columns(self.y, a3.shape[-1])]
        for name, line, own, got, total, out in (
            ("a", self.along_y, own, [a3.at[d] for d in (1, 2, 3)], a3s, self.o_att),
            ("u", self.along_x, u2s.at[pl.ds(self.xh, 1)],
             [u3.at[pl.ds(d, 1)] for d in (1, 2, 3)], u3s, self.o_up),
            ("m", self.along_z, m2s.at[pl.ds(self.z, 1)],
             [m3.at[pl.ds(d, 1)] for d in (1, 2, 3)], m3s, self.o_mix),
        ):
            for d in (1, 2, 3):
                dst = a3.at[d] if name == "a" else (u3 if name == "u" else m3).at[d]
                self.copies.arrived((name + "3", d), dst, line[3 - d])
            add_up([own] + got, total)
            if name == "u":
                spot = out.at[:, columns(self.y, total.shape[-1])]
                for d in (1, 2, 3):
                    self.copies.push(("u4", d), total.at[0], spot, self.along_y[d - 1])
            else:
                spot = out.at[:, self.spot(self.seq, total)]
                for e in range(1, 8):
                    self.copies.push((name + "4", e), total.at[0], spot, self.peers[e - 1])
            self.keep(total.at[0], spot)

    def spot(self, seq, total):
        return columns((seq % 2) * 4 + seq // 2, total.shape[-1])

    def last(self):
        for d in (1, 2, 3):
            got = self.o_up.at[:, columns(step(self.y, -d), self.o_up.shape[-1] // 4)]
            self.copies.arrived(("u4", d), got, self.along_y[3 - d])
        for name, total, out in (
            ("a4", self.scratch[11], self.o_att), ("m4", self.scratch[17], self.o_mix),
        ):
            for e in range(1, 8):
                got = out.at[:, self.spot((self.seq + 8 - e) % 8, total)]
                self.copies.arrived((name, e), got, self.peers[7 - e])


class Stays:
    def __init__(self, local):
        self.local, self.copies, self.done = local, [], 0

    def __call__(self, src, dst):
        copy = pltpu.make_async_copy(src, dst, self.local.at[len(self.copies)])
        copy.start()
        self.copies.append(copy)

    def wait(self):
        for copy in self.copies[self.done :]:
            copy.wait()
        self.done = len(self.copies)


def back_kernel(
    up, mix, heads, grad_rows, o_up, o_mix, o_att, o_flat,
    sent, grads, mixed, joined, key_sum, value_sum, *rest,
):
    scratch, (local, send, recv) = rest[:18], rest[18:]
    copies, keep = Copies(send, recv), Stays(local)
    work = Scatter(
        (up, 0, 2560), [(up, 2560, 2048), (mix, 0, 1024)], [(mix, 1024, 5120)],
        (o_up, o_mix, o_att), scratch, copies, keep,
    )
    seq, peers = seq_peers()
    greet(unique(work.x, work.y, work.z, work.c, []))
    for to, what, at in head_slices(grad_rows):
        sent[to, :, what] = grad_rows[:, at]
    own = exchange(copies, "in", seq, peers, sent, grads, local.at[16])
    work.first()
    exchanged(copies, "in", seq, peers, grads, own)
    for h in (0, 1):
        attend_back(heads, grads, h, mixed, key_sum, value_sum)
    own = exchange(copies, "out", seq, peers, mixed, joined, local.at[17])
    keep.wait()
    work.second()
    work.third()
    exchanged(copies, "out", seq, peers, joined, own)
    for at, what, to in head_slices(o_flat):
        o_flat[:, to] = joined[at, :, what]
    work.fourth()
    work.last()
    keep.wait()
    copies.finish()


def scatter_back(up, mix, heads, grad_rows):
    bf16 = lambda *shape: jax.ShapeDtypeStruct(shape, jnp.bfloat16)
    vmem = lambda *shape: pltpu.VMEM(shape, jnp.bfloat16)
    return pl.pallas_call(
        back_kernel,
        out_shape=(
            bf16(HD, 2560), bf16(HD, 3072), bf16(HD, 5120), bf16(128, 24 * PAIR),
        ),
        in_specs=[ANYWHERE] * 2 + [ON_CHIP] * 2,
        out_specs=(ANYWHERE,) * 3 + (ON_CHIP,),
        scratch_shapes=[
            vmem(8, 128, PAIR), vmem(8, 128, PAIR), vmem(8, 128, 3 * PAIR), vmem(8, 128, 3 * PAIR),
            pltpu.VMEM((1024, HD), jnp.float32), pltpu.VMEM((1024, HD), jnp.float32),
        ]
        + Scatter.buffers(2560, 3072, 5120)
        + semaphores(18, 80, 80),
        compiler_params=parameters(2),
    )(up, mix, heads, grad_rows)


def rest_kernel(
    qkv, small, down, mod, cap, o_up, o_mix, o_att, o_down, o_mod, o_cap,
    d1, d1s, d2, d2s, t1, *rest,
):
    scratch, (local, send, recv) = rest[:18], rest[18:]
    copies, keep = Copies(send, recv), Stays(local)
    work = Scatter(
        (qkv, 0, 1536), [(qkv, 1536, 1024)], [(qkv, 2560, 896), (small, 0, 128)],
        (o_up, o_mix, o_att), scratch, copies, keep,
    )
    seq, peers, along_y = work.seq, work.peers, work.along_y
    greet(unique(work.x, work.y, work.z, work.c, []))
    for d in (1, 2, 3):
        copies.push(("d1", d), down.at[step(work.y, d)], d1.at[d], along_y[d - 1])
    work.first()
    for e in range(1, 8):
        copies.push(("t1", e), mod, t1.at[e], peers[e - 1])
        copies.push(("cap", e), cap, o_cap.at[seq], peers[e - 1])
    keep(down.at[work.y], d1.at[0])
    keep(mod, t1.at[0])
    keep(cap, o_cap.at[seq])
    keep.wait()
    beside = device(work.xh * 2 + 1 - work.xl, work.y, work.z, work.c)
    for d in (1, 2, 3):
        copies.arrived(("d1", d), d1.at[d], along_y[3 - d])
    add_up([d1.at[pl.ds(i, 1)] for i in range(4)], d1s)
    copies.push(("d2",), d1s, d2, beside)
    work.second()
    copies.arrived(("d2",), d2, beside)
    add_up([d1s, d2], d2s)
    keep(d2s.at[0], o_down.at[work.y])
    for d in (1, 2, 3):
        copies.push(("d3", d), d2s.at[0], o_down.at[work.y], along_y[d - 1])
    work.third()
    total = t1[0].astype(jnp.float32)
    for e in range(1, 8):
        copies.arrived(("t1", e), t1.at[e], peers[7 - e])
        total = total + t1[e].astype(jnp.float32)
    o_mod[...] = total
    work.fourth()
    work.last()
    for d in (1, 2, 3):
        copies.arrived(("d3", d), o_down.at[step(work.y, -d)], along_y[3 - d])
    for e in range(1, 8):
        copies.arrived(("cap", e), o_cap.at[(seq + 8 - e) % 8], peers[7 - e])
    keep.wait()
    copies.finish()


def scatter_rest(qkv, small, down, mod, cap):
    width = down.shape[-1]
    bf16 = lambda *shape: jax.ShapeDtypeStruct(shape, jnp.bfloat16)
    vmem = lambda *shape: pltpu.VMEM(shape, jnp.bfloat16)
    return pl.pallas_call(
        rest_kernel,
        out_shape=(
            bf16(HD, 1536), bf16(HD, 1024), bf16(HD, 1024), bf16(4, HD, width),
            jax.ShapeDtypeStruct(mod.shape, jnp.float32), bf16(8, *cap.shape),
        ),
        in_specs=[ANYWHERE] * 5,
        out_specs=(ANYWHERE,) * 4 + (ON_CHIP, ANYWHERE),
        scratch_shapes=[
            vmem(4, HD, width), vmem(1, HD, width), vmem(1, HD, width), vmem(1, HD, width),
            vmem(8, *mod.shape),
        ]
        + Scatter.buffers(1536, 1024, 1024)
        + semaphores(18, 96, 96),
        compiler_params=parameters(3),
    )(qkv, small, down, mod, cap)


GELU = 0.7978845608028654
CUBE = 0.044715


def mlp_kernel(
    rows, other, own, grad, up, down, bias, out, grad_rows, bias_grad, up_other, up_own, down_grad
):
    @pl.when(pl.program_id(0) == 0)
    def _():
        out[...] = jnp.zeros_like(out)
        grad_rows[...] = jnp.zeros_like(grad_rows)

    across = (((1,), (1,)), ((), ()))
    hidden = project(rows[...], up[...]) + bias[...]
    square = hidden * hidden
    bend = jnp.tanh(GELU * (hidden + CUBE * hidden * square))
    active = (0.5 * hidden * (1.0 + bend)).astype(jnp.bfloat16)
    slope = 0.5 * (1.0 + bend) + 0.5 * hidden * (1.0 - bend * bend) * (
        GELU * (1.0 + 3.0 * CUBE * square)
    )
    out[...] += project(active, down[...])
    grad_act = lax.dot_general(grad[...], down[...], across, preferred_element_type=jnp.float32)
    grad_hidden = grad_act * slope
    rounded = grad_hidden.astype(jnp.bfloat16)
    bias_grad[...] = jnp.sum(rounded.astype(jnp.float32), axis=0, keepdims=True)
    grad_rows[...] += lax.dot_general(rounded, up[...], across, preferred_element_type=jnp.float32)
    up_other[...] = project(other[...], rounded).astype(jnp.bfloat16)
    up_own[...] = project(own[...], rounded).astype(jnp.bfloat16)
    down_grad[...] = lax.dot_general(
        active, grad[...], (((0,), (0,)), ((), ())), preferred_element_type=jnp.float32
    ).astype(jnp.bfloat16)


def mlp(rows, grad, up, down, bias):
    tokens, width = rows.shape
    units, size = up.shape[1], 512
    own, other = by_core(rows.T)
    fixed = lambda *shape: pl.BlockSpec(shape, lambda j: (0, 0))
    wide = lambda n: pl.BlockSpec((n, size), lambda j: (0, j))
    tall = pl.BlockSpec((size, width), lambda j: (j, 0))
    f32 = lambda *shape: jax.ShapeDtypeStruct(shape, jnp.float32)
    bf16 = lambda *shape: jax.ShapeDtypeStruct(shape, jnp.bfloat16)
    return pl.pallas_call(
        mlp_kernel,
        grid=(units // size,),
        out_shape=(
            f32(tokens, width), f32(tokens, width), f32(1, units),
            bf16(width // 2, units), bf16(width // 2, units), bf16(units, width),
        ),
        in_specs=[
            fixed(tokens, width), fixed(width // 2, tokens), fixed(width // 2, tokens),
            fixed(tokens, width), wide(width), tall, wide(1),
        ],
        out_specs=(
            fixed(tokens, width), fixed(tokens, width), wide(1),
            wide(width // 2), wide(width // 2), tall,
        ),
        compiler_params=pltpu.CompilerParams(vmem_limit_bytes=48 * 1024 * 1024),
    )(rows, other, own, grad, up, down, bias)


def sibling_pairs():
    return [(i, i + 1 - 2 * (i % 2)) for i in range(16)]


def by_core(matrix):
    core = lax.axis_index("fsdp") % 2
    split = matrix.reshape((8, 2, -1) + matrix.shape[1:])
    pick = lambda which: lax.dynamic_index_in_dim(split, which, 1, keepdims=False).reshape(
        (-1,) + matrix.shape[1:]
    )
    return pick(core), pick(1 - core)


def pair_grad(former, latter):
    own, other = by_core(former.T)
    theirs = project(other, latter).astype(jnp.bfloat16)
    received = lax.ppermute(theirs, "fsdp", sibling_pairs())
    return (project(own, latter) + received.astype(jnp.float32)).astype(jnp.bfloat16)


def on_device(
    latents,
    timestep,
    caption,
    shift_table,
    qkv_weight,
    query_bias,
    value_bias,
    proj_weight,
    proj_bias,
    cross_query,
    cross_qbias,
    cross_kv,
    cross_vbias,
    cross_proj,
    cross_pbias,
    up_weight,
    up_bias,
    down_weight,
    down_bias,
    cotangent,
):
    group = lax.axis_index("fsdp")
    small = jnp.zeros((32 * HD * 16,), jnp.bfloat16)
    at = 0
    for vector in (
        shift_table, query_bias, value_bias, proj_bias, cross_qbias, cross_vbias, cross_pbias,
        down_bias, up_bias,
    ):
        small = lax.dynamic_update_slice(small, vector, (at + group * vector.shape[0],))
        at += 16 * vector.shape[0]
    full_qkv, each_small = gather_early(qkv_weight, small.reshape(32, -1))
    full_small = jnp.sum(each_small.reshape(16, 32, -1).astype(jnp.float32), axis=0)
    full_table = full_small[:6]
    full_qbias, full_vbias, full_pbias, full_cqbias, full_cvbias, full_cpbias, full_dbias = (
        full_small[6 + i] for i in range(7)
    )
    full_ubias = full_small[13:17].reshape(-1)
    latent_count, local_len, model_width = latents.shape
    inputs = latents.astype(jnp.float32)
    modulation = (full_table + timestep.astype(jnp.float32).reshape(6, model_width)).reshape(
        latent_count, 6, 1, model_width
    )
    shift_one, scale_one, gate_one = (modulation[:, 0], modulation[:, 1], modulation[:, 2])
    shift_two, scale_two, gate_two = (modulation[:, 3], modulation[:, 4], modulation[:, 5])
    pre_one, pull_one = jax.vjp(modulate, inputs, shift_one, scale_one)
    normed_one = pre_one.astype(jnp.bfloat16)
    qkv_bias = jnp.concatenate([full_qbias, jnp.zeros_like(full_qbias), full_vbias]).astype(
        jnp.float32
    )
    packed = (project(normed_one, full_qkv) + qkv_bias).astype(jnp.bfloat16)
    full_up, full_cquery, full_ckv, full_pair, full_down, heads, rows = gather_late(
        (
            up_weight,
            cross_query,
            cross_kv,
            jnp.concatenate([proj_weight, cross_proj], axis=1),
            down_weight,
        ),
        packed[0],
    )
    full_proj, full_cproj = jnp.split(full_pair, 2, axis=1)
    tok_major = rows[None]
    branch_one = project(tok_major, full_proj) + full_pbias.astype(jnp.float32)
    after_one = inputs + gate_one * branch_one
    middle = after_one.astype(jnp.bfloat16)
    cross_rows = (project(middle, full_cquery) + full_cqbias.astype(jnp.float32)).astype(
        jnp.bfloat16
    )
    kv_bias = jnp.concatenate([jnp.zeros_like(full_cvbias), full_cvbias]).astype(jnp.float32)
    text_kv = (project(caption, full_ckv) + kv_bias).astype(jnp.bfloat16)
    text_keys = by_heads(text_kv[..., :model_width])
    text_values = by_heads(text_kv[..., model_width:])
    cross_heads, _ = jax.vmap(attend_forward)(
        by_heads(cross_rows), text_keys, text_values
    )
    crossed = cross_heads.reshape(latent_count, local_len, model_width)
    branch_two = project(crossed, full_cproj) + full_cpbias.astype(jnp.float32)
    after_two = after_one + branch_two
    pre_two, pull_two = jax.vjp(modulate, after_two, shift_two, scale_two)
    normed_two = pre_two.astype(jnp.bfloat16)
    grad_out = cotangent.astype(jnp.float32)
    grad_three = (gate_two * grad_out).astype(jnp.bfloat16)
    product, grad_pre_two, up_bgrad, up_other, up_own, down_grad = mlp(
        normed_two[0], grad_three[0], full_up, full_down, full_ubias.reshape(1, -1)
    )
    up_received = lax.ppermute(up_other, "fsdp", sibling_pairs())
    down_part = lax.psum_scatter(down_grad, "fsdp", scatter_dimension=0, tiled=True)
    branch_three = product[None] + full_dbias.astype(jnp.float32)
    block_out = (after_two + gate_two * branch_three).astype(jnp.bfloat16)
    grad_gate_two = jnp.sum(grad_out * branch_three, axis=1, keepdims=True)
    down_bgrad = token_sum(grad_three)
    up_grad = (up_own.astype(jnp.float32) + up_received.astype(jnp.float32)).astype(jnp.bfloat16)
    grad_pre_two = grad_pre_two[None]
    grad_mid_two, grad_shift_two, grad_scale_two = pull_two(grad_pre_two)
    grad_after_two = grad_out + grad_mid_two
    grad_branch_two = grad_after_two.astype(jnp.bfloat16)
    cproj_grad = pair_grad(crossed[0], grad_branch_two[0])
    cproj_bgrad = token_sum(grad_branch_two)
    grad_cross, grad_text = cross_back(
        cross_rows[0], text_kv[0], grad_branch_two[0], full_cproj
    )
    grad_cross_rows = grad_cross[None]
    cquery_grad = pair_grad(middle[0], grad_cross_rows[0])
    cquery_bgrad = token_sum(grad_cross_rows)
    grad_after_one = grad_after_two + project(grad_cross_rows, full_cquery.T)
    text_piece = grad_text.shape[0] // 8
    text_pieces = lax.all_to_all(
        grad_text.reshape(8, text_piece, grad_text.shape[1]), "seq", 0, 0
    )
    grad_gate_one = jnp.sum(grad_after_one * branch_one, axis=1, keepdims=True)
    grad_branch_one = (gate_one * grad_after_one).astype(jnp.bfloat16)
    proj_grad = pair_grad(tok_major[0], grad_branch_one[0])
    proj_bgrad = token_sum(grad_branch_one)
    grad_tok = project(grad_branch_one, full_proj.T).astype(jnp.bfloat16)
    text_pieces, grad_tok, up_grad, proj_grad, cquery_grad, cproj_grad = (
        lax.optimization_barrier(
            (text_pieces, grad_tok, up_grad, proj_grad, cquery_grad, cproj_grad)
        )
    )
    text_grad = jnp.sum(text_pieces.astype(jnp.float32), axis=0).astype(jnp.bfloat16)
    caption_part = lax.dynamic_slice_in_dim(
        jnp.pad(caption[0], ((0, grad_text.shape[0] - caption.shape[1]), (0, 0))),
        lax.axis_index("seq") * text_piece, text_piece, 0
    )
    ckv_grad = pair_grad(caption_part, text_grad)
    cvalue_bgrad = jnp.sum(text_grad[:, model_width:].astype(jnp.float32), axis=0)
    caption_piece = project(text_grad, full_ckv.T)
    blocks = lambda grad: grad.reshape(4, 2, HD, -1)
    mix = jnp.concatenate(
        [proj_grad, cproj_grad, cquery_grad, ckv_grad, jnp.zeros((8 * HD, 384), jnp.bfloat16)],
        axis=1,
    )
    sum_up, sum_mix, sum_att, flat = scatter_back(
        blocks(up_grad), blocks(mix), heads, grad_tok[0]
    )
    up_one, mix_one, up_two, mix_two = jnp.split(sum_mix, (1024, 1536, 2560), axis=1)
    sum_up = jnp.concatenate([sum_up, up_one, up_two], axis=1)
    sum_mix = jnp.concatenate([mix_one, mix_two, sum_att], axis=1)
    grad_flat = flat[None]
    qkv_grad = pair_grad(normed_one[0], grad_flat[0])
    qbias_grad = token_sum(grad_flat[..., :model_width])
    vbias_grad = token_sum(grad_flat[..., 2 * model_width :])
    grad_pre_one = project(grad_flat, full_qkv.T)
    grad_norm_one, grad_shift_one, grad_scale_one = pull_one(grad_pre_one)
    grad_latents = grad_after_one + grad_norm_one
    grad_mod = jnp.concatenate(
        [
            grad_shift_one,
            grad_scale_one,
            grad_gate_one,
            grad_shift_two,
            grad_scale_two,
            grad_gate_two,
        ],
        axis=1,
    )
    grad_mod = grad_mod.reshape(latent_count, 6 * model_width)
    small_grad = jnp.concatenate(
        [
            grad_mod.reshape(-1, 6),
            qbias_grad.reshape(-1, 1),
            vbias_grad.reshape(-1, 1),
            proj_bgrad.reshape(-1, 1),
            cquery_bgrad.reshape(-1, 1),
            cvalue_bgrad.reshape(-1, 1),
            cproj_bgrad.reshape(-1, 1),
            down_bgrad.reshape(-1, 1),
            up_bgrad.reshape(-1, 4),
        ],
        axis=1,
    )
    small_own, small_other = by_core(small_grad)
    small_sum = small_own + lax.ppermute(
        small_other.astype(jnp.bfloat16), "fsdp", sibling_pairs()
    ).astype(jnp.float32)
    sum_q, sum_k, sum_v, sum_down, sum_mod, caption_all = scatter_rest(
        blocks(qkv_grad),
        jnp.pad(blocks(small_sum.astype(jnp.bfloat16)), ((0, 0), (0, 0), (0, 0), (0, 111))),
        down_part.reshape(4, HD, model_width),
        jnp.pad(grad_mod.astype(jnp.bfloat16).reshape(-1, 128), ((0, 10), (0, 0))),
        caption_piece.astype(jnp.bfloat16),
    )
    wide = lambda part: part.astype(jnp.float32)
    sum_small = wide(sum_v[:, 896 : 896 + 17])
    return (
        block_out,
        grad_latents,
        sum_mod[:54].reshape(1, -1),
        wide(caption_all.reshape(1, -1, model_width)[:, : caption.shape[1]]),
        sum_small[:, :6].reshape(-1),
        jnp.concatenate([wide(sum_q), wide(sum_k), wide(sum_v[:, :896])], axis=1),
        sum_small[:, 6],
        sum_small[:, 7],
        wide(sum_mix[:, :model_width]),
        sum_small[:, 8],
        wide(sum_mix[:, 2 * model_width : 3 * model_width]),
        sum_small[:, 9],
        wide(sum_mix[:, 3 * model_width : 5 * model_width]),
        sum_small[:, 10],
        wide(sum_mix[:, model_width : 2 * model_width]),
        sum_small[:, 11],
        wide(sum_up),
        sum_small[:, 13:17].reshape(-1),
        wide(sum_down.reshape(4 * HD, model_width)),
        sum_small[:, 12],
    )


def solution(mesh):
    placed = (
        P("fsdp", "seq", None),
        P("fsdp", None),
        P("fsdp", None, None),
        P("fsdp"),
        P("fsdp", None),
        P("fsdp"),
        P("fsdp"),
        P("fsdp", None),
        P("fsdp"),
        P("fsdp", None),
        P("fsdp"),
        P("fsdp", None),
        P("fsdp"),
        P("fsdp", None),
        P("fsdp"),
        P("fsdp", None),
        P("fsdp"),
        P("fsdp", None),
        P("fsdp"),
        P("fsdp", "seq", None),
    )
    return jax.shard_map(
        on_device,
        mesh=mesh,
        in_specs=placed,
        out_specs=(
            P("fsdp", "seq", None),
            P("fsdp", "seq", None),
            P("fsdp", None),
            P("fsdp", None, None),
            P("fsdp"),
            P("fsdp", None),
            P("fsdp"),
            P("fsdp"),
            P("fsdp", None),
            P("fsdp"),
            P("fsdp", None),
            P("fsdp"),
            P("fsdp", None),
            P("fsdp"),
            P("fsdp", None),
            P("fsdp"),
            P("fsdp", None),
            P("fsdp"),
            P("fsdp", None),
            P("fsdp"),
        ),
        check_vma=False,
    )
```

```python
import functools

import jax
import jax.numpy as jnp
from jax import lax
from jax.experimental import pallas as pl
from jax.experimental.pallas import tpu as pltpu
from jax.sharding import PartitionSpec as P

HD = 72
MESH = pl.DeviceIdType.MESH


epsilon = 1e-06


def for_sending(array):

    def short(part):
        return part.astype(jnp.bfloat16) if part.dtype == jnp.float32 else part

    return jax.tree.map(short, array)


def normalize(values):
    centre = values - jnp.mean(values, axis=-1, keepdims=True)
    spread = jnp.mean(centre * centre, axis=-1, keepdims=True)
    return centre * lax.rsqrt(spread + epsilon)


def modulate(values, shift, scale):
    return normalize(values) * (1.0 + scale) + shift


def project(former, latter):
    return jnp.dot(former, latter, preferred_element_type=jnp.float32)


def token_sum(values):
    return jnp.sum(values.astype(jnp.float32), axis=(0, 1))


def by_heads(matrix):
    return matrix.reshape(matrix.shape[:-1] + (matrix.shape[-1] // HD, HD))


def attend_forward(queries, key_rows, values):
    factor = HD ** (-0.5)
    scores = (
        jnp.einsum("qhd,khd->hqk", queries, key_rows, preferred_element_type=jnp.float32) * factor
    )
    largest = jnp.max(scores, axis=-1, keepdims=True)
    exponent = jnp.exp(scores - largest)
    partition = jnp.sum(exponent, axis=-1, keepdims=True)
    weights = (exponent / partition).astype(jnp.bfloat16)
    output = jnp.einsum("hqk,khd->qhd", weights, values, preferred_element_type=jnp.float32)
    return (output.astype(jnp.bfloat16), largest + jnp.log(partition))


def place():
    seq, fsdp = lax.axis_index("seq"), lax.axis_index("fsdp")
    y, x_lo = seq // 2, seq % 2
    z, rest = fsdp // 4, fsdp % 4
    x_hi, core = rest // 2, rest % 2
    return x_hi * 2 + x_lo, y, z, core


def device(x, y, z, core):
    return (y * 2 + x % 2, z * 4 + (x // 2) * 2 + core)


def step(value, by):
    return (value + by + 4) % 4


class Copies:
    def __init__(self, send, recv):
        self.send, self.recv, self.index, self.started = send, recv, {}, []

    def number(self, key):
        return self.index.setdefault(key, len(self.index))

    def push(self, key, src, dst, target):
        at = self.number(key)
        copy = pltpu.make_async_remote_copy(
            src_ref=src,
            dst_ref=dst,
            send_sem=self.send.at[at],
            recv_sem=self.recv.at[at],
            device_id=target,
            device_id_type=MESH,
        )
        copy.start()
        self.started.append(copy)

    def arrived(self, key, dst, source):
        at = self.number(key)
        pltpu.make_async_remote_copy(
            src_ref=dst,
            dst_ref=dst,
            send_sem=self.send.at[at],
            recv_sem=self.recv.at[at],
            device_id=source,
            device_id_type=MESH,
        ).wait_recv()

    def finish(self):
        for copy in self.started:
            copy.wait_send()


def greet(others):
    barrier = pltpu.get_barrier_semaphore()
    for other in others:
        pl.semaphore_signal(barrier, inc=1, device_id=other, device_id_type=MESH)
    pl.semaphore_wait(barrier, len(others))


class Piece:
    def __init__(self, source, out, axis, dim, start, size):
        self.source, self.out, self.axis = source, out, axis
        self.dim, self.start, self.size = dim, start, size

    def cut(self, part):
        parts = {"x": 2, "y": 4, "z": 1}[self.axis]
        size = self.size // parts
        unit = 128 if self.dim == 1 else 16
        start = self.start if parts == 1 else pl.multiple_of(self.start + part * size, unit)
        window = pl.ds(start, size)
        return (slice(None), window) if self.dim == 1 else (window, slice(None))


class Gather:
    def __init__(self, pieces, copies, local):
        self.pieces, self.copies, self.local = pieces, copies, local
        self.x, self.y, self.z, self.c = x, y, z, c = place()
        self.xh, self.xl = x // 2, x % 2
        self.sibling = device(x, y, z, 1 - c)
        self.far = device(step(x, 2), y, z, c)
        self.lines = {
            "x": [device(step(x, d), y, z, c) for d in (1, 2, 3)],
            "y": [device(x, step(y, d), z, c) for d in (1, 2, 3)],
            "z": [device(x, y, step(z, d), c) for d in (1, 2, 3)],
        }
        self.part = {"x": self.xl, "y": y, "z": 0}

    def others(self):
        return [self.sibling] + self.lines["x"] + self.lines["y"] + self.lines["z"]

    def block(self, p, dz, flip, part, core=None):
        core = self.c if core is None else core
        return p.out.at[(step(self.z, -dz), (self.xh + flip) % 2, core) + p.cut(part)]

    def both(self, key, src, dst, axis):
        self.copies.push(key + (1,), src, dst, self.lines[axis][0])
        self.copies.push(key + (3,), src, dst, self.lines[axis][2])

    def first(self):
        self.stays = []
        for n, p in enumerate(self.pieces):
            mine = p.source.at[p.cut(self.part[p.axis])]
            there = self.block(p, 0, 0, self.part[p.axis])
            copy = pltpu.make_async_copy(mine, there, self.local.at[n])
            copy.start()
            self.stays.append(copy)
            if p.axis != "x":
                self.copies.push((n, "far"), mine, there, self.far)
            if p.axis != "z":
                for d in (1, 2, 3):
                    self.copies.push((n, "mid", 0, d), mine, there, self.lines["z"][d - 1])
        for n, p in enumerate(self.pieces):
            mine = p.source.at[p.cut(self.part[p.axis])]
            self.both((n, "end", 0, 0), mine, self.block(p, 0, 0, self.part[p.axis]), p.axis)

    def second(self):
        for n, p in enumerate(self.pieces):
            if p.axis == "x":
                continue
            block = self.block(p, 0, 1, self.part[p.axis])
            self.copies.arrived((n, "far"), block, self.far)
            if p.axis == "y":
                for d in (1, 2, 3):
                    self.copies.push((n, "mid", 1, d), block, block, self.lines["z"][d - 1])
            self.both((n, "end", 0, 1), block, block, p.axis)

    def third(self):
        for dz in (1, 3, 2):
            for n, p in enumerate(self.pieces):
                if p.axis == "z":
                    continue
                for flip in (0, 1) if p.axis == "y" else (0,):
                    block = self.block(p, dz, flip, self.part[p.axis])
                    self.copies.arrived((n, "mid", flip, dz), block, self.lines["z"][3 - dz])
                    self.both((n, "end", dz, flip), block, block, p.axis)

    def blocks(self, p):
        if p.axis == "z":
            return ((0, 0), (0, 1))
        return tuple((dz, f) for dz in (0, 1, 3, 2) for f in ((0, 1) if p.axis == "y" else (0,)))

    def ended(self, n, p, dz, flip, d):
        if p.axis == "z":
            block = self.block(p, d, flip, 0)
        elif p.axis == "y":
            block = self.block(p, dz, flip, step(self.y, -d))
        else:
            from_x = step(self.x, -d)
            block = p.out.at[(step(self.z, -dz), from_x // 2, self.c) + p.cut(from_x % 2)]
        self.copies.arrived((n, "end", dz, flip, d), block, self.lines[p.axis][3 - d])
        return block

    def group(self, p, d, core):
        if p.axis == "z":
            return p.out.at[(step(self.z, -d), slice(None), core) + p.cut(0)]
        if p.axis == "y":
            return p.out.at[(slice(None), slice(None), core) + p.cut(step(self.y, -d))]
        from_x = step(self.x, -d)
        return p.out.at[(slice(None), from_x // 2, core) + p.cut(from_x % 2)]

    def share(self, n, p, d):
        block = self.group(p, d, self.c)
        self.copies.push((n, "core", d), block, block, self.sibling)

    def fourth(self):
        for copy in self.stays:
            copy.wait()
        for n, p in enumerate(self.pieces):
            self.share(n, p, 0)
        for at in range(8):
            for n, p in enumerate(self.pieces):
                if at >= len(self.blocks(p)):
                    continue
                dz, flip = self.blocks(p)[at]
                line = self.lines[p.axis]
                for d in (1, 3):
                    block = self.ended(n, p, dz, flip, d)
                    if (at % 2 == 0) == (d == 1):
                        on = line[0] if d == 1 else line[2]
                        self.copies.push((n, "end", dz, flip, 2), block, block, on)
                if at == len(self.blocks(p)) - 1:
                    self.share(n, p, 1)
                    self.share(n, p, 3)

    def last(self):
        for n, p in enumerate(self.pieces):
            for dz, flip in self.blocks(p):
                self.ended(n, p, dz, flip, 2)
            self.share(n, p, 2)
        for d in (0, 1, 3, 2):
            for n, p in enumerate(self.pieces):
                block = self.group(p, d, 1 - self.c)
                self.copies.arrived((n, "core", d), block, self.sibling)


def early_kernel(qkv, small, o_qkv, o_small, local, send, recv):
    pieces = [
        Piece(small, o_small, "z", 0, 0, small.shape[0]),
        Piece(qkv, o_qkv, "z", 1, 18 * 128, 9 * 128),
        Piece(qkv, o_qkv, "x", 1, 8 * 128, 10 * 128),
        Piece(qkv, o_qkv, "y", 1, 0, 8 * 128),
    ]
    copies = Copies(send, recv)
    work = Gather(pieces, copies, local)
    greet(work.others())
    work.first()
    work.second()
    work.third()
    work.fourth()
    work.last()
    copies.finish()


PAIR = 2 * HD


def head_slices(rows):
    for j in range(rows.shape[1] // (8 * PAIR)):
        for to in range(8):
            yield to, pl.ds(j * PAIR, PAIR), pl.ds((j * 8 + to) * PAIR, PAIR)


def exchange(copies, name, seq, peers, sent, got, local):
    for e in range(1, 8):
        copies.push((name, e), sent.at[(seq + e) % 8], got.at[seq], peers[e - 1])
    copy = pltpu.make_async_copy(sent.at[seq], got.at[seq], local)
    copy.start()
    return copy


def exchanged(copies, name, seq, peers, got, copy):
    copy.wait()
    for e in range(1, 8):
        copies.arrived((name, e), got.at[(seq + 8 - e) % 8], peers[7 - e])


def seq_peers():
    x, y, z, c = place()
    seq = y * 2 + x % 2
    return seq, [((seq + e) % 8, z * 4 + (x // 2) * 2 + c) for e in range(1, 8)]


def unique(x, y, z, c, extra):
    _, peers = seq_peers()
    far = [device((1 - x // 2) * 2 + e, y, z, c) for e in (0, 1)]
    return peers + far + [device(x, y, step(z, d), c) for d in (1, 2, 3)] + extra


CHUNK = 256


def head(which, h):
    return pl.ds(which * PAIR + h * HD, HD)


def attend(heads, h, out):
    tokens = 8 * 128
    keys = heads[:, :, head(1, h)].reshape(tokens, HD)
    values = heads[:, :, head(2, h)].reshape(tokens, HD)

    @pl.loop(0, tokens // CHUNK)
    def _(i):
        queries = heads[pl.ds(i * 2, 2), :, head(0, h)].reshape(CHUNK, HD)
        scores = lax.dot_general(
            queries, keys, (((1,), (1,)), ((), ())), preferred_element_type=jnp.float32
        ) * (HD**-0.5)
        exponent = jnp.exp(scores - jnp.max(scores, axis=1, keepdims=True))
        weights = exponent * (1.0 / jnp.sum(exponent, axis=1, keepdims=True))
        got = jnp.dot(weights.astype(jnp.bfloat16), values, preferred_element_type=jnp.float32)
        out[pl.ds(i * 2, 2), :, head(0, h)] = got.astype(jnp.bfloat16).reshape(2, 128, HD)


def head_back(queries, keys, values, grad, mask):
    across = (((1,), (1,)), ((), ()))
    scores = lax.dot_general(keys, queries, across, preferred_element_type=jnp.float32)
    scores = scores * (HD**-0.5) if mask is None else scores * (HD**-0.5) + mask
    exponent = jnp.exp(scores - jnp.max(scores, axis=0, keepdims=True))
    weights = exponent * (1.0 / jnp.sum(exponent, axis=0, keepdims=True))
    grad_weights = lax.dot_general(values, grad, across, preferred_element_type=jnp.float32)
    inner = jnp.sum(weights * grad_weights, axis=0, keepdims=True)
    grad_scores = (weights * (grad_weights - inner)).astype(jnp.bfloat16)
    grad_q = lax.dot_general(
        grad_scores, keys, (((0,), (0,)), ((), ())), preferred_element_type=jnp.float32
    ) * (HD**-0.5)
    return weights.astype(jnp.bfloat16), grad_scores, grad_q.astype(jnp.bfloat16)


def attend_back(heads, grads, h, out, key_sum, value_sum):
    tokens = 8 * 128
    keys = heads[:, :, head(1, h)].reshape(tokens, HD)
    values = heads[:, :, head(2, h)].reshape(tokens, HD)
    key_sum[...] = jnp.zeros_like(key_sum)
    value_sum[...] = jnp.zeros_like(value_sum)

    @pl.loop(0, tokens // CHUNK)
    def _(i):
        queries = heads[pl.ds(i * 2, 2), :, head(0, h)].reshape(CHUNK, HD)
        grad = grads[pl.ds(i * 2, 2), :, head(0, h)].reshape(CHUNK, HD)
        weights, grad_scores, grad_q = head_back(queries, keys, values, grad, None)
        value_sum[...] += project(weights, grad)
        key_sum[...] += project(grad_scores, queries)
        out[pl.ds(i * 2, 2), :, head(0, h)] = grad_q.reshape(2, 128, HD)

    out[:, :, head(1, h)] = (key_sum[...] * (HD**-0.5)).astype(jnp.bfloat16).reshape(8, 128, HD)
    out[:, :, head(2, h)] = value_sum[...].astype(jnp.bfloat16).reshape(8, 128, HD)


def cross_kernel(queries, text, grad_out, weight, grad_queries, grad_text, *, real):
    grad = lax.dot_general(
        grad_out[...], weight[...], (((1,), (1,)), ((), ())), preferred_element_type=jnp.float32
    ).astype(jnp.bfloat16)
    rows = lax.broadcasted_iota(jnp.int32, (text.shape[0], queries.shape[0]), 0)
    mask = jnp.where(rows < real, 0.0, -1e30)
    width = queries.shape[1]
    for h in range(width // HD):
        mine, values = pl.ds(h * HD, HD), pl.ds(width + h * HD, HD)
        slopes = grad[:, h * HD : (h + 1) * HD]
        weights, grad_scores, grad_q = head_back(
            queries[:, mine], text[:, mine], text[:, values], slopes, mask
        )
        grad_queries[:, mine] = grad_q
        grad_key = project(grad_scores, queries[:, mine]) * (HD**-0.5)
        grad_text[:, mine] = grad_key.astype(jnp.bfloat16)
        grad_text[:, values] = project(weights, slopes).astype(jnp.bfloat16)


def cross_back(queries, text, grad_out, weight):
    real = text.shape[0]
    text = jnp.pad(text, ((0, -real % 128), (0, 0)))
    bf16 = lambda like: jax.ShapeDtypeStruct(like.shape, jnp.bfloat16)
    return pl.pallas_call(
        functools.partial(cross_kernel, real=real),
        out_shape=(bf16(queries), bf16(text)),
        in_specs=[ON_CHIP] * 4,
        out_specs=(ON_CHIP,) * 2,
        compiler_params=pltpu.CompilerParams(vmem_limit_bytes=48 * 1024 * 1024),
    )(queries, text, grad_out, weight)


def late_kernel(
    up, cq, ckv, proj, cproj, down, packed,
    o_up, o_cq, o_ckv, o_proj, o_cproj, o_down, o_heads, o_rows,
    sent, heads, mixed, joined, local, send, recv,
):
    height = down.shape[0]
    pieces = [
        Piece(proj, o_proj, "z", 1, 0, proj.shape[1]),
        Piece(cq, o_cq, "z", 1, 0, cq.shape[1]),
        Piece(cproj, o_cproj, "z", 1, 0, cproj.shape[1]),
        Piece(ckv, o_ckv, "x", 1, 0, ckv.shape[1]),
        Piece(up, o_up, "y", 1, 0, up.shape[1]),
        Piece(down, o_down, "x", 0, 128, height - 128),
        Piece(down, o_down, "y", 0, 0, 128),
    ]
    copies = Copies(send, recv)
    work = Gather(pieces, copies, local)
    seq, peers = seq_peers()
    greet(unique(work.x, work.y, work.z, work.c, [work.sibling]))
    for to, what, at in head_slices(packed):
        sent[to, :, what] = packed[:, at]
    own = exchange(copies, "in", seq, peers, sent, heads, local.at[7])
    work.first()
    exchanged(copies, "in", seq, peers, heads, own)
    keep = pltpu.make_async_copy(heads, o_heads, local.at[8])
    keep.start()
    attend(heads, 0, mixed)
    work.second()
    attend(heads, 1, mixed)
    own = exchange(copies, "out", seq, peers, mixed, joined, local.at[9])
    work.third()
    work.fourth()
    exchanged(copies, "out", seq, peers, joined, own)
    for at, what, to in head_slices(o_rows):
        o_rows[:, to] = joined[at, :, what]
    work.last()
    keep.wait()
    copies.finish()


def whole(out):
    return out.reshape((-1,) + out.shape[4:])


def full_shapes(shards):
    return tuple(jax.ShapeDtypeStruct((4, 2, 2) + s.shape, s.dtype) for s in shards)


def semaphores(*counts):
    return [pltpu.SemaphoreType.DMA((n,)) for n in counts]


ANYWHERE = pl.BlockSpec(memory_space=pl.ANY)
ON_CHIP = pl.BlockSpec(memory_space=pltpu.VMEM)


def parameters(collective):
    return pltpu.CompilerParams(
        collective_id=collective, has_side_effects=True, vmem_limit_bytes=48 * 1024 * 1024
    )


def gather_early(*shards):
    outs = pl.pallas_call(
        early_kernel,
        out_shape=full_shapes(shards),
        in_specs=[ANYWHERE] * 2,
        out_specs=(ANYWHERE,) * 2,
        scratch_shapes=semaphores(4, 128, 128),
        compiler_params=parameters(0),
    )(*shards)
    return tuple(whole(out) for out in outs)


def gather_late(shards, packed):
    bf16 = lambda *shape: jax.ShapeDtypeStruct(shape, jnp.bfloat16)
    vmem = lambda *shape: pltpu.VMEM(shape, jnp.bfloat16)
    outs = pl.pallas_call(
        late_kernel,
        out_shape=full_shapes(shards) + (bf16(8, 128, 3 * PAIR), bf16(128, 8 * PAIR)),
        in_specs=[ANYWHERE] * 6 + [ON_CHIP],
        out_specs=(ANYWHERE,) * 7 + (ON_CHIP,),
        scratch_shapes=[
            vmem(8, 128, 3 * PAIR), vmem(8, 128, 3 * PAIR), vmem(8, 128, PAIR), vmem(8, 128, PAIR),
        ]
        + semaphores(10, 256, 256),
        compiler_params=parameters(1),
    )(*shards, packed)
    return tuple(whole(out) for out in outs[:6]) + outs[6:]


def add_up(parts, out):
    blocks, _, columns = out.shape
    tile = next(t for t in (384, 512, 256, 128) if columns % t == 0)

    @pl.loop(0, blocks * (columns // tile))
    def _(i):
        block = i // (columns // tile)
        cols = pl.ds(pl.multiple_of((i % (columns // tile)) * tile, 128), tile)
        total = parts[0][block, :, cols].astype(jnp.float32)
        for part in parts[1:]:
            total = total + part[block, :, cols].astype(jnp.float32)
        out[block, :, cols] = total.astype(out.dtype)


def columns(part, width, start=0):
    return pl.ds(pl.multiple_of(start + part * width, 128), width)


class Scatter:
    def __init__(self, by_y, by_x, by_z, outs, scratch, copies, keep):
        self.by_y, self.by_x, self.by_z = by_y, by_x, by_z
        self.o_up, self.o_mix, self.o_att = outs
        self.scratch, self.copies, self.keep = scratch, copies, keep
        self.x, self.y, self.z, self.c = x, y, z, c = place()
        self.xh, self.xl = x // 2, x % 2
        self.seq, self.peers = seq_peers()
        self.along_x = [device(step(x, d), y, z, c) for d in (1, 2, 3)]
        self.along_y = [device(x, step(y, d), z, c) for d in (1, 2, 3)]
        self.along_z = [device(x, y, step(z, d), c) for d in (1, 2, 3)]

    @staticmethod
    def buffers(by_y, by_x, by_z):
        vmem = lambda *shape: pltpu.VMEM(shape, jnp.bfloat16)
        wy, wx, wz = by_y // 4, by_x // 2, by_z
        return [
            vmem(4, 4, 2, HD, wy), vmem(4, 2, HD, wy), vmem(4, 2, HD, wy),
            vmem(2, HD, wy), vmem(4, HD, wy), vmem(1, HD, wy),
            vmem(4, 2, HD, wz), vmem(2, HD, wz), vmem(4, 1, HD, wz // 2),
            vmem(1, HD, wz // 2), vmem(4, 1, HD, wz // 8), vmem(1, HD, wz // 8),
            vmem(4, 4, HD, wx), vmem(4, HD, wx), vmem(4, 4, HD, wx // 4),
            vmem(4, HD, wx // 4), vmem(4, HD, wx // 4), vmem(1, HD, wx // 4),
        ]

    def first(self):
        u1, a1, m1 = self.scratch[0], self.scratch[6], self.scratch[12]
        up, up_at, up_size = self.by_y
        for d in (1, 2, 3):
            to_x, to_y, to_z = step(self.x, d), step(self.y, d), step(self.z, d)
            cols = columns(to_y, up_size // 4, up_at)
            self.copies.push(("u1", d), up.at[:, :, :, cols], u1.at[d], self.along_y[d - 1])
            at = 0
            for n, (source, start, size) in enumerate(self.by_x):
                self.copies.push(
                    ("m1", n, d),
                    source.at[:, to_x // 2, :, columns(to_x % 2, size // 2, start)],
                    m1.at[d, :, :, pl.ds(at, size // 2)],
                    self.along_x[d - 1],
                )
                at += size // 2
            at = 0
            for n, (source, start, size) in enumerate(self.by_z):
                self.copies.push(
                    ("a1", n, d),
                    source.at[to_z, :, :, pl.ds(start, size)],
                    a1.at[d, :, :, pl.ds(at, size)],
                    self.along_z[d - 1],
                )
                at += size
        self.keep(up.at[:, :, :, columns(self.y, up_size // 4, up_at)], u1.at[0])
        at = 0
        for source, start, size in self.by_x:
            self.keep(
                source.at[:, self.xh, :, columns(self.xl, size // 2, start)],
                m1.at[0, :, :, pl.ds(at, size // 2)],
            )
            at += size // 2
        at = 0
        for source, start, size in self.by_z:
            self.keep(
                source.at[self.z, :, :, pl.ds(start, size)], a1.at[0, :, :, pl.ds(at, size)]
            )
            at += size

    def second(self):
        u1, u1s, u2 = self.scratch[:3]
        a1, a1s, a2 = self.scratch[6:9]
        m1, m1s, m2 = self.scratch[12:15]
        for d in (1, 2, 3):
            at = 0
            for n, (_, _, size) in enumerate(self.by_z):
                got = a1.at[d, :, :, pl.ds(at, size)]
                self.copies.arrived(("a1", n, d), got, self.along_z[3 - d])
                at += size
        add_up([a1.at[i] for i in range(4)], a1s)
        for d in (1, 2, 3):
            to = step(self.x, d)
            part = a1s.at[pl.ds(to // 2, 1), :, columns(to % 2, a2.shape[-1])]
            self.copies.push(("a2", d), part, a2.at[d], self.along_x[d - 1])
        for d in (1, 2, 3):
            at = 0
            for n, (_, _, size) in enumerate(self.by_x):
                got = m1.at[d, :, :, pl.ds(at, size // 2)]
                self.copies.arrived(("m1", n, d), got, self.along_x[3 - d])
                at += size // 2
        add_up([m1.at[i] for i in range(4)], m1s)
        for d in (1, 2, 3):
            cols = columns(step(self.y, d), m2.shape[-1])
            self.copies.push(("m2", d), m1s.at[:, :, cols], m2.at[d], self.along_y[d - 1])
        for d in (1, 2, 3):
            self.copies.arrived(("u1", d), u1.at[d], self.along_y[3 - d])
        for zz in range(4):
            add_up([u1.at[i, zz] for i in range(4)], u1s.at[zz])
        for d in (1, 2, 3):
            self.copies.push(
                ("u2", d), u1s.at[step(self.z, d)], u2.at[d], self.along_z[d - 1]
            )

    def third(self):
        u1s, u2, u2s, u3 = self.scratch[1:5]
        a1s, a2, a2s, a3 = self.scratch[7:11]
        m1s, m2, m2s, m3 = self.scratch[13:17]
        for d in (1, 2, 3):
            self.copies.arrived(("a2", d), a2.at[d], self.along_x[3 - d])
        mine = a1s.at[pl.ds(self.xh, 1), :, columns(self.xl, a2.shape[-1])]
        add_up([mine] + [a2.at[d] for d in (1, 2, 3)], a2s)
        for d in (1, 2, 3):
            part = a2s.at[:, :, columns(step(self.y, d), a3.shape[-1])]
            self.copies.push(("a3", d), part, a3.at[d], self.along_y[d - 1])
        for d in (1, 2, 3):
            self.copies.arrived(("m2", d), m2.at[d], self.along_y[3 - d])
        add_up(
            [m1s.at[:, :, columns(self.y, m2.shape[-1])]] + [m2.at[d] for d in (1, 2, 3)], m2s
        )
        for d in (1, 2, 3):
            self.copies.push(("m3", d), m2s.at[step(self.z, d)], m3.at[d], self.along_z[d - 1])
        for d in (1, 2, 3):
            self.copies.arrived(("u2", d), u2.at[d], self.along_z[3 - d])
        add_up([u1s.at[self.z]] + [u2.at[d] for d in (1, 2, 3)], u2s)
        for d in (1, 2, 3):
            to = step(self.x, d) // 2
            self.copies.push(("u3", d), u2s.at[to], u3.at[d], self.along_x[d - 1])

    def fourth(self):
        u2s, u3, u3s = self.scratch[3:6]
        a2s, a3, a3s = self.scratch[9:12]
        m2s, m3, m3s = self.scratch[15:18]
        own = a2s.at[:, :, columns(self.y, a3.shape[-1])]
        for name, line, own, got, total, out in (
            ("a", self.along_y, own, [a3.at[d] for d in (1, 2, 3)], a3s, self.o_att),
            ("u", self.along_x, u2s.at[pl.ds(self.xh, 1)],
             [u3.at[pl.ds(d, 1)] for d in (1, 2, 3)], u3s, self.o_up),
            ("m", self.along_z, m2s.at[pl.ds(self.z, 1)],
             [m3.at[pl.ds(d, 1)] for d in (1, 2, 3)], m3s, self.o_mix),
        ):
            for d in (1, 2, 3):
                dst = a3.at[d] if name == "a" else (u3 if name == "u" else m3).at[d]
                self.copies.arrived((name + "3", d), dst, line[3 - d])
            add_up([own] + got, total)
            if name == "u":
                spot = out.at[:, columns(self.y, total.shape[-1])]
                for d in (1, 2, 3):
                    self.copies.push(("u4", d), total.at[0], spot, self.along_y[d - 1])
            else:
                spot = out.at[:, self.spot(self.seq, total)]
                for e in range(1, 8):
                    self.copies.push((name + "4", e), total.at[0], spot, self.peers[e - 1])
            self.keep(total.at[0], spot)

    def spot(self, seq, total):
        return columns((seq % 2) * 4 + seq // 2, total.shape[-1])

    def last(self):
        for d in (1, 2, 3):
            got = self.o_up.at[:, columns(step(self.y, -d), self.o_up.shape[-1] // 4)]
            self.copies.arrived(("u4", d), got, self.along_y[3 - d])
        for name, total, out in (
            ("a4", self.scratch[11], self.o_att), ("m4", self.scratch[17], self.o_mix),
        ):
            for e in range(1, 8):
                got = out.at[:, self.spot((self.seq + 8 - e) % 8, total)]
                self.copies.arrived((name, e), got, self.peers[7 - e])


class Stays:
    def __init__(self, local):
        self.local, self.copies, self.done = local, [], 0

    def __call__(self, src, dst):
        copy = pltpu.make_async_copy(src, dst, self.local.at[len(self.copies)])
        copy.start()
        self.copies.append(copy)

    def wait(self):
        for copy in self.copies[self.done :]:
            copy.wait()
        self.done = len(self.copies)


def back_kernel(
    up, ckv, proj, cproj, cq, heads, grad_rows, o_up, o_mix, o_att, o_flat,
    sent, grads, mixed, joined, key_sum, value_sum, *rest,
):
    scratch, (local, send, recv) = rest[:18], rest[18:]
    copies, keep = Copies(send, recv), Stays(local)
    work = Scatter(
        (up, 0, 2560), [(up, 2560, 2048), (ckv, 0, 1024)],
        [(ckv, 1024, 1280), (proj, 0, 1152), (cproj, 0, 1152), (cq, 0, 1152)],
        (o_up, o_mix, o_att), scratch, copies, keep,
    )
    seq, peers = seq_peers()
    greet(unique(work.x, work.y, work.z, work.c, []))
    for to, what, at in head_slices(grad_rows):
        sent[to, :, what] = grad_rows[:, at]
    own = exchange(copies, "in", seq, peers, sent, grads, local.at[16])
    work.first()
    spare = scratch[6]
    spare[:, :, :, 4736:] = jnp.zeros(spare.shape[:3] + (384,), spare.dtype)
    exchanged(copies, "in", seq, peers, grads, own)
    for h in (0, 1):
        attend_back(heads, grads, h, mixed, key_sum, value_sum)
    own = exchange(copies, "out", seq, peers, mixed, joined, local.at[17])
    keep.wait()
    work.second()
    work.third()
    exchanged(copies, "out", seq, peers, joined, own)
    for at, what, to in head_slices(o_flat):
        o_flat[:, to] = joined[at, :, what]
    work.fourth()
    work.last()
    keep.wait()
    copies.finish()


def scatter_back(up, ckv, proj, cproj, cq, heads, grad_rows):
    bf16 = lambda *shape: jax.ShapeDtypeStruct(shape, jnp.bfloat16)
    vmem = lambda *shape: pltpu.VMEM(shape, jnp.bfloat16)
    return pl.pallas_call(
        back_kernel,
        out_shape=(
            bf16(HD, 2560), bf16(HD, 3072), bf16(HD, 5120), bf16(128, 24 * PAIR),
        ),
        in_specs=[ANYWHERE] * 5 + [ON_CHIP] * 2,
        out_specs=(ANYWHERE,) * 3 + (ON_CHIP,),
        scratch_shapes=[
            vmem(8, 128, PAIR), vmem(8, 128, PAIR), vmem(8, 128, 3 * PAIR), vmem(8, 128, 3 * PAIR),
            pltpu.VMEM((1024, HD), jnp.float32), pltpu.VMEM((1024, HD), jnp.float32),
        ]
        + Scatter.buffers(2560, 3072, 5120)
        + semaphores(18, 80, 80),
        compiler_params=parameters(2),
    )(up, ckv, proj, cproj, cq, heads, grad_rows)


def rest_kernel(
    qkv, small, down, mod, cap, o_up, o_mix, o_att, o_down, o_mod, o_cap,
    d1, d1s, d2, d2s, t1, *rest,
):
    scratch, (local, send, recv) = rest[:18], rest[18:]
    copies, keep = Copies(send, recv), Stays(local)
    work = Scatter(
        (qkv, 0, 512), [(qkv, 512, 1024)], [(qkv, 1536, 1920), (small, 0, 128)],
        (o_up, o_mix, o_att), scratch, copies, keep,
    )
    seq, peers, along_y = work.seq, work.peers, work.along_y
    greet(unique(work.x, work.y, work.z, work.c, []))
    for d in (1, 2, 3):
        copies.push(("d1", d), down.at[step(work.y, d)], d1.at[d], along_y[d - 1])
    work.first()
    for e in range(1, 8):
        copies.push(("t1", e), mod, t1.at[e], peers[e - 1])
        copies.push(("cap", e), cap, o_cap.at[seq], peers[e - 1])
    keep(down.at[work.y], d1.at[0])
    keep(mod, t1.at[0])
    keep(cap, o_cap.at[seq])
    keep.wait()
    beside = device(work.xh * 2 + 1 - work.xl, work.y, work.z, work.c)
    for d in (1, 2, 3):
        copies.arrived(("d1", d), d1.at[d], along_y[3 - d])
    add_up([d1.at[pl.ds(i, 1)] for i in range(4)], d1s)
    copies.push(("d2",), d1s, d2, beside)
    work.second()
    copies.arrived(("d2",), d2, beside)
    add_up([d1s, d2], d2s)
    keep(d2s.at[0], o_down.at[work.y])
    for d in (1, 2, 3):
        copies.push(("d3", d), d2s.at[0], o_down.at[work.y], along_y[d - 1])
    work.third()
    total = t1[0].astype(jnp.float32)
    for e in range(1, 8):
        copies.arrived(("t1", e), t1.at[e], peers[7 - e])
        total = total + t1[e].astype(jnp.float32)
    o_mod[...] = total
    work.fourth()
    work.last()
    for d in (1, 2, 3):
        copies.arrived(("d3", d), o_down.at[step(work.y, -d)], along_y[3 - d])
    for e in range(1, 8):
        copies.arrived(("cap", e), o_cap.at[(seq + 8 - e) % 8], peers[7 - e])
    keep.wait()
    copies.finish()


def scatter_rest(qkv, small, down, mod, cap):
    width = down.shape[-1]
    bf16 = lambda *shape: jax.ShapeDtypeStruct(shape, jnp.bfloat16)
    vmem = lambda *shape: pltpu.VMEM(shape, jnp.bfloat16)
    return pl.pallas_call(
        rest_kernel,
        out_shape=(
            bf16(HD, 512), bf16(HD, 1024), bf16(HD, 2048), bf16(4, HD, width),
            jax.ShapeDtypeStruct(mod.shape, jnp.float32), bf16(8, *cap.shape),
        ),
        in_specs=[ANYWHERE] * 5,
        out_specs=(ANYWHERE,) * 4 + (ON_CHIP, ANYWHERE),
        scratch_shapes=[
            vmem(4, HD, width), vmem(1, HD, width), vmem(1, HD, width), vmem(1, HD, width),
            vmem(8, *mod.shape),
        ]
        + Scatter.buffers(512, 1024, 2048)
        + semaphores(18, 96, 96),
        compiler_params=parameters(3),
    )(qkv, small, down, mod, cap)


GELU = 0.7978845608028654
CUBE = 0.044715


def mlp_kernel(
    rows, other, own, grad, up, down, bias, out, grad_rows, bias_grad, up_other, up_own, down_grad
):
    @pl.when(pl.program_id(0) == 0)
    def _():
        out[...] = jnp.zeros_like(out)
        grad_rows[...] = jnp.zeros_like(grad_rows)

    across = (((1,), (1,)), ((), ()))
    hidden = project(rows[...], up[...]) + bias[...]
    square = hidden * hidden
    bend = jnp.tanh(GELU * (hidden + CUBE * hidden * square))
    active = (0.5 * hidden * (1.0 + bend)).astype(jnp.bfloat16)
    slope = 0.5 * (1.0 + bend) + 0.5 * hidden * (1.0 - bend * bend) * (
        GELU * (1.0 + 3.0 * CUBE * square)
    )
    out[...] += project(active, down[...])
    grad_act = lax.dot_general(grad[...], down[...], across, preferred_element_type=jnp.float32)
    grad_hidden = grad_act * slope
    rounded = grad_hidden.astype(jnp.bfloat16)
    bias_grad[...] = jnp.sum(rounded.astype(jnp.float32), axis=0, keepdims=True)
    grad_rows[...] += lax.dot_general(rounded, up[...], across, preferred_element_type=jnp.float32)
    up_other[...] = project(other[...], rounded).astype(jnp.bfloat16)
    up_own[...] = project(own[...], rounded).astype(jnp.bfloat16)
    down_grad[...] = lax.dot_general(
        active, grad[...], (((0,), (0,)), ((), ())), preferred_element_type=jnp.float32
    ).astype(jnp.bfloat16)


def mlp(rows, grad, up, down, bias):
    tokens, width = rows.shape
    units, size = up.shape[1], 512
    own, other = by_core(rows.T)
    fixed = lambda *shape: pl.BlockSpec(shape, lambda j: (0, 0))
    wide = lambda n: pl.BlockSpec((n, size), lambda j: (0, j))
    tall = pl.BlockSpec((size, width), lambda j: (j, 0))
    f32 = lambda *shape: jax.ShapeDtypeStruct(shape, jnp.float32)
    bf16 = lambda *shape: jax.ShapeDtypeStruct(shape, jnp.bfloat16)
    return pl.pallas_call(
        mlp_kernel,
        grid=(units // size,),
        out_shape=(
            f32(tokens, width), f32(tokens, width), f32(1, units),
            bf16(width // 2, units), bf16(width // 2, units), bf16(units, width),
        ),
        in_specs=[
            fixed(tokens, width), fixed(width // 2, tokens), fixed(width // 2, tokens),
            fixed(tokens, width), wide(width), tall, wide(1),
        ],
        out_specs=(
            fixed(tokens, width), fixed(tokens, width), wide(1),
            wide(width // 2), wide(width // 2), tall,
        ),
        compiler_params=pltpu.CompilerParams(vmem_limit_bytes=48 * 1024 * 1024),
    )(rows, other, own, grad, up, down, bias)


def sibling_pairs():
    return [(i, i + 1 - 2 * (i % 2)) for i in range(16)]


def by_core(matrix):
    core = lax.axis_index("fsdp") % 2
    split = matrix.reshape((8, 2, -1) + matrix.shape[1:])
    pick = lambda which: lax.dynamic_index_in_dim(split, which, 1, keepdims=False).reshape(
        (-1,) + matrix.shape[1:]
    )
    return pick(core), pick(1 - core)


def pair_grad(former, latter):
    own, other = by_core(former.T)
    theirs = project(other, latter).astype(jnp.bfloat16)
    received = lax.ppermute(theirs, "fsdp", sibling_pairs())
    return (project(own, latter) + received.astype(jnp.float32)).astype(jnp.bfloat16)


def on_device(
    latents,
    timestep,
    caption,
    shift_table,
    qkv_weight,
    query_bias,
    value_bias,
    proj_weight,
    proj_bias,
    cross_query,
    cross_qbias,
    cross_kv,
    cross_vbias,
    cross_proj,
    cross_pbias,
    up_weight,
    up_bias,
    down_weight,
    down_bias,
    cotangent,
):
    small = jnp.concatenate(
        [
            shift_table, query_bias, value_bias, proj_bias, cross_qbias, cross_vbias, cross_pbias,
            down_bias, up_bias,
        ]
    ).reshape(-1, HD)
    rows_used = small.shape[0]
    full_qkv, each_small = gather_early(
        qkv_weight, jnp.pad(small, ((0, 32 - rows_used), (0, 128 - HD)))
    )
    each_small = each_small.reshape(16, 32, 128)[:, :rows_used, :HD].astype(jnp.float32)
    full_table = each_small[:, :6].reshape(6, -1)
    full_biases = each_small[:, 6:13].transpose(1, 0, 2).reshape(7, -1)
    full_qbias, full_vbias, full_pbias, full_cqbias, full_cvbias, full_cpbias, full_dbias = (
        full_biases[i] for i in range(7)
    )
    full_ubias = each_small[:, 13:17].reshape(-1)
    latent_count, local_len, model_width = latents.shape
    inputs = latents.astype(jnp.float32)
    modulation = (full_table + timestep.astype(jnp.float32).reshape(6, model_width)).reshape(
        latent_count, 6, 1, model_width
    )
    shift_one, scale_one, gate_one = (modulation[:, 0], modulation[:, 1], modulation[:, 2])
    shift_two, scale_two, gate_two = (modulation[:, 3], modulation[:, 4], modulation[:, 5])
    pre_one, pull_one = jax.vjp(modulate, inputs, shift_one, scale_one)
    normed_one = pre_one.astype(jnp.bfloat16)
    qkv_bias = jnp.concatenate([full_qbias, jnp.zeros_like(full_qbias), full_vbias]).astype(
        jnp.float32
    )
    packed = (project(normed_one, full_qkv) + qkv_bias).astype(jnp.bfloat16)
    full_up, full_cquery, full_ckv, full_proj, full_cproj, full_down, heads, rows = gather_late(
        (up_weight, cross_query, cross_kv, proj_weight, cross_proj, down_weight), packed[0]
    )
    tok_major = rows[None]
    branch_one = project(tok_major, full_proj) + full_pbias.astype(jnp.float32)
    after_one = inputs + gate_one * branch_one
    middle = after_one.astype(jnp.bfloat16)
    cross_rows = (project(middle, full_cquery) + full_cqbias.astype(jnp.float32)).astype(
        jnp.bfloat16
    )
    kv_bias = jnp.concatenate([jnp.zeros_like(full_cvbias), full_cvbias]).astype(jnp.float32)
    text_kv = (project(caption, full_ckv) + kv_bias).astype(jnp.bfloat16)
    text_keys = by_heads(text_kv[..., :model_width])
    text_values = by_heads(text_kv[..., model_width:])
    cross_heads, _ = jax.vmap(attend_forward)(
        by_heads(cross_rows), text_keys, text_values
    )
    crossed = cross_heads.reshape(latent_count, local_len, model_width)
    branch_two = project(crossed, full_cproj) + full_cpbias.astype(jnp.float32)
    after_two = after_one + branch_two
    pre_two, pull_two = jax.vjp(modulate, after_two, shift_two, scale_two)
    normed_two = pre_two.astype(jnp.bfloat16)
    grad_out = cotangent.astype(jnp.float32)
    grad_three = (gate_two * grad_out).astype(jnp.bfloat16)
    product, grad_pre_two, up_bgrad, up_other, up_own, down_grad = mlp(
        normed_two[0], grad_three[0], full_up, full_down, full_ubias.reshape(1, -1)
    )
    up_received = lax.ppermute(up_other, "fsdp", sibling_pairs())
    down_part = lax.psum_scatter(down_grad, "fsdp", scatter_dimension=0, tiled=True)
    branch_three = product[None] + full_dbias.astype(jnp.float32)
    block_out = (after_two + gate_two * branch_three).astype(jnp.bfloat16)
    grad_gate_two = jnp.sum(grad_out * branch_three, axis=1, keepdims=True)
    down_bgrad = token_sum(grad_three)
    up_grad = (up_own.astype(jnp.float32) + up_received.astype(jnp.float32)).astype(jnp.bfloat16)
    grad_pre_two = grad_pre_two[None]
    grad_mid_two, grad_shift_two, grad_scale_two = pull_two(grad_pre_two)
    grad_after_two = grad_out + grad_mid_two
    grad_branch_two = grad_after_two.astype(jnp.bfloat16)
    cproj_grad = pair_grad(crossed[0], grad_branch_two[0])
    cproj_bgrad = token_sum(grad_branch_two)
    grad_cross, grad_text = cross_back(
        cross_rows[0], text_kv[0], grad_branch_two[0], full_cproj
    )
    grad_cross_rows = grad_cross[None]
    cquery_grad = pair_grad(middle[0], grad_cross_rows[0])
    cquery_bgrad = token_sum(grad_cross_rows)
    grad_after_one = grad_after_two + project(grad_cross_rows, full_cquery.T)
    text_piece = grad_text.shape[0] // 8
    text_pieces = lax.all_to_all(
        grad_text.reshape(8, text_piece, grad_text.shape[1]), "seq", 0, 0
    )
    grad_gate_one = jnp.sum(grad_after_one * branch_one, axis=1, keepdims=True)
    grad_branch_one = (gate_one * grad_after_one).astype(jnp.bfloat16)
    proj_grad = pair_grad(tok_major[0], grad_branch_one[0])
    proj_bgrad = token_sum(grad_branch_one)
    grad_tok = project(grad_branch_one, full_proj.T).astype(jnp.bfloat16)
    text_pieces, grad_tok, up_grad, proj_grad, cquery_grad, cproj_grad = (
        lax.optimization_barrier(
            (text_pieces, grad_tok, up_grad, proj_grad, cquery_grad, cproj_grad)
        )
    )
    text_grad = jnp.sum(text_pieces.astype(jnp.float32), axis=0).astype(jnp.bfloat16)
    caption_part = lax.dynamic_slice_in_dim(
        jnp.pad(caption[0], ((0, grad_text.shape[0] - caption.shape[1]), (0, 0))),
        lax.axis_index("seq") * text_piece, text_piece, 0
    )
    ckv_grad = pair_grad(caption_part, text_grad)
    cvalue_bgrad = jnp.sum(text_grad[:, model_width:].astype(jnp.float32), axis=0)
    caption_piece = project(text_grad, full_ckv.T)
    blocks = lambda grad: grad.reshape(4, 2, HD, -1)
    sum_up, sum_mix, sum_att, flat = scatter_back(
        *(blocks(grad) for grad in (up_grad, ckv_grad, proj_grad, cproj_grad, cquery_grad)),
        heads,
        grad_tok[0],
    )
    up_one, ckv_one, up_two, ckv_two = jnp.split(sum_mix, (1024, 1536, 2560), axis=1)
    sum_up = jnp.concatenate([sum_up, up_one, up_two], axis=1)
    ckv_three, sum_proj, sum_cproj, sum_cquery, _ = jnp.split(
        sum_att, (1280, 2432, 3584, 4736), axis=1
    )
    sum_ckv = jnp.concatenate([ckv_one, ckv_two, ckv_three], axis=1)
    grad_flat = flat[None]
    qkv_grad = pair_grad(normed_one[0], grad_flat[0])
    qbias_grad = token_sum(grad_flat[..., :model_width])
    vbias_grad = token_sum(grad_flat[..., 2 * model_width :])
    grad_pre_one = project(grad_flat, full_qkv.T)
    grad_norm_one, grad_shift_one, grad_scale_one = pull_one(grad_pre_one)
    grad_latents = grad_after_one + grad_norm_one
    grad_mod = jnp.concatenate(
        [
            grad_shift_one,
            grad_scale_one,
            grad_gate_one,
            grad_shift_two,
            grad_scale_two,
            grad_gate_two,
        ],
        axis=1,
    )
    grad_mod = grad_mod.reshape(latent_count, 6 * model_width)
    small_grad = jnp.concatenate(
        [
            grad_mod.reshape(-1, 6),
            qbias_grad.reshape(-1, 1),
            vbias_grad.reshape(-1, 1),
            proj_bgrad.reshape(-1, 1),
            cquery_bgrad.reshape(-1, 1),
            cvalue_bgrad.reshape(-1, 1),
            cproj_bgrad.reshape(-1, 1),
            down_bgrad.reshape(-1, 1),
            up_bgrad.reshape(-1, 4),
        ],
        axis=1,
    )
    small_own, small_other = by_core(small_grad)
    small_sum = small_own + lax.ppermute(
        small_other.astype(jnp.bfloat16), "fsdp", sibling_pairs()
    ).astype(jnp.float32)
    sum_q, sum_k, sum_v, sum_down, sum_mod, caption_all = scatter_rest(
        blocks(qkv_grad),
        jnp.pad(blocks(small_sum.astype(jnp.bfloat16)), ((0, 0), (0, 0), (0, 0), (0, 111))),
        down_part.reshape(4, HD, model_width),
        jnp.pad(grad_mod.astype(jnp.bfloat16).reshape(-1, 128), ((0, 10), (0, 0))),
        caption_piece.astype(jnp.bfloat16),
    )
    wide = lambda part: part.astype(jnp.float32)
    sum_small = wide(sum_v[:, 1920 : 1920 + 17])
    return (
        block_out,
        grad_latents,
        sum_mod[:54].reshape(1, -1),
        wide(caption_all.reshape(1, -1, model_width)[:, : caption.shape[1]]),
        sum_small[:, :6].reshape(-1),
        jnp.concatenate([wide(sum_q), wide(sum_k), wide(sum_v[:, :1920])], axis=1),
        sum_small[:, 6],
        sum_small[:, 7],
        wide(sum_proj),
        sum_small[:, 8],
        wide(sum_cquery),
        sum_small[:, 9],
        wide(sum_ckv),
        sum_small[:, 10],
        wide(sum_cproj),
        sum_small[:, 11],
        wide(sum_up),
        sum_small[:, 13:17].reshape(-1),
        wide(sum_down.reshape(4 * HD, model_width)),
        sum_small[:, 12],
    )


def solution(mesh):
    placed = (
        P("fsdp", "seq", None),
        P("fsdp", None),
        P("fsdp", None, None),
        P("fsdp"),
        P("fsdp", None),
        P("fsdp"),
        P("fsdp"),
        P("fsdp", None),
        P("fsdp"),
        P("fsdp", None),
        P("fsdp"),
        P("fsdp", None),
        P("fsdp"),
        P("fsdp", None),
        P("fsdp"),
        P("fsdp", None),
        P("fsdp"),
        P("fsdp", None),
        P("fsdp"),
        P("fsdp", "seq", None),
    )
    return jax.shard_map(
        on_device,
        mesh=mesh,
        in_specs=placed,
        out_specs=(
            P("fsdp", "seq", None),
            P("fsdp", "seq", None),
            P("fsdp", None),
            P("fsdp", None, None),
            P("fsdp"),
            P("fsdp", None),
            P("fsdp"),
            P("fsdp"),
            P("fsdp", None),
            P("fsdp"),
            P("fsdp", None),
            P("fsdp"),
            P("fsdp", None),
            P("fsdp"),
            P("fsdp", None),
            P("fsdp"),
            P("fsdp", None),
            P("fsdp"),
            P("fsdp", None),
            P("fsdp"),
        ),
        check_vma=False,
    )
```

```python
import functools

import jax
import jax.numpy as jnp
from jax import lax
from jax.experimental import pallas as pl
from jax.experimental.pallas import tpu as pltpu
from jax.sharding import PartitionSpec as P

HD = 72
MESH = pl.DeviceIdType.MESH


epsilon = 1e-06


def for_sending(array):

    def short(part):
        return part.astype(jnp.bfloat16) if part.dtype == jnp.float32 else part

    return jax.tree.map(short, array)


def normalize(values):
    centre = values - jnp.mean(values, axis=-1, keepdims=True)
    spread = jnp.mean(centre * centre, axis=-1, keepdims=True)
    return centre * lax.rsqrt(spread + epsilon)


def modulate(values, shift, scale):
    return normalize(values) * (1.0 + scale) + shift


def project(former, latter):
    return jnp.dot(former, latter, preferred_element_type=jnp.float32)


def token_sum(values):
    return jnp.sum(values.astype(jnp.float32), axis=(0, 1))


def by_heads(matrix):
    return matrix.reshape(matrix.shape[:-1] + (matrix.shape[-1] // HD, HD))


def attend_forward(queries, key_rows, values):
    factor = HD ** (-0.5)
    scores = (
        jnp.einsum("qhd,khd->hqk", queries, key_rows, preferred_element_type=jnp.float32) * factor
    )
    largest = jnp.max(scores, axis=-1, keepdims=True)
    exponent = jnp.exp(scores - largest)
    partition = jnp.sum(exponent, axis=-1, keepdims=True)
    weights = (exponent / partition).astype(jnp.bfloat16)
    output = jnp.einsum("hqk,khd->qhd", weights, values, preferred_element_type=jnp.float32)
    return (output.astype(jnp.bfloat16), largest + jnp.log(partition))


def place():
    seq, fsdp = lax.axis_index("seq"), lax.axis_index("fsdp")
    y, x_lo = seq // 2, seq % 2
    z, rest = fsdp // 4, fsdp % 4
    x_hi, core = rest // 2, rest % 2
    return x_hi * 2 + x_lo, y, z, core


def device(x, y, z, core):
    return (y * 2 + x % 2, z * 4 + (x // 2) * 2 + core)


def step(value, by):
    return (value + by + 4) % 4


class Copies:
    def __init__(self, send, recv):
        self.send, self.recv, self.index, self.started = send, recv, {}, []

    def number(self, key):
        return self.index.setdefault(key, len(self.index))

    def push(self, key, src, dst, target):
        at = self.number(key)
        copy = pltpu.make_async_remote_copy(
            src_ref=src,
            dst_ref=dst,
            send_sem=self.send.at[at],
            recv_sem=self.recv.at[at],
            device_id=target,
            device_id_type=MESH,
        )
        copy.start()
        self.started.append(copy)

    def arrived(self, key, dst, source):
        at = self.number(key)
        pltpu.make_async_remote_copy(
            src_ref=dst,
            dst_ref=dst,
            send_sem=self.send.at[at],
            recv_sem=self.recv.at[at],
            device_id=source,
            device_id_type=MESH,
        ).wait_recv()

    def finish(self):
        for copy in self.started:
            copy.wait_send()


def greet(others):
    barrier = pltpu.get_barrier_semaphore()
    for other in others:
        pl.semaphore_signal(barrier, inc=1, device_id=other, device_id_type=MESH)
    pl.semaphore_wait(barrier, len(others))


class Piece:
    def __init__(self, source, out, axis, dim, start, size):
        self.source, self.out, self.axis = source, out, axis
        self.dim, self.start, self.size = dim, start, size

    def cut(self, part):
        parts = {"x": 2, "y": 4, "z": 1}[self.axis]
        size = self.size // parts
        unit = 128 if self.dim == 1 else 16
        start = self.start if parts == 1 else pl.multiple_of(self.start + part * size, unit)
        window = pl.ds(start, size)
        return (slice(None), window) if self.dim == 1 else (window, slice(None))


class Gather:
    def __init__(self, pieces, copies, local):
        self.pieces, self.copies, self.local = pieces, copies, local
        self.x, self.y, self.z, self.c = x, y, z, c = place()
        self.xh, self.xl = x // 2, x % 2
        self.sibling = device(x, y, z, 1 - c)
        self.far = device(step(x, 2), y, z, c)
        self.lines = {
            "x": [device(step(x, d), y, z, c) for d in (1, 2, 3)],
            "y": [device(x, step(y, d), z, c) for d in (1, 2, 3)],
            "z": [device(x, y, step(z, d), c) for d in (1, 2, 3)],
        }
        self.part = {"x": self.xl, "y": y, "z": 0}

    def others(self):
        return [self.sibling] + self.lines["x"] + self.lines["y"] + self.lines["z"]

    def block(self, p, dz, flip, part, core=None):
        core = self.c if core is None else core
        return p.out.at[(step(self.z, -dz), (self.xh + flip) % 2, core) + p.cut(part)]

    def both(self, key, src, dst, axis):
        self.copies.push(key + (1,), src, dst, self.lines[axis][0])
        self.copies.push(key + (3,), src, dst, self.lines[axis][2])

    def first(self):
        self.stays = []
        for n, p in enumerate(self.pieces):
            mine = p.source.at[p.cut(self.part[p.axis])]
            there = self.block(p, 0, 0, self.part[p.axis])
            copy = pltpu.make_async_copy(mine, there, self.local.at[n])
            copy.start()
            self.stays.append(copy)
            if p.axis != "x":
                self.copies.push((n, "far"), mine, there, self.far)
            if p.axis != "z":
                for d in (1, 2, 3):
                    self.copies.push((n, "mid", 0, d), mine, there, self.lines["z"][d - 1])
        for n, p in enumerate(self.pieces):
            mine = p.source.at[p.cut(self.part[p.axis])]
            self.both((n, "end", 0, 0), mine, self.block(p, 0, 0, self.part[p.axis]), p.axis)

    def second(self):
        for n, p in enumerate(self.pieces):
            if p.axis == "x":
                continue
            block = self.block(p, 0, 1, self.part[p.axis])
            self.copies.arrived((n, "far"), block, self.far)
            if p.axis == "y":
                for d in (1, 2, 3):
                    self.copies.push((n, "mid", 1, d), block, block, self.lines["z"][d - 1])
            self.both((n, "end", 0, 1), block, block, p.axis)

    def third(self):
        for dz in (1, 3, 2):
            for n, p in enumerate(self.pieces):
                if p.axis == "z":
                    continue
                for flip in (0, 1) if p.axis == "y" else (0,):
                    block = self.block(p, dz, flip, self.part[p.axis])
                    self.copies.arrived((n, "mid", flip, dz), block, self.lines["z"][3 - dz])
                    self.both((n, "end", dz, flip), block, block, p.axis)

    def blocks(self, p):
        if p.axis == "z":
            return ((0, 0), (0, 1))
        return tuple((dz, f) for dz in (0, 1, 3, 2) for f in ((0, 1) if p.axis == "y" else (0,)))

    def ended(self, n, p, dz, flip, d):
        if p.axis == "z":
            block = self.block(p, d, flip, 0)
        elif p.axis == "y":
            block = self.block(p, dz, flip, step(self.y, -d))
        else:
            from_x = step(self.x, -d)
            block = p.out.at[(step(self.z, -dz), from_x // 2, self.c) + p.cut(from_x % 2)]
        self.copies.arrived((n, "end", dz, flip, d), block, self.lines[p.axis][3 - d])
        return block

    def group(self, p, d, core):
        if p.axis == "z":
            return p.out.at[(step(self.z, -d), slice(None), core) + p.cut(0)]
        if p.axis == "y":
            return p.out.at[(slice(None), slice(None), core) + p.cut(step(self.y, -d))]
        from_x = step(self.x, -d)
        return p.out.at[(slice(None), from_x // 2, core) + p.cut(from_x % 2)]

    def share(self, n, p, d):
        block = self.group(p, d, self.c)
        self.copies.push((n, "core", d), block, block, self.sibling)

    def fourth(self):
        for copy in self.stays:
            copy.wait()
        for n, p in enumerate(self.pieces):
            self.share(n, p, 0)
        for at in range(8):
            for n, p in enumerate(self.pieces):
                if at >= len(self.blocks(p)):
                    continue
                dz, flip = self.blocks(p)[at]
                line = self.lines[p.axis]
                for d in (1, 3):
                    block = self.ended(n, p, dz, flip, d)
                    if (at % 2 == 0) == (d == 1):
                        on = line[0] if d == 1 else line[2]
                        self.copies.push((n, "end", dz, flip, 2), block, block, on)
                if at == len(self.blocks(p)) - 1:
                    self.share(n, p, 1)
                    self.share(n, p, 3)

    def last(self):
        for n, p in enumerate(self.pieces):
            for dz, flip in self.blocks(p):
                self.ended(n, p, dz, flip, 2)
            self.share(n, p, 2)
        for d in (0, 1, 3, 2):
            for n, p in enumerate(self.pieces):
                block = self.group(p, d, 1 - self.c)
                self.copies.arrived((n, "core", d), block, self.sibling)


def early_kernel(qkv, small, o_qkv, o_small, local, send, recv):
    pieces = [
        Piece(small, o_small, "z", 0, 0, small.shape[0]),
        Piece(qkv, o_qkv, "z", 1, 18 * 128, 9 * 128),
        Piece(qkv, o_qkv, "x", 1, 8 * 128, 10 * 128),
        Piece(qkv, o_qkv, "y", 1, 0, 8 * 128),
    ]
    copies = Copies(send, recv)
    work = Gather(pieces, copies, local)
    greet(work.others())
    work.first()
    work.second()
    work.third()
    work.fourth()
    work.last()
    copies.finish()


PAIR = 2 * HD


def head_slices(rows):
    for j in range(rows.shape[1] // (8 * PAIR)):
        for to in range(8):
            yield to, pl.ds(j * PAIR, PAIR), pl.ds((j * 8 + to) * PAIR, PAIR)


def exchange(copies, name, seq, peers, sent, got, local):
    for e in range(1, 8):
        copies.push((name, e), sent.at[(seq + e) % 8], got.at[seq], peers[e - 1])
    copy = pltpu.make_async_copy(sent.at[seq], got.at[seq], local)
    copy.start()
    return copy


def exchanged(copies, name, seq, peers, got, copy):
    copy.wait()
    for e in range(1, 8):
        copies.arrived((name, e), got.at[(seq + 8 - e) % 8], peers[7 - e])


def seq_peers():
    x, y, z, c = place()
    seq = y * 2 + x % 2
    return seq, [((seq + e) % 8, z * 4 + (x // 2) * 2 + c) for e in range(1, 8)]


def unique(x, y, z, c, extra):
    _, peers = seq_peers()
    far = [device((1 - x // 2) * 2 + e, y, z, c) for e in (0, 1)]
    return peers + far + [device(x, y, step(z, d), c) for d in (1, 2, 3)] + extra


CHUNK = 256


def head(which, h):
    return pl.ds(which * PAIR + h * HD, HD)


def attend(heads, h, out):
    tokens = 8 * 128
    keys = heads[:, :, head(1, h)].reshape(tokens, HD)
    values = heads[:, :, head(2, h)].reshape(tokens, HD)

    @pl.loop(0, tokens // CHUNK)
    def _(i):
        queries = heads[pl.ds(i * 2, 2), :, head(0, h)].reshape(CHUNK, HD)
        scores = lax.dot_general(
            queries, keys, (((1,), (1,)), ((), ())), preferred_element_type=jnp.float32
        ) * (HD**-0.5)
        exponent = jnp.exp(scores - jnp.max(scores, axis=1, keepdims=True))
        weights = exponent * (1.0 / jnp.sum(exponent, axis=1, keepdims=True))
        got = jnp.dot(weights.astype(jnp.bfloat16), values, preferred_element_type=jnp.float32)
        out[pl.ds(i * 2, 2), :, head(0, h)] = got.astype(jnp.bfloat16).reshape(2, 128, HD)


def head_back(queries, keys, values, grad, mask):
    across = (((1,), (1,)), ((), ()))
    scores = lax.dot_general(keys, queries, across, preferred_element_type=jnp.float32)
    scores = scores * (HD**-0.5) if mask is None else scores * (HD**-0.5) + mask
    exponent = jnp.exp(scores - jnp.max(scores, axis=0, keepdims=True))
    weights = exponent * (1.0 / jnp.sum(exponent, axis=0, keepdims=True))
    grad_weights = lax.dot_general(values, grad, across, preferred_element_type=jnp.float32)
    inner = jnp.sum(weights * grad_weights, axis=0, keepdims=True)
    grad_scores = (weights * (grad_weights - inner)).astype(jnp.bfloat16)
    grad_q = lax.dot_general(
        grad_scores, keys, (((0,), (0,)), ((), ())), preferred_element_type=jnp.float32
    ) * (HD**-0.5)
    return weights.astype(jnp.bfloat16), grad_scores, grad_q.astype(jnp.bfloat16)


def attend_back(heads, grads, h, out, key_sum, value_sum):
    tokens = 8 * 128
    keys = heads[:, :, head(1, h)].reshape(tokens, HD)
    values = heads[:, :, head(2, h)].reshape(tokens, HD)
    key_sum[...] = jnp.zeros_like(key_sum)
    value_sum[...] = jnp.zeros_like(value_sum)

    @pl.loop(0, tokens // CHUNK)
    def _(i):
        queries = heads[pl.ds(i * 2, 2), :, head(0, h)].reshape(CHUNK, HD)
        grad = grads[pl.ds(i * 2, 2), :, head(0, h)].reshape(CHUNK, HD)
        weights, grad_scores, grad_q = head_back(queries, keys, values, grad, None)
        value_sum[...] += project(weights, grad)
        key_sum[...] += project(grad_scores, queries)
        out[pl.ds(i * 2, 2), :, head(0, h)] = grad_q.reshape(2, 128, HD)

    out[:, :, head(1, h)] = (key_sum[...] * (HD**-0.5)).astype(jnp.bfloat16).reshape(8, 128, HD)
    out[:, :, head(2, h)] = value_sum[...].astype(jnp.bfloat16).reshape(8, 128, HD)


def cross_kernel(queries, text, grad_out, weight, grad_queries, grad_text, *, real):
    grad = lax.dot_general(
        grad_out[...], weight[...], (((1,), (1,)), ((), ())), preferred_element_type=jnp.float32
    ).astype(jnp.bfloat16)
    rows = lax.broadcasted_iota(jnp.int32, (text.shape[0], queries.shape[0]), 0)
    mask = jnp.where(rows < real, 0.0, -1e30)
    width = queries.shape[1]
    for h in range(width // HD):
        mine, values = pl.ds(h * HD, HD), pl.ds(width + h * HD, HD)
        slopes = grad[:, h * HD : (h + 1) * HD]
        weights, grad_scores, grad_q = head_back(
            queries[:, mine], text[:, mine], text[:, values], slopes, mask
        )
        grad_queries[:, mine] = grad_q
        grad_key = project(grad_scores, queries[:, mine]) * (HD**-0.5)
        grad_text[:, mine] = grad_key.astype(jnp.bfloat16)
        grad_text[:, values] = project(weights, slopes).astype(jnp.bfloat16)


def cross_back(queries, text, grad_out, weight):
    real = text.shape[0]
    text = jnp.pad(text, ((0, -real % 128), (0, 0)))
    bf16 = lambda like: jax.ShapeDtypeStruct(like.shape, jnp.bfloat16)
    return pl.pallas_call(
        functools.partial(cross_kernel, real=real),
        out_shape=(bf16(queries), bf16(text)),
        in_specs=[ON_CHIP] * 4,
        out_specs=(ON_CHIP,) * 2,
        compiler_params=pltpu.CompilerParams(vmem_limit_bytes=48 * 1024 * 1024),
    )(queries, text, grad_out, weight)


def late_kernel(
    up, cq, ckv, proj, cproj, down, packed,
    o_up, o_cq, o_ckv, o_proj, o_cproj, o_down, o_heads, o_rows,
    sent, heads, mixed, joined, local, send, recv,
):
    height = down.shape[0]
    pieces = [
        Piece(proj, o_proj, "z", 1, 0, proj.shape[1]),
        Piece(cq, o_cq, "z", 1, 0, cq.shape[1]),
        Piece(cproj, o_cproj, "z", 1, 0, cproj.shape[1]),
        Piece(ckv, o_ckv, "x", 1, 0, ckv.shape[1]),
        Piece(up, o_up, "y", 1, 0, up.shape[1]),
        Piece(down, o_down, "x", 0, 128, height - 128),
        Piece(down, o_down, "y", 0, 0, 128),
    ]
    copies = Copies(send, recv)
    work = Gather(pieces, copies, local)
    seq, peers = seq_peers()
    greet(unique(work.x, work.y, work.z, work.c, [work.sibling]))
    for to, what, at in head_slices(packed):
        sent[to, :, what] = packed[:, at]
    own = exchange(copies, "in", seq, peers, sent, heads, local.at[7])
    work.first()
    exchanged(copies, "in", seq, peers, heads, own)
    keep = pltpu.make_async_copy(heads, o_heads, local.at[8])
    keep.start()
    attend(heads, 0, mixed)
    work.second()
    attend(heads, 1, mixed)
    own = exchange(copies, "out", seq, peers, mixed, joined, local.at[9])
    work.third()
    work.fourth()
    exchanged(copies, "out", seq, peers, joined, own)
    for at, what, to in head_slices(o_rows):
        o_rows[:, to] = joined[at, :, what]
    work.last()
    keep.wait()
    copies.finish()


def whole(out):
    return out.reshape((-1,) + out.shape[4:])


def full_shapes(shards):
    return tuple(jax.ShapeDtypeStruct((4, 2, 2) + s.shape, s.dtype) for s in shards)


def semaphores(*counts):
    return [pltpu.SemaphoreType.DMA((n,)) for n in counts]


ANYWHERE = pl.BlockSpec(memory_space=pl.ANY)
ON_CHIP = pl.BlockSpec(memory_space=pltpu.VMEM)


def parameters(collective):
    return pltpu.CompilerParams(
        collective_id=collective, has_side_effects=True, vmem_limit_bytes=48 * 1024 * 1024
    )


def gather_early(*shards):
    outs = pl.pallas_call(
        early_kernel,
        out_shape=full_shapes(shards),
        in_specs=[ANYWHERE] * 2,
        out_specs=(ANYWHERE,) * 2,
        scratch_shapes=semaphores(4, 128, 128),
        compiler_params=parameters(0),
    )(*shards)
    return tuple(whole(out) for out in outs)


def gather_late(shards, packed):
    bf16 = lambda *shape: jax.ShapeDtypeStruct(shape, jnp.bfloat16)
    vmem = lambda *shape: pltpu.VMEM(shape, jnp.bfloat16)
    outs = pl.pallas_call(
        late_kernel,
        out_shape=full_shapes(shards) + (bf16(8, 128, 3 * PAIR), bf16(128, 8 * PAIR)),
        in_specs=[ANYWHERE] * 6 + [ON_CHIP],
        out_specs=(ANYWHERE,) * 7 + (ON_CHIP,),
        scratch_shapes=[
            vmem(8, 128, 3 * PAIR), vmem(8, 128, 3 * PAIR), vmem(8, 128, PAIR), vmem(8, 128, PAIR),
        ]
        + semaphores(10, 256, 256),
        compiler_params=parameters(1),
    )(*shards, packed)
    return tuple(whole(out) for out in outs[:6]) + outs[6:]


def add_up(parts, out):
    blocks, _, columns = out.shape
    tile = next(t for t in (384, 512, 256, 128) if columns % t == 0)

    @pl.loop(0, blocks * (columns // tile))
    def _(i):
        block = i // (columns // tile)
        cols = pl.ds(pl.multiple_of((i % (columns // tile)) * tile, 128), tile)
        total = parts[0][block, :, cols].astype(jnp.float32)
        for part in parts[1:]:
            total = total + part[block, :, cols].astype(jnp.float32)
        out[block, :, cols] = total.astype(out.dtype)


def columns(part, width, start=0):
    return pl.ds(pl.multiple_of(start + part * width, 128), width)


class Scatter:
    def __init__(self, by_y, by_x, by_z, outs, scratch, copies, keep):
        self.by_y, self.by_x, self.by_z = by_y, by_x, by_z
        self.o_up, self.o_mix, self.o_att = outs
        self.scratch, self.copies, self.keep = scratch, copies, keep
        self.x, self.y, self.z, self.c = x, y, z, c = place()
        self.xh, self.xl = x // 2, x % 2
        self.seq, self.peers = seq_peers()
        self.along_x = [device(step(x, d), y, z, c) for d in (1, 2, 3)]
        self.along_y = [device(x, step(y, d), z, c) for d in (1, 2, 3)]
        self.along_z = [device(x, y, step(z, d), c) for d in (1, 2, 3)]

    @staticmethod
    def buffers(by_y, by_x, by_z):
        vmem = lambda *shape: pltpu.VMEM(shape, jnp.bfloat16)
        wy, wx, wz = by_y // 4, by_x // 2, by_z
        return [
            vmem(4, 4, 2, HD, wy), vmem(4, 2, HD, wy), vmem(4, 2, HD, wy),
            vmem(2, HD, wy), vmem(4, HD, wy), vmem(1, HD, wy),
            vmem(4, 2, HD, wz), vmem(2, HD, wz), vmem(4, 1, HD, wz // 2),
            vmem(1, HD, wz // 2), vmem(4, 1, HD, wz // 8), vmem(1, HD, wz // 8),
            vmem(4, 4, HD, wx), vmem(4, HD, wx), vmem(4, 4, HD, wx // 4),
            vmem(4, HD, wx // 4), vmem(4, HD, wx // 4), vmem(1, HD, wx // 4),
        ]

    def first(self):
        u1, a1, m1 = self.scratch[0], self.scratch[6], self.scratch[12]
        up, up_at, up_size = self.by_y
        for d in (1, 2, 3):
            to_x, to_y, to_z = step(self.x, d), step(self.y, d), step(self.z, d)
            cols = columns(to_y, up_size // 4, up_at)
            self.copies.push(("u1", d), up.at[:, :, :, cols], u1.at[d], self.along_y[d - 1])
            at = 0
            for n, (source, start, size) in enumerate(self.by_x):
                self.copies.push(
                    ("m1", n, d),
                    source.at[:, to_x // 2, :, columns(to_x % 2, size // 2, start)],
                    m1.at[d, :, :, pl.ds(at, size // 2)],
                    self.along_x[d - 1],
                )
                at += size // 2
            at = 0
            for n, (source, start, size) in enumerate(self.by_z):
                self.copies.push(
                    ("a1", n, d),
                    source.at[to_z, :, :, pl.ds(start, size)],
                    a1.at[d, :, :, pl.ds(at, size)],
                    self.along_z[d - 1],
                )
                at += size
        self.keep(up.at[:, :, :, columns(self.y, up_size // 4, up_at)], u1.at[0])
        at = 0
        for source, start, size in self.by_x:
            self.keep(
                source.at[:, self.xh, :, columns(self.xl, size // 2, start)],
                m1.at[0, :, :, pl.ds(at, size // 2)],
            )
            at += size // 2
        at = 0
        for source, start, size in self.by_z:
            self.keep(
                source.at[self.z, :, :, pl.ds(start, size)], a1.at[0, :, :, pl.ds(at, size)]
            )
            at += size

    def second(self):
        u1, u1s, u2 = self.scratch[:3]
        a1, a1s, a2 = self.scratch[6:9]
        m1, m1s, m2 = self.scratch[12:15]
        for d in (1, 2, 3):
            at = 0
            for n, (_, _, size) in enumerate(self.by_z):
                got = a1.at[d, :, :, pl.ds(at, size)]
                self.copies.arrived(("a1", n, d), got, self.along_z[3 - d])
                at += size
        add_up([a1.at[i] for i in range(4)], a1s)
        for d in (1, 2, 3):
            to = step(self.x, d)
            part = a1s.at[pl.ds(to // 2, 1), :, columns(to % 2, a2.shape[-1])]
            self.copies.push(("a2", d), part, a2.at[d], self.along_x[d - 1])
        for d in (1, 2, 3):
            at = 0
            for n, (_, _, size) in enumerate(self.by_x):
                got = m1.at[d, :, :, pl.ds(at, size // 2)]
                self.copies.arrived(("m1", n, d), got, self.along_x[3 - d])
                at += size // 2
        add_up([m1.at[i] for i in range(4)], m1s)
        for d in (1, 2, 3):
            cols = columns(step(self.y, d), m2.shape[-1])
            self.copies.push(("m2", d), m1s.at[:, :, cols], m2.at[d], self.along_y[d - 1])
        for d in (1, 2, 3):
            self.copies.arrived(("u1", d), u1.at[d], self.along_y[3 - d])
        for zz in range(4):
            add_up([u1.at[i, zz] for i in range(4)], u1s.at[zz])
        for d in (1, 2, 3):
            self.copies.push(
                ("u2", d), u1s.at[step(self.z, d)], u2.at[d], self.along_z[d - 1]
            )

    def third(self):
        u1s, u2, u2s, u3 = self.scratch[1:5]
        a1s, a2, a2s, a3 = self.scratch[7:11]
        m1s, m2, m2s, m3 = self.scratch[13:17]
        for d in (1, 2, 3):
            self.copies.arrived(("a2", d), a2.at[d], self.along_x[3 - d])
        mine = a1s.at[pl.ds(self.xh, 1), :, columns(self.xl, a2.shape[-1])]
        add_up([mine] + [a2.at[d] for d in (1, 2, 3)], a2s)
        for d in (1, 2, 3):
            part = a2s.at[:, :, columns(step(self.y, d), a3.shape[-1])]
            self.copies.push(("a3", d), part, a3.at[d], self.along_y[d - 1])
        for d in (1, 2, 3):
            self.copies.arrived(("m2", d), m2.at[d], self.along_y[3 - d])
        add_up(
            [m1s.at[:, :, columns(self.y, m2.shape[-1])]] + [m2.at[d] for d in (1, 2, 3)], m2s
        )
        for d in (1, 2, 3):
            self.copies.push(("m3", d), m2s.at[step(self.z, d)], m3.at[d], self.along_z[d - 1])
        for d in (1, 2, 3):
            self.copies.arrived(("u2", d), u2.at[d], self.along_z[3 - d])
        add_up([u1s.at[self.z]] + [u2.at[d] for d in (1, 2, 3)], u2s)
        for d in (1, 2, 3):
            to = step(self.x, d) // 2
            self.copies.push(("u3", d), u2s.at[to], u3.at[d], self.along_x[d - 1])

    def fourth(self):
        u2s, u3, u3s = self.scratch[3:6]
        a2s, a3, a3s = self.scratch[9:12]
        m2s, m3, m3s = self.scratch[15:18]
        own = a2s.at[:, :, columns(self.y, a3.shape[-1])]
        for name, line, own, got, total, out in (
            ("a", self.along_y, own, [a3.at[d] for d in (1, 2, 3)], a3s, self.o_att),
            ("u", self.along_x, u2s.at[pl.ds(self.xh, 1)],
             [u3.at[pl.ds(d, 1)] for d in (1, 2, 3)], u3s, self.o_up),
            ("m", self.along_z, m2s.at[pl.ds(self.z, 1)],
             [m3.at[pl.ds(d, 1)] for d in (1, 2, 3)], m3s, self.o_mix),
        ):
            for d in (1, 2, 3):
                dst = a3.at[d] if name == "a" else (u3 if name == "u" else m3).at[d]
                self.copies.arrived((name + "3", d), dst, line[3 - d])
            add_up([own] + got, total)
            if name == "u":
                spot = out.at[:, columns(self.y, total.shape[-1])]
                for d in (1, 2, 3):
                    self.copies.push(("u4", d), total.at[0], spot, self.along_y[d - 1])
            else:
                spot = out.at[:, self.spot(self.seq, total)]
                for e in range(1, 8):
                    self.copies.push((name + "4", e), total.at[0], spot, self.peers[e - 1])
            self.keep(total.at[0], spot)

    def spot(self, seq, total):
        return columns((seq % 2) * 4 + seq // 2, total.shape[-1])

    def last(self):
        for d in (1, 2, 3):
            got = self.o_up.at[:, columns(step(self.y, -d), self.o_up.shape[-1] // 4)]
            self.copies.arrived(("u4", d), got, self.along_y[3 - d])
        for name, total, out in (
            ("a4", self.scratch[11], self.o_att), ("m4", self.scratch[17], self.o_mix),
        ):
            for e in range(1, 8):
                got = out.at[:, self.spot((self.seq + 8 - e) % 8, total)]
                self.copies.arrived((name, e), got, self.peers[7 - e])


class Stays:
    def __init__(self, local):
        self.local, self.copies, self.done = local, [], 0

    def __call__(self, src, dst):
        copy = pltpu.make_async_copy(src, dst, self.local.at[len(self.copies)])
        copy.start()
        self.copies.append(copy)

    def wait(self):
        for copy in self.copies[self.done :]:
            copy.wait()
        self.done = len(self.copies)


def back_kernel(
    up, ckv, proj, cproj, cq, heads, grad_rows, o_up, o_mix, o_att, o_flat,
    sent, grads, mixed, joined, key_sum, value_sum, *rest,
):
    scratch, (local, send, recv) = rest[:18], rest[18:]
    copies, keep = Copies(send, recv), Stays(local)
    work = Scatter(
        (up, 0, 2560), [(up, 2560, 2048), (ckv, 0, 1024)],
        [(ckv, 1024, 1280), (proj, 0, 1152), (cproj, 0, 1152), (cq, 0, 1152)],
        (o_up, o_mix, o_att), scratch, copies, keep,
    )
    seq, peers = seq_peers()
    greet(unique(work.x, work.y, work.z, work.c, []))
    for to, what, at in head_slices(grad_rows):
        sent[to, :, what] = grad_rows[:, at]
    own = exchange(copies, "in", seq, peers, sent, grads, local.at[16])
    work.first()
    spare = scratch[6]
    spare[:, :, :, 4736:] = jnp.zeros(spare.shape[:3] + (384,), spare.dtype)
    exchanged(copies, "in", seq, peers, grads, own)
    for h in (0, 1):
        attend_back(heads, grads, h, mixed, key_sum, value_sum)
    own = exchange(copies, "out", seq, peers, mixed, joined, local.at[17])
    keep.wait()
    work.second()
    work.third()
    exchanged(copies, "out", seq, peers, joined, own)
    for at, what, to in head_slices(o_flat):
        o_flat[:, to] = joined[at, :, what]
    work.fourth()
    work.last()
    keep.wait()
    copies.finish()


def scatter_back(up, ckv, proj, cproj, cq, heads, grad_rows):
    bf16 = lambda *shape: jax.ShapeDtypeStruct(shape, jnp.bfloat16)
    vmem = lambda *shape: pltpu.VMEM(shape, jnp.bfloat16)
    return pl.pallas_call(
        back_kernel,
        out_shape=(
            bf16(HD, 2560), bf16(HD, 3072), bf16(HD, 5120), bf16(128, 24 * PAIR),
        ),
        in_specs=[ANYWHERE] * 5 + [ON_CHIP] * 2,
        out_specs=(ANYWHERE,) * 3 + (ON_CHIP,),
        scratch_shapes=[
            vmem(8, 128, PAIR), vmem(8, 128, PAIR), vmem(8, 128, 3 * PAIR), vmem(8, 128, 3 * PAIR),
            pltpu.VMEM((1024, HD), jnp.float32), pltpu.VMEM((1024, HD), jnp.float32),
        ]
        + Scatter.buffers(2560, 3072, 5120)
        + semaphores(18, 80, 80),
        compiler_params=parameters(2),
    )(up, ckv, proj, cproj, cq, heads, grad_rows)


def rest_kernel(
    qkv, small, down, mod, cap, o_up, o_mix, o_att, o_down, o_mod, o_cap,
    d1, d1s, d2, d2s, t1, *rest,
):
    scratch, (local, send, recv) = rest[:18], rest[18:]
    copies, keep = Copies(send, recv), Stays(local)
    work = Scatter(
        (qkv, 0, 512), [(qkv, 512, 1024)], [(qkv, 1536, 1920), (small, 0, 128)],
        (o_up, o_mix, o_att), scratch, copies, keep,
    )
    seq, peers, along_y = work.seq, work.peers, work.along_y
    greet(unique(work.x, work.y, work.z, work.c, []))
    for d in (1, 2, 3):
        copies.push(("d1", d), down.at[step(work.y, d)], d1.at[d], along_y[d - 1])
    work.first()
    for e in range(1, 8):
        copies.push(("t1", e), mod, t1.at[e], peers[e - 1])
        copies.push(("cap", e), cap, o_cap.at[seq], peers[e - 1])
    keep(down.at[work.y], d1.at[0])
    keep(mod, t1.at[0])
    keep(cap, o_cap.at[seq])
    keep.wait()
    beside = device(work.xh * 2 + 1 - work.xl, work.y, work.z, work.c)
    for d in (1, 2, 3):
        copies.arrived(("d1", d), d1.at[d], along_y[3 - d])
    add_up([d1.at[pl.ds(i, 1)] for i in range(4)], d1s)
    copies.push(("d2",), d1s, d2, beside)
    work.second()
    copies.arrived(("d2",), d2, beside)
    add_up([d1s, d2], d2s)
    keep(d2s.at[0], o_down.at[work.y])
    for d in (1, 2, 3):
        copies.push(("d3", d), d2s.at[0], o_down.at[work.y], along_y[d - 1])
    work.third()
    total = t1[0].astype(jnp.float32)
    for e in range(1, 8):
        copies.arrived(("t1", e), t1.at[e], peers[7 - e])
        total = total + t1[e].astype(jnp.float32)
    o_mod[...] = total
    work.fourth()
    work.last()
    for d in (1, 2, 3):
        copies.arrived(("d3", d), o_down.at[step(work.y, -d)], along_y[3 - d])
    for e in range(1, 8):
        copies.arrived(("cap", e), o_cap.at[(seq + 8 - e) % 8], peers[7 - e])
    keep.wait()
    copies.finish()


def scatter_rest(qkv, small, down, mod, cap):
    width = down.shape[-1]
    bf16 = lambda *shape: jax.ShapeDtypeStruct(shape, jnp.bfloat16)
    vmem = lambda *shape: pltpu.VMEM(shape, jnp.bfloat16)
    return pl.pallas_call(
        rest_kernel,
        out_shape=(
            bf16(HD, 512), bf16(HD, 1024), bf16(HD, 2048), bf16(4, HD, width),
            jax.ShapeDtypeStruct(mod.shape, jnp.float32), bf16(8, *cap.shape),
        ),
        in_specs=[ANYWHERE] * 5,
        out_specs=(ANYWHERE,) * 4 + (ON_CHIP, ANYWHERE),
        scratch_shapes=[
            vmem(4, HD, width), vmem(1, HD, width), vmem(1, HD, width), vmem(1, HD, width),
            vmem(8, *mod.shape),
        ]
        + Scatter.buffers(512, 1024, 2048)
        + semaphores(18, 96, 96),
        compiler_params=parameters(3),
    )(qkv, small, down, mod, cap)


GELU = 0.7978845608028654
CUBE = 0.044715


def mlp_kernel(
    rows, other, own, grad, up, down, bias, out, grad_rows, bias_grad, up_other, up_own, down_grad
):
    @pl.when(pl.program_id(0) == 0)
    def _():
        out[...] = jnp.zeros_like(out)
        grad_rows[...] = jnp.zeros_like(grad_rows)

    across = (((1,), (1,)), ((), ()))
    hidden = project(rows[...], up[...]) + bias[...]
    square = hidden * hidden
    bend = jnp.tanh(GELU * (hidden + CUBE * hidden * square))
    active = (0.5 * hidden * (1.0 + bend)).astype(jnp.bfloat16)
    slope = 0.5 * (1.0 + bend) + 0.5 * hidden * (1.0 - bend * bend) * (
        GELU * (1.0 + 3.0 * CUBE * square)
    )
    out[...] += project(active, down[...])
    grad_act = lax.dot_general(grad[...], down[...], across, preferred_element_type=jnp.float32)
    grad_hidden = grad_act * slope
    rounded = grad_hidden.astype(jnp.bfloat16)
    bias_grad[...] = jnp.sum(rounded.astype(jnp.float32), axis=0, keepdims=True)
    grad_rows[...] += lax.dot_general(rounded, up[...], across, preferred_element_type=jnp.float32)
    up_other[...] = project(other[...], rounded).astype(jnp.bfloat16)
    up_own[...] = project(own[...], rounded).astype(jnp.bfloat16)
    down_grad[...] = lax.dot_general(
        active, grad[...], (((0,), (0,)), ((), ())), preferred_element_type=jnp.float32
    ).astype(jnp.bfloat16)


def mlp(rows, grad, up, down, bias):
    tokens, width = rows.shape
    units, size = up.shape[1], 512
    own, other = by_core(rows.T)
    fixed = lambda *shape: pl.BlockSpec(shape, lambda j: (0, 0))
    wide = lambda n: pl.BlockSpec((n, size), lambda j: (0, j))
    tall = pl.BlockSpec((size, width), lambda j: (j, 0))
    f32 = lambda *shape: jax.ShapeDtypeStruct(shape, jnp.float32)
    bf16 = lambda *shape: jax.ShapeDtypeStruct(shape, jnp.bfloat16)
    return pl.pallas_call(
        mlp_kernel,
        grid=(units // size,),
        out_shape=(
            f32(tokens, width), f32(tokens, width), f32(1, units),
            bf16(width // 2, units), bf16(width // 2, units), bf16(units, width),
        ),
        in_specs=[
            fixed(tokens, width), fixed(width // 2, tokens), fixed(width // 2, tokens),
            fixed(tokens, width), wide(width), tall, wide(1),
        ],
        out_specs=(
            fixed(tokens, width), fixed(tokens, width), wide(1),
            wide(width // 2), wide(width // 2), tall,
        ),
        compiler_params=pltpu.CompilerParams(vmem_limit_bytes=48 * 1024 * 1024),
    )(rows, other, own, grad, up, down, bias)


def sibling_pairs():
    return [(i, i + 1 - 2 * (i % 2)) for i in range(16)]


def by_core(matrix):
    core = lax.axis_index("fsdp") % 2
    split = matrix.reshape((8, 2, -1) + matrix.shape[1:])
    pick = lambda which: lax.dynamic_index_in_dim(split, which, 1, keepdims=False).reshape(
        (-1,) + matrix.shape[1:]
    )
    return pick(core), pick(1 - core)


def pair_grad(former, latter):
    own, other = by_core(former.T)
    theirs = project(other, latter).astype(jnp.bfloat16)
    received = lax.ppermute(theirs, "fsdp", sibling_pairs())
    return (project(own, latter) + received.astype(jnp.float32)).astype(jnp.bfloat16)


def on_device(
    latents,
    timestep,
    caption,
    shift_table,
    qkv_weight,
    query_bias,
    value_bias,
    proj_weight,
    proj_bias,
    cross_query,
    cross_qbias,
    cross_kv,
    cross_vbias,
    cross_proj,
    cross_pbias,
    up_weight,
    up_bias,
    down_weight,
    down_bias,
    cotangent,
):
    group = lax.axis_index("fsdp")
    small = jnp.zeros((32 * HD * 16,), jnp.bfloat16)
    at = 0
    for vector in (
        shift_table, query_bias, value_bias, proj_bias, cross_qbias, cross_vbias, cross_pbias,
        down_bias, up_bias,
    ):
        small = lax.dynamic_update_slice(small, vector, (at + group * vector.shape[0],))
        at += 16 * vector.shape[0]
    full_qkv, each_small = gather_early(qkv_weight, small.reshape(32, -1))
    full_small = jnp.sum(each_small.reshape(16, 32, -1).astype(jnp.float32), axis=0)
    full_table = full_small[:6]
    full_qbias, full_vbias, full_pbias, full_cqbias, full_cvbias, full_cpbias, full_dbias = (
        full_small[6 + i] for i in range(7)
    )
    full_ubias = full_small[13:17].reshape(-1)
    latent_count, local_len, model_width = latents.shape
    inputs = latents.astype(jnp.float32)
    modulation = (full_table + timestep.astype(jnp.float32).reshape(6, model_width)).reshape(
        latent_count, 6, 1, model_width
    )
    shift_one, scale_one, gate_one = (modulation[:, 0], modulation[:, 1], modulation[:, 2])
    shift_two, scale_two, gate_two = (modulation[:, 3], modulation[:, 4], modulation[:, 5])
    pre_one, pull_one = jax.vjp(modulate, inputs, shift_one, scale_one)
    normed_one = pre_one.astype(jnp.bfloat16)
    qkv_bias = jnp.concatenate([full_qbias, jnp.zeros_like(full_qbias), full_vbias]).astype(
        jnp.float32
    )
    packed = (project(normed_one, full_qkv) + qkv_bias).astype(jnp.bfloat16)
    full_up, full_cquery, full_ckv, full_proj, full_cproj, full_down, heads, rows = gather_late(
        (up_weight, cross_query, cross_kv, proj_weight, cross_proj, down_weight), packed[0]
    )
    tok_major = rows[None]
    branch_one = project(tok_major, full_proj) + full_pbias.astype(jnp.float32)
    after_one = inputs + gate_one * branch_one
    middle = after_one.astype(jnp.bfloat16)
    cross_rows = (project(middle, full_cquery) + full_cqbias.astype(jnp.float32)).astype(
        jnp.bfloat16
    )
    kv_bias = jnp.concatenate([jnp.zeros_like(full_cvbias), full_cvbias]).astype(jnp.float32)
    text_kv = (project(caption, full_ckv) + kv_bias).astype(jnp.bfloat16)
    text_keys = by_heads(text_kv[..., :model_width])
    text_values = by_heads(text_kv[..., model_width:])
    cross_heads, _ = jax.vmap(attend_forward)(
        by_heads(cross_rows), text_keys, text_values
    )
    crossed = cross_heads.reshape(latent_count, local_len, model_width)
    branch_two = project(crossed, full_cproj) + full_cpbias.astype(jnp.float32)
    after_two = after_one + branch_two
    pre_two, pull_two = jax.vjp(modulate, after_two, shift_two, scale_two)
    normed_two = pre_two.astype(jnp.bfloat16)
    grad_out = cotangent.astype(jnp.float32)
    grad_three = (gate_two * grad_out).astype(jnp.bfloat16)
    product, grad_pre_two, up_bgrad, up_other, up_own, down_grad = mlp(
        normed_two[0], grad_three[0], full_up, full_down, full_ubias.reshape(1, -1)
    )
    up_received = lax.ppermute(up_other, "fsdp", sibling_pairs())
    down_part = lax.psum_scatter(down_grad, "fsdp", scatter_dimension=0, tiled=True)
    branch_three = product[None] + full_dbias.astype(jnp.float32)
    block_out = (after_two + gate_two * branch_three).astype(jnp.bfloat16)
    grad_gate_two = jnp.sum(grad_out * branch_three, axis=1, keepdims=True)
    down_bgrad = token_sum(grad_three)
    up_grad = (up_own.astype(jnp.float32) + up_received.astype(jnp.float32)).astype(jnp.bfloat16)
    grad_pre_two = grad_pre_two[None]
    grad_mid_two, grad_shift_two, grad_scale_two = pull_two(grad_pre_two)
    grad_after_two = grad_out + grad_mid_two
    grad_branch_two = grad_after_two.astype(jnp.bfloat16)
    cproj_grad = pair_grad(crossed[0], grad_branch_two[0])
    cproj_bgrad = token_sum(grad_branch_two)
    grad_cross, grad_text = cross_back(
        cross_rows[0], text_kv[0], grad_branch_two[0], full_cproj
    )
    grad_cross_rows = grad_cross[None]
    cquery_grad = pair_grad(middle[0], grad_cross_rows[0])
    cquery_bgrad = token_sum(grad_cross_rows)
    grad_after_one = grad_after_two + project(grad_cross_rows, full_cquery.T)
    text_piece = grad_text.shape[0] // 8
    text_pieces = lax.all_to_all(
        grad_text.reshape(8, text_piece, grad_text.shape[1]), "seq", 0, 0
    )
    grad_gate_one = jnp.sum(grad_after_one * branch_one, axis=1, keepdims=True)
    grad_branch_one = (gate_one * grad_after_one).astype(jnp.bfloat16)
    proj_grad = pair_grad(tok_major[0], grad_branch_one[0])
    proj_bgrad = token_sum(grad_branch_one)
    grad_tok = project(grad_branch_one, full_proj.T).astype(jnp.bfloat16)
    text_pieces, grad_tok, up_grad, proj_grad, cquery_grad, cproj_grad = (
        lax.optimization_barrier(
            (text_pieces, grad_tok, up_grad, proj_grad, cquery_grad, cproj_grad)
        )
    )
    text_grad = jnp.sum(text_pieces.astype(jnp.float32), axis=0).astype(jnp.bfloat16)
    caption_part = lax.dynamic_slice_in_dim(
        jnp.pad(caption[0], ((0, grad_text.shape[0] - caption.shape[1]), (0, 0))),
        lax.axis_index("seq") * text_piece, text_piece, 0
    )
    ckv_grad = pair_grad(caption_part, text_grad)
    cvalue_bgrad = jnp.sum(text_grad[:, model_width:].astype(jnp.float32), axis=0)
    caption_piece = project(text_grad, full_ckv.T)
    blocks = lambda grad: grad.reshape(4, 2, HD, -1)
    sum_up, sum_mix, sum_att, flat = scatter_back(
        *(blocks(grad) for grad in (up_grad, ckv_grad, proj_grad, cproj_grad, cquery_grad)),
        heads,
        grad_tok[0],
    )
    up_one, ckv_one, up_two, ckv_two = jnp.split(sum_mix, (1024, 1536, 2560), axis=1)
    sum_up = jnp.concatenate([sum_up, up_one, up_two], axis=1)
    ckv_three, sum_proj, sum_cproj, sum_cquery, _ = jnp.split(
        sum_att, (1280, 2432, 3584, 4736), axis=1
    )
    sum_ckv = jnp.concatenate([ckv_one, ckv_two, ckv_three], axis=1)
    grad_flat = flat[None]
    qkv_grad = pair_grad(normed_one[0], grad_flat[0])
    qbias_grad = token_sum(grad_flat[..., :model_width])
    vbias_grad = token_sum(grad_flat[..., 2 * model_width :])
    grad_pre_one = project(grad_flat, full_qkv.T)
    grad_norm_one, grad_shift_one, grad_scale_one = pull_one(grad_pre_one)
    grad_latents = grad_after_one + grad_norm_one
    grad_mod = jnp.concatenate(
        [
            grad_shift_one,
            grad_scale_one,
            grad_gate_one,
            grad_shift_two,
            grad_scale_two,
            grad_gate_two,
        ],
        axis=1,
    )
    grad_mod = grad_mod.reshape(latent_count, 6 * model_width)
    small_grad = jnp.concatenate(
        [
            grad_mod.reshape(-1, 6),
            qbias_grad.reshape(-1, 1),
            vbias_grad.reshape(-1, 1),
            proj_bgrad.reshape(-1, 1),
            cquery_bgrad.reshape(-1, 1),
            cvalue_bgrad.reshape(-1, 1),
            cproj_bgrad.reshape(-1, 1),
            down_bgrad.reshape(-1, 1),
            up_bgrad.reshape(-1, 4),
        ],
        axis=1,
    )
    small_own, small_other = by_core(small_grad)
    small_sum = small_own + lax.ppermute(
        small_other.astype(jnp.bfloat16), "fsdp", sibling_pairs()
    ).astype(jnp.float32)
    sum_q, sum_k, sum_v, sum_down, sum_mod, caption_all = scatter_rest(
        blocks(qkv_grad),
        jnp.pad(blocks(small_sum.astype(jnp.bfloat16)), ((0, 0), (0, 0), (0, 0), (0, 111))),
        down_part.reshape(4, HD, model_width),
        jnp.pad(grad_mod.astype(jnp.bfloat16).reshape(-1, 128), ((0, 10), (0, 0))),
        caption_piece.astype(jnp.bfloat16),
    )
    wide = lambda part: part.astype(jnp.float32)
    sum_small = wide(sum_v[:, 1920 : 1920 + 17])
    return (
        block_out,
        grad_latents,
        sum_mod[:54].reshape(1, -1),
        wide(caption_all.reshape(1, -1, model_width)[:, : caption.shape[1]]),
        sum_small[:, :6].reshape(-1),
        jnp.concatenate([wide(sum_q), wide(sum_k), wide(sum_v[:, :1920])], axis=1),
        sum_small[:, 6],
        sum_small[:, 7],
        wide(sum_proj),
        sum_small[:, 8],
        wide(sum_cquery),
        sum_small[:, 9],
        wide(sum_ckv),
        sum_small[:, 10],
        wide(sum_cproj),
        sum_small[:, 11],
        wide(sum_up),
        sum_small[:, 13:17].reshape(-1),
        wide(sum_down.reshape(4 * HD, model_width)),
        sum_small[:, 12],
    )


def solution(mesh):
    placed = (
        P("fsdp", "seq", None),
        P("fsdp", None),
        P("fsdp", None, None),
        P("fsdp"),
        P("fsdp", None),
        P("fsdp"),
        P("fsdp"),
        P("fsdp", None),
        P("fsdp"),
        P("fsdp", None),
        P("fsdp"),
        P("fsdp", None),
        P("fsdp"),
        P("fsdp", None),
        P("fsdp"),
        P("fsdp", None),
        P("fsdp"),
        P("fsdp", None),
        P("fsdp"),
        P("fsdp", "seq", None),
    )
    return jax.shard_map(
        on_device,
        mesh=mesh,
        in_specs=placed,
        out_specs=(
            P("fsdp", "seq", None),
            P("fsdp", "seq", None),
            P("fsdp", None),
            P("fsdp", None, None),
            P("fsdp"),
            P("fsdp", None),
            P("fsdp"),
            P("fsdp"),
            P("fsdp", None),
            P("fsdp"),
            P("fsdp", None),
            P("fsdp"),
            P("fsdp", None),
            P("fsdp"),
            P("fsdp", None),
            P("fsdp"),
            P("fsdp", None),
            P("fsdp"),
            P("fsdp", None),
            P("fsdp"),
        ),
        check_vma=False,
    )
```
